512 devices in a mesh: noise: 32 (over y, x, core), dp: 16 (over z).
Axes of the slice: x: 4, y: 4, z: 16, core: 2. Of those that a mesh axis runs over, the one named last changes fastest.
Arguments:
- noise_rows: bfloat16 [4096, 16384], P('noise', 'dp'), may hold values from -10 to 10
- data_rows: bfloat16 [4096, 16384], P('noise', 'dp'), may hold values from -6 to 6
Outputs:
- targets: bfloat16 [4096, 16384], P('noise', 'dp')
- noise_potential: float32 [4096], P('noise')
- data_potential: float32 [4096], P('dp')
The draws below stay inside these ranges and needn't reach their ends.
All inputs are finite; a program needn't handle non-finite values.
Results may differ from the reference program's by a relative error of at most 0.0045.
Values may be sent and summed in bfloat16 or wider, within the bound.
No kernel may reach another device: no remote copies, remote signals or barrier semaphores. Data moves between devices by JAX's collectives and lax.ppermute only.
A program may use at most 64 MiB of HBM per device.

```python
import math
import jax
import jax.numpy as jnp
from jax import lax

D = 16384
ITERS = 4
TOKENS = 4096


def draw_noise_rows(key, part):
    key = jax.random.fold_in(key, 11)
    base_key, pick_key, sign_key = jax.random.split(key, 3)
    base = jnp.clip(jax.random.normal(base_key, (TOKENS, D), jnp.float32), -6.0, 6.0)
    picked = jax.random.randint(pick_key, (TOKENS, 1), 0, 4) == 0
    signs = (jax.random.randint(sign_key, (TOKENS, 1), 0, 2) * 2 - 1).astype(jnp.float32)
    offset = jnp.where(picked, 4.0 * signs, 0.0)
    return (base + offset).astype(jnp.bfloat16)


def block_levels(stream_key, shape, shards, low, largest):
    def one(dim, shards_of):
        heights = jax.random.uniform(jax.random.fold_in(jax.random.fold_in(stream_key, 6), dim), (shards_of,), jnp.float32, low / len(shards), largest / len(shards))
        return jnp.repeat(jnp.exp(heights), shape[dim] // shards_of).reshape((-1,) + (1,) * (len(shape) - dim - 1))

    gain = one(*shards[0])
    for cut in shards[1:]:
        gain = gain * one(*cut)
    return gain


def bell_draw(key, dims, spread, most, pieces=(), dtype=jnp.bfloat16):
    values = spread * jax.random.normal(key, dims, jnp.float32)
    if pieces:
        values = values * block_levels(key, dims, pieces, -0.22, 0.18)
    return jnp.clip(values, -most, most).astype(dtype)


def setup_inputs(seed: int = 0) -> dict:
    seeds = jax.random.split(jax.random.key(seed), 3)
    noise_rows = draw_noise_rows(jax.random.fold_in(seeds[2], 71), 0)
    data_rows = bell_draw(seeds[1], (TOKENS, D), 1.0, 6.0, ((0, 32), (1, 16)))
    return {"noise_rows": noise_rows, "data_rows": data_rows}


def log_sum_exp(values, axis):
    peak = lax.optimization_barrier(jnp.max(values, axis=axis, keepdims=True))
    total = lax.optimization_barrier(jnp.sum(jnp.exp(values - peak), axis=axis))
    return jnp.squeeze(peak, axis) + jnp.log(total)

def reference(noise_rows, data_rows):
    noise_wide = noise_rows.astype(jnp.float32)
    data_wide = data_rows.astype(jnp.float32)
    noise_square = lax.optimization_barrier(jnp.sum(noise_wide * noise_wide, axis=1))
    data_square = lax.optimization_barrier(jnp.sum(data_wide * data_wide, axis=1))
    cross = jnp.dot(noise_rows, data_rows.T, preferred_element_type=jnp.float32)
    cost = (noise_square[:, None] + data_square[None, :] - 2.0 * cross) / D
    epsilon = 0.7 / math.sqrt(D)
    log_weight = -math.log(TOKENS)
    noise_potential = jnp.zeros((TOKENS,), jnp.float32)
    data_potential = jnp.zeros((TOKENS,), jnp.float32)
    for step in range(ITERS):
        noise_potential = epsilon * log_weight - epsilon * log_sum_exp((data_potential[None, :] - cost) / epsilon, 1)
        data_potential = epsilon * log_weight - epsilon * log_sum_exp((noise_potential[:, None] - cost) / epsilon, 0)
    plan = jnp.exp((noise_potential[:, None] + data_potential[None, :] - cost) / epsilon + math.log(TOKENS)).astype(jnp.bfloat16)
    mass = lax.optimization_barrier(jnp.sum(plan.astype(jnp.float32), axis=1))
    weighted = jnp.dot(plan, data_rows, preferred_element_type=jnp.float32)
    targets = (weighted / mass[:, None]).astype(jnp.bfloat16)
    return (targets, noise_potential, data_potential)
```

```python
import functools
import math

import jax
import jax.numpy as jnp
from jax import lax
from jax.experimental import pallas as pl
from jax.experimental.pallas import tpu as pltpu
from jax.sharding import PartitionSpec as P

D = 16384
ITERS = 4
YS, XS, CORES = 4, 4, 2
LOG2E = math.log2(math.e)
VMEM = pl.BlockSpec(memory_space=pltpu.VMEM)
SMEM = pl.BlockSpec(memory_space=pltpu.SMEM)
PARAMS = pltpu.CompilerParams(vmem_limit_bytes=48 * 1024 * 1024)


def send(value, dy=0, dx=0, dc=0):
    pairs = []
    for y in range(YS):
        for x in range(XS):
            for c in range(CORES):
                source = (y * XS + x) * CORES + c
                target = ((y + dy) % YS * XS + (x + dx) % XS) * CORES + (c + dc) % CORES
                pairs.append((source, target))
    return lax.ppermute(value, "noise", pairs)


def send_z(value, dz):
    size = lax.axis_size("dp")
    return lax.ppermute(value, "dp", [(z, (z + dz) % size) for z in range(size)])


def gather4(block, **axis):
    (name,) = axis
    before, after = send(block, **{name: 1}), send(block, **{name: -1})
    return jnp.concatenate([block, before, send(block, **{name: 2}), after], axis=0)


def squares_row(block):
    wide = block.astype(jnp.float32)
    column = jnp.sum(wide * wide, axis=1, keepdims=True)
    n = block.shape[0]
    row_at = lax.broadcasted_iota(jnp.int32, (n, n), 0)
    column_at = lax.broadcasted_iota(jnp.int32, (n, n), 1)
    return jnp.sum(jnp.where(row_at == column_at, column, 0.0), axis=0, keepdims=True)


def partial_kernel(scale, place_ref, x_here, x_there, y_ref, *refs):
    outs, (x_all, y_squares) = refs[:-2], refs[-2:]
    rows = x_here.shape[0] // XS
    high = outs[0].shape[0]
    x, c = place_ref[2], place_ref[3]
    for k in range(XS):
        at = lax.rem(x + XS - k, XS) * CORES
        block = slice(k * rows, (k + 1) * rows)
        x_all[at + c] = x_here[block, :]
        x_all[at + 1 - c] = x_there[block, :]
    for k in range(YS):
        block = slice(k * rows, (k + 1) * rows)
        y_squares[:, block] = scale * squares_row(y_ref[block, :])
    for k in range(XS * CORES):
        value = x_all[k]
        wide = value.astype(jnp.float32)
        x_squares = scale * jnp.sum(wide * wide, axis=1, keepdims=True)
        cross = lax.dot_general(
            value, y_ref[...], (((1,), (1,)), ((), ())), preferred_element_type=jnp.float32
        )
        value = (2.0 * scale) * cross - x_squares - y_squares[...]
        for t in range(rows // high):
            outs[k * (rows // high) + t][...] = value[t * high : (t + 1) * high]


def joined(parts):
    peak = jnp.max(parts, axis=0)
    return peak + jnp.log(jnp.sum(jnp.exp2(parts - peak), axis=0)) * LOG2E


def on_diagonal(n):
    rows = lax.broadcasted_iota(jnp.int32, (n, n), 0)
    return rows == lax.broadcasted_iota(jnp.int32, (n, n), 1)


def column_of(u, k):
    n = u.shape[1]
    return jnp.sum(jnp.where(on_diagonal(n), u[k : k + 1], 0.0), axis=1, keepdims=True)


def row_of(parts_ref, log_weight):
    v = log_weight - joined(parts_ref[...])
    return jnp.concatenate([v[k : k + 1] for k in range(YS)], axis=1)


def copy_out(out_ref):
    whole = out_ref[0]
    for k in range(1, out_ref.shape[0]):
        out_ref[k] = whole


def row_sums(a_ref, v, out_ref):
    n = out_ref.shape[2]
    for k in range(out_ref.shape[1]):
        value = a_ref[k * n : (k + 1) * n, :]
        if v is not None:
            value = value + v
        peak = jnp.max(value, axis=1, keepdims=True)
        total = jnp.sum(jnp.exp2(value - peak), axis=1, keepdims=True)
        part = peak + jnp.log(total) * LOG2E
        out_ref[0, k : k + 1, :] = jnp.sum(jnp.where(on_diagonal(n), part, 0.0), axis=0, keepdims=True)
    copy_out(out_ref)


def first_rows_kernel(*refs):
    pieces, (a_ref, out_ref) = refs[:-2], refs[-2:]
    high = pieces[0].shape[0]
    for k, piece in enumerate(pieces):
        a_ref[k * high : (k + 1) * high, :] = piece[...]
    row_sums(a_ref, None, out_ref)


def rows_kernel(log_weight, a_ref, parts_ref, out_ref):
    row_sums(a_ref, row_of(parts_ref, log_weight), out_ref)


def columns_kernel(log_weight, a_ref, parts_ref, u_ref, out_ref, shifted):
    u = log_weight - joined(parts_ref[...])
    u_ref[...] = u
    blocks, n = u.shape
    width = a_ref.shape[1]
    peak = None
    for k in range(blocks):
        value = a_ref[k * n : (k + 1) * n, :] + column_of(u, k)
        shifted[k * n : (k + 1) * n, :] = value
        block_peak = jnp.max(value.reshape(n // 8, 8, width), axis=0)
        peak = block_peak if peak is None else jnp.maximum(peak, block_peak)
    peak = jnp.max(peak, axis=0, keepdims=True)
    total = jnp.zeros((8, width), jnp.float32)
    for k in range(blocks):
        value = jnp.exp2(shifted[k * n : (k + 1) * n, :] - peak)
        total = total + jnp.sum(value.reshape(n // 8, 8, width), axis=0)
    part = peak + jnp.log(jnp.sum(total, axis=0, keepdims=True)) * LOG2E
    for k in range(2 * YS):
        at = k % YS * n
        out_ref[0, k : k + 1, :] = part[:, at : at + n]
    copy_out(out_ref)


def plan_kernel(log_weight, a_ref, u_ref, parts_ref, out_ref):
    v = row_of(parts_ref, log_weight)
    u = u_ref[...] - log_weight
    blocks, n = u.shape
    top = v.astype(jnp.bfloat16).astype(jnp.float32)
    rest = v - top
    middle = rest.astype(jnp.bfloat16).astype(jnp.float32)
    extra = out_ref.shape[1] - n
    row = lax.broadcasted_iota(jnp.int32, (extra, v.shape[1]), 0)
    under = jnp.where(row == 0, top, jnp.where(row == 1, middle, jnp.where(row == 2, rest - middle, 0.0)))
    under = under.astype(jnp.bfloat16)
    for k in range(blocks):
        value = a_ref[k * n : (k + 1) * n, :] + (column_of(u, k) + v)
        out_ref[k, :n, :] = jnp.exp2(value).astype(jnp.bfloat16)
        out_ref[k, n:, :] = under


def target_kernel(unit, place_ref, plan_ref, u_ref, y_ref, out_ref, f_ref, g_ref, total, mass):
    step = pl.program_id(0)
    z, x, c = place_ref[0], place_ref[2], place_ref[3]
    blocks = plan_ref.shape[0]
    n = out_ref.shape[0]

    @pl.when(step == 0)
    def _():
        total[...] = jnp.zeros_like(total)
        mass[...] = jnp.zeros_like(mass)
        f_ref[...] = unit * u_ref[pl.ds(x * CORES + c, 1), :]

    plan = jnp.concatenate([plan_ref[k, :n, :] for k in range(blocks)], axis=1)
    mass[...] += jnp.sum(plan.astype(jnp.float32), axis=1, keepdims=True)
    total[...] += jnp.dot(plan, y_ref[...], preferred_element_type=jnp.float32)

    @pl.when(step == z // XS)
    def _():
        for k in range(CORES):
            v = plan_ref[lax.rem(z, XS) * CORES + k, n:, :].astype(jnp.float32)
            g_ref[:, k * n : (k + 1) * n] = unit * (v[0:1] + v[1:2] + v[2:3])

    @pl.when(step == YS - 1)
    def _():
        out_ref[...] = (total[...] / mass[...]).astype(out_ref.dtype)


def on_device(noise_rows, data_rows):
    rows, features = noise_rows.shape
    tokens = rows * lax.axis_size("noise")
    depth = lax.axis_size("dp")
    me, z = lax.axis_index("noise"), lax.axis_index("dp")
    place = jnp.stack([z, me // (XS * CORES), me // CORES % XS, me % CORES]).astype(jnp.int32)
    epsilon = 0.7 / math.sqrt(D)
    log_weight = -math.log2(tokens)
    f32 = jnp.float32

    x_here = gather4(noise_rows, dx=1)
    x_there = send(x_here, dc=1)
    group = XS * CORES
    y_groups = [[y * group + k for y in range(YS)] for k in range(group)]
    x_groups = [[y * group + k for k in range(group)] for y in range(YS)]

    def swap(value, groups):
        return lax.all_to_all(value, "noise", 0, 0, axis_index_groups=groups, tiled=True)

    y_near = lax.all_gather(data_rows, "noise", axis_index_groups=y_groups, tiled=True)
    tall, wide = group * rows, YS * rows
    high = 16
    partial_value = pl.pallas_call(
        functools.partial(partial_kernel, LOG2E / (epsilon * D)),
        out_shape=[jax.ShapeDtypeStruct((high, wide), f32)] * (tall // high),
        in_specs=[SMEM] + [VMEM] * 3,
        out_specs=[VMEM] * (tall // high),
        scratch_shapes=[
            pltpu.VMEM((group, rows, features), jnp.bfloat16),
            pltpu.VMEM((1, wide), f32),
        ],
        compiler_params=PARAMS,
    )(place, x_here, x_there, y_near)
    late_rows, partial_value = lax.optimization_barrier((data_rows, partial_value))

    pieces = lax.psum(partial_value, "dp")
    row_shape = jax.ShapeDtypeStruct((group, group, rows), f32)
    column_shape = jax.ShapeDtypeStruct((YS, 2 * YS, rows), f32)
    u_shape = jax.ShapeDtypeStruct((group, rows), f32)
    a, part = pl.pallas_call(
        first_rows_kernel,
        out_shape=[jax.ShapeDtypeStruct((tall, wide), f32), row_shape],
        in_specs=[VMEM] * (tall // high),
        out_specs=[VMEM] * 2,
        compiler_params=PARAMS,
    )(*pieces)
    for step in range(ITERS):
        if step > 0:
            part = pl.pallas_call(
                functools.partial(rows_kernel, log_weight),
                out_shape=row_shape,
                in_specs=[VMEM] * 2,
                out_specs=VMEM,
                compiler_params=PARAMS,
            )(a, part)
        part = swap(part, x_groups)
        u, part = pl.pallas_call(
            functools.partial(columns_kernel, log_weight),
            out_shape=[u_shape, column_shape],
            in_specs=[VMEM] * 2,
            out_specs=[VMEM] * 2,
            scratch_shapes=[pltpu.VMEM((tall, wide), f32)],
            compiler_params=PARAMS,
        )(a, part)
        part = swap(part, y_groups)
    plan = pl.pallas_call(
        functools.partial(plan_kernel, log_weight),
        out_shape=jax.ShapeDtypeStruct((group, rows + 16, wide), jnp.bfloat16),
        in_specs=[VMEM] * 3,
        out_specs=VMEM,
        compiler_params=PARAMS,
    )(a, u, part)
    plan = swap(plan, x_groups)

    everything = lax.all_gather(late_rows, "noise", axis=0, tiled=True)
    targets, noise_potential, data_potential = pl.pallas_call(
        functools.partial(target_kernel, epsilon / LOG2E),
        grid=(YS,),
        out_shape=[
            jax.ShapeDtypeStruct((rows, features), jnp.bfloat16),
            jax.ShapeDtypeStruct((1, rows), f32),
            jax.ShapeDtypeStruct((1, CORES * rows), f32),
        ],
        in_specs=[
            SMEM,
            pl.BlockSpec((group, rows + 16, rows), lambda k: (0, 0, k)),
            pl.BlockSpec((group, rows), lambda k: (0, 0)),
            pl.BlockSpec((group * rows, features), lambda k: (k, 0)),
        ],
        out_specs=[
            pl.BlockSpec((rows, features), lambda k: (0, 0)),
            pl.BlockSpec((1, rows), lambda k: (0, 0)),
            pl.BlockSpec((1, CORES * rows), lambda k: (0, 0)),
        ],
        scratch_shapes=[
            pltpu.VMEM((rows, features), f32),
            pltpu.VMEM((rows, 1), f32),
        ],
        compiler_params=PARAMS,
    )(place, plan, u, everything)
    return targets, noise_potential.reshape(rows), data_potential.reshape(CORES * rows)


def solution(mesh):
    return jax.shard_map(
        on_device,
        mesh=mesh,
        in_specs=(P("noise", "dp"), P("noise", "dp")),
        out_specs=(P("noise", "dp"), P("noise"), P("dp")),
        check_vma=False,
    )
```

```python
import functools
import math

import jax
import jax.numpy as jnp
from jax import lax
from jax.experimental import pallas as pl
from jax.experimental.pallas import tpu as pltpu
from jax.sharding import PartitionSpec as P

D = 16384
ITERS = 4
YS, XS, CORES = 4, 4, 2
LOG2E = math.log2(math.e)
VMEM = pl.BlockSpec(memory_space=pltpu.VMEM)
SMEM = pl.BlockSpec(memory_space=pltpu.SMEM)
PARAMS = pltpu.CompilerParams(vmem_limit_bytes=48 * 1024 * 1024)


def send(value, dy=0, dx=0, dc=0):
    pairs = []
    for y in range(YS):
        for x in range(XS):
            for c in range(CORES):
                source = (y * XS + x) * CORES + c
                target = ((y + dy) % YS * XS + (x + dx) % XS) * CORES + (c + dc) % CORES
                pairs.append((source, target))
    return lax.ppermute(value, "noise", pairs)


def send_z(value, ahead):
    size = lax.axis_size("dp")
    pairs = []
    for n in range(YS * XS * CORES):
        step = ahead if n % CORES == 0 else -ahead
        pairs += [(n * size + z, n * size + (z + step) % size) for z in range(size)]
    return lax.ppermute(value, ("noise", "dp"), pairs)


def gather4(block, **axis):
    (name,) = axis
    before, after = send(block, **{name: 1}), send(block, **{name: -1})
    return [block, before, send(block, **{name: 2}), after]


def squares_row(block):
    wide = block.astype(jnp.float32)
    column = jnp.sum(wide * wide, axis=1, keepdims=True)
    n = block.shape[0]
    row_at = lax.broadcasted_iota(jnp.int32, (n, n), 0)
    column_at = lax.broadcasted_iota(jnp.int32, (n, n), 1)
    return jnp.sum(jnp.where(row_at == column_at, column, 0.0), axis=0, keepdims=True)


def partial_kernel(scale, place_ref, x_here, x_there, *refs):
    ys, (own, ahead, back, ahead_rest, back_rest, x_all, y_all, y_squares, chunks) = refs[:YS], refs[YS:]
    rows = ys[0].shape[0]
    depth = chunks.shape[0]
    high = rows // depth
    z, y, x, c = place_ref[0], place_ref[1], place_ref[2], place_ref[3]
    for k in range(XS):
        at = lax.rem(x + XS - k, XS) * CORES
        block = slice(k * rows, (k + 1) * rows)
        x_all[at + c] = x_here[block, :]
        x_all[at + 1 - c] = x_there[block, :]
    for k in range(YS):
        at = pl.multiple_of(lax.rem(y + YS - k, YS) * rows, rows)
        y_all[pl.ds(at, rows), :] = ys[k][...]
    for k in range(YS):
        block = slice(k * rows, (k + 1) * rows)
        y_squares[:, block] = scale * squares_row(y_all[block, :])
    for k in range(XS * CORES):
        value = x_all[k]
        wide = value.astype(jnp.float32)
        x_squares = scale * jnp.sum(wide * wide, axis=1, keepdims=True)
        cross = lax.dot_general(
            value, y_all[...], (((1,), (1,)), ((), ())), preferred_element_type=jnp.float32
        )
        value = (2.0 * scale) * cross - x_squares - y_squares[...]
        for t in range(depth):
            at = jnp.where(c == 0, lax.rem(t + depth - z, depth), lax.rem(z + depth - t, depth))
            chunks[at, k * high : (k + 1) * high, :] = value[t * high : (t + 1) * high]
    middle = depth // 2
    own[...] = chunks[0]
    ahead[...] = chunks[middle]
    back[...] = chunks[middle + 1]
    for k in range(1, middle):
        ahead_rest[middle - 1 - k] = chunks[k]
    for k in range(middle + 2, depth):
        back_rest[k - middle - 2] = chunks[k]


def joined(parts):
    peak = jnp.max(parts, axis=0)
    return peak + jnp.log(jnp.sum(jnp.exp2(parts - peak), axis=0)) * LOG2E


def on_diagonal(n):
    rows = lax.broadcasted_iota(jnp.int32, (n, n), 0)
    return rows == lax.broadcasted_iota(jnp.int32, (n, n), 1)


def column_of(u, k):
    n = u.shape[1]
    return jnp.sum(jnp.where(on_diagonal(n), u[k : k + 1], 0.0), axis=1, keepdims=True)


def row_of(parts_ref, log_weight):
    v = log_weight - joined(parts_ref[...])
    return jnp.concatenate([v[k : k + 1] for k in range(YS)], axis=1)


def copy_out(out_ref):
    whole = out_ref[0]
    for k in range(1, out_ref.shape[0]):
        out_ref[k] = whole


def row_sums(a_ref, v, out_ref):
    n = out_ref.shape[2]
    for k in range(out_ref.shape[1]):
        value = a_ref[k * n : (k + 1) * n, :]
        if v is not None:
            value = value + v
        peak = jnp.max(value, axis=1, keepdims=True)
        total = jnp.sum(jnp.exp2(value - peak), axis=1, keepdims=True)
        part = peak + jnp.log(total) * LOG2E
        out_ref[0, k : k + 1, :] = jnp.sum(jnp.where(on_diagonal(n), part, 0.0), axis=0, keepdims=True)
    copy_out(out_ref)


def first_rows_kernel(place_ref, *refs):
    chunks, (a_ref, out_ref) = refs[:-2], refs[-2:]
    blocks, n = out_ref.shape[1:]
    depth = len(chunks)
    high = n // depth
    z, c = place_ref[0], place_ref[3]
    for k, chunk in enumerate(chunks):
        at = jnp.where(c == 0, lax.rem(z + k, depth), lax.rem(z + depth - k, depth)) * high
        for block in range(blocks):
            to = pl.ds(pl.multiple_of(block * n + at, high), high)
            a_ref[to, :] = chunk[block * high : (block + 1) * high, :]
    row_sums(a_ref, None, out_ref)


def rows_kernel(log_weight, a_ref, parts_ref, out_ref):
    row_sums(a_ref, row_of(parts_ref, log_weight), out_ref)


def columns_kernel(log_weight, a_ref, parts_ref, u_ref, out_ref, shifted):
    u = log_weight - joined(parts_ref[...])
    u_ref[...] = u
    blocks, n = u.shape
    width = a_ref.shape[1]
    peak = None
    for k in range(blocks):
        value = a_ref[k * n : (k + 1) * n, :] + column_of(u, k)
        shifted[k * n : (k + 1) * n, :] = value
        block_peak = jnp.max(value.reshape(n // 8, 8, width), axis=0)
        peak = block_peak if peak is None else jnp.maximum(peak, block_peak)
    peak = jnp.max(peak, axis=0, keepdims=True)
    total = jnp.zeros((8, width), jnp.float32)
    for k in range(blocks):
        value = jnp.exp2(shifted[k * n : (k + 1) * n, :] - peak)
        total = total + jnp.sum(value.reshape(n // 8, 8, width), axis=0)
    part = peak + jnp.log(jnp.sum(total, axis=0, keepdims=True)) * LOG2E
    for k in range(2 * YS):
        at = k % YS * n
        out_ref[0, k : k + 1, :] = part[:, at : at + n]
    copy_out(out_ref)


def plan_kernel(log_weight, a_ref, u_ref, parts_ref, out_ref):
    v = row_of(parts_ref, log_weight)
    u = u_ref[...] - log_weight
    blocks, n = u.shape
    top = v.astype(jnp.bfloat16).astype(jnp.float32)
    rest = v - top
    middle = rest.astype(jnp.bfloat16).astype(jnp.float32)
    extra = out_ref.shape[1] - n
    row = lax.broadcasted_iota(jnp.int32, (extra, v.shape[1]), 0)
    under = jnp.where(row == 0, top, jnp.where(row == 1, middle, jnp.where(row == 2, rest - middle, 0.0)))
    under = under.astype(jnp.bfloat16)
    for k in range(blocks):
        value = a_ref[k * n : (k + 1) * n, :] + (column_of(u, k) + v)
        out_ref[k, :n, :] = jnp.exp2(value).astype(jnp.bfloat16)
        out_ref[k, n:, :] = under


def target_kernel(unit, place_ref, plan_ref, u_ref, y_ref, out_ref, f_ref, g_ref, total, mass):
    step = pl.program_id(0)
    z, x, c = place_ref[0], place_ref[2], place_ref[3]
    blocks = plan_ref.shape[0]
    n = out_ref.shape[0]

    @pl.when(step == 0)
    def _():
        total[...] = jnp.zeros_like(total)
        mass[...] = jnp.zeros_like(mass)
        f_ref[...] = unit * u_ref[pl.ds(x * CORES + c, 1), :]

    plan = jnp.concatenate([plan_ref[k, :n, :] for k in range(blocks)], axis=1)
    mass[...] += jnp.sum(plan.astype(jnp.float32), axis=1, keepdims=True)
    total[...] += jnp.dot(plan, y_ref[...], preferred_element_type=jnp.float32)

    @pl.when(step == z // XS)
    def _():
        for k in range(CORES):
            v = plan_ref[lax.rem(z, XS) * CORES + k, n:, :].astype(jnp.float32)
            g_ref[:, k * n : (k + 1) * n] = unit * (v[0:1] + v[1:2] + v[2:3])

    @pl.when(step == YS - 1)
    def _():
        out_ref[...] = (total[...] / mass[...]).astype(out_ref.dtype)


def on_device(noise_rows, data_rows):
    rows, features = noise_rows.shape
    tokens = rows * lax.axis_size("noise")
    depth = lax.axis_size("dp")
    me, z = lax.axis_index("noise"), lax.axis_index("dp")
    place = jnp.stack([z, me // (XS * CORES), me // CORES % XS, me % CORES]).astype(jnp.int32)
    epsilon = 0.7 / math.sqrt(D)
    log_weight = -math.log2(tokens)
    f32 = jnp.float32

    group = XS * CORES
    y_groups = [[y * group + k for y in range(YS)] for k in range(group)]
    x_groups = [[y * group + k for k in range(group)] for y in range(YS)]

    def swap(value, groups):
        return lax.all_to_all(value, "noise", 0, 0, axis_index_groups=groups, tiled=True)

    xs, ys = lax.optimization_barrier((gather4(noise_rows, dx=1), gather4(data_rows, dy=1)))
    x_here = jnp.concatenate(xs, axis=0)
    x_there = send(x_here, dc=1)
    tall, wide = group * rows, YS * rows
    middle = depth // 2
    chunk = (tall // depth, wide)
    own, ahead, back, ahead_rest, back_rest = pl.pallas_call(
        functools.partial(partial_kernel, LOG2E / (epsilon * D)),
        out_shape=[
            jax.ShapeDtypeStruct(chunk, f32),
            jax.ShapeDtypeStruct(chunk, f32),
            jax.ShapeDtypeStruct(chunk, f32),
            jax.ShapeDtypeStruct((middle - 1,) + chunk, f32),
            jax.ShapeDtypeStruct((middle - 2,) + chunk, f32),
        ],
        in_specs=[SMEM] + [VMEM] * (2 + YS),
        out_specs=[VMEM] * 5,
        scratch_shapes=[
            pltpu.VMEM((group, rows, features), jnp.bfloat16),
            pltpu.VMEM((YS * rows, features), jnp.bfloat16),
            pltpu.VMEM((1, wide), f32),
            pltpu.VMEM((depth,) + chunk, f32),
        ],
        compiler_params=PARAMS,
    )(place, x_here, x_there, *ys)
    late_rows, own = lax.optimization_barrier((data_rows, own))

    for step in range(middle):
        ahead = send_z(ahead, 1)
        if step < middle - 1:
            ahead = ahead + ahead_rest[step]
            back = send_z(back, -1)
            if step < middle - 2:
                back = back + back_rest[step]
    own = own + ahead + back

    chunks = [own] * depth
    ahead, back = own, own
    for step in range(1, middle + 1):
        ahead = send_z(ahead, 1)
        chunks[depth - step] = ahead
        if step < middle:
            back = send_z(back, -1)
            chunks[step] = back
    row_shape = jax.ShapeDtypeStruct((group, group, rows), f32)
    column_shape = jax.ShapeDtypeStruct((YS, 2 * YS, rows), f32)
    u_shape = jax.ShapeDtypeStruct((group, rows), f32)
    a, part = pl.pallas_call(
        first_rows_kernel,
        out_shape=[jax.ShapeDtypeStruct((tall, wide), f32), row_shape],
        in_specs=[SMEM] + [VMEM] * depth,
        out_specs=[VMEM] * 2,
        compiler_params=PARAMS,
    )(place, *chunks)
    for step in range(ITERS):
        if step > 0:
            part = pl.pallas_call(
                functools.partial(rows_kernel, log_weight),
                out_shape=row_shape,
                in_specs=[VMEM] * 2,
                out_specs=VMEM,
                compiler_params=PARAMS,
            )(a, part)
        part = swap(part, x_groups)
        u, part = pl.pallas_call(
            functools.partial(columns_kernel, log_weight),
            out_shape=[u_shape, column_shape],
            in_specs=[VMEM] * 2,
            out_specs=[VMEM] * 2,
            scratch_shapes=[pltpu.VMEM((tall, wide), f32)],
            compiler_params=PARAMS,
        )(a, part)
        part = swap(part, y_groups)
    plan = pl.pallas_call(
        functools.partial(plan_kernel, log_weight),
        out_shape=jax.ShapeDtypeStruct((group, rows + 16, wide), jnp.bfloat16),
        in_specs=[VMEM] * 3,
        out_specs=VMEM,
        compiler_params=PARAMS,
    )(a, u, part)
    plan = swap(plan, x_groups)

    everything = lax.all_gather(late_rows, "noise", axis=0, tiled=True)
    targets, noise_potential, data_potential = pl.pallas_call(
        functools.partial(target_kernel, epsilon / LOG2E),
        grid=(YS,),
        out_shape=[
            jax.ShapeDtypeStruct((rows, features), jnp.bfloat16),
            jax.ShapeDtypeStruct((1, rows), f32),
            jax.ShapeDtypeStruct((1, CORES * rows), f32),
        ],
        in_specs=[
            SMEM,
            pl.BlockSpec((group, rows + 16, rows), lambda k: (0, 0, k)),
            pl.BlockSpec((group, rows), lambda k: (0, 0)),
            pl.BlockSpec((group * rows, features), lambda k: (k, 0)),
        ],
        out_specs=[
            pl.BlockSpec((rows, features), lambda k: (0, 0)),
            pl.BlockSpec((1, rows), lambda k: (0, 0)),
            pl.BlockSpec((1, CORES * rows), lambda k: (0, 0)),
        ],
        scratch_shapes=[
            pltpu.VMEM((rows, features), f32),
            pltpu.VMEM((rows, 1), f32),
        ],
        compiler_params=PARAMS,
    )(place, plan, u, everything)
    return targets, noise_potential.reshape(rows), data_potential.reshape(CORES * rows)


def solution(mesh):
    return jax.shard_map(
        on_device,
        mesh=mesh,
        in_specs=(P("noise", "dp"), P("noise", "dp")),
        out_specs=(P("noise", "dp"), P("noise"), P("dp")),
        check_vma=False,
    )
```

```python
import functools
import math

import jax
import jax.numpy as jnp
from jax import lax
from jax.experimental import pallas as pl
from jax.experimental.pallas import tpu as pltpu
from jax.sharding import PartitionSpec as P

D = 16384
ITERS = 4
YS, XS, CORES = 4, 4, 2
LOG2E = math.log2(math.e)
VMEM = pl.BlockSpec(memory_space=pltpu.VMEM)
SMEM = pl.BlockSpec(memory_space=pltpu.SMEM)
PARAMS = pltpu.CompilerParams(vmem_limit_bytes=48 * 1024 * 1024)


def send(value, dy=0, dx=0, dc=0):
    pairs = []
    for y in range(YS):
        for x in range(XS):
            for c in range(CORES):
                source = (y * XS + x) * CORES + c
                target = ((y + dy) % YS * XS + (x + dx) % XS) * CORES + (c + dc) % CORES
                pairs.append((source, target))
    return lax.ppermute(value, "noise", pairs)


def send_z(value, ahead):
    size = lax.axis_size("dp")
    pairs = []
    for n in range(YS * XS * CORES):
        step = ahead if n % CORES == 0 else -ahead
        pairs += [(n * size + z, n * size + (z + step) % size) for z in range(size)]
    return lax.ppermute(value, ("noise", "dp"), pairs)


def gather4(block, **axis):
    (name,) = axis
    before, after = send(block, **{name: 1}), send(block, **{name: -1})
    return [block, before, send(block, **{name: 2}), after]


def squares_row(block):
    wide = block.astype(jnp.float32)
    column = jnp.sum(wide * wide, axis=1, keepdims=True)
    n = block.shape[0]
    row_at = lax.broadcasted_iota(jnp.int32, (n, n), 0)
    column_at = lax.broadcasted_iota(jnp.int32, (n, n), 1)
    return jnp.sum(jnp.where(row_at == column_at, column, 0.0), axis=0, keepdims=True)


def partial_kernel(scale, place_ref, x_here, x_there, *refs):
    ys, (own, ahead, back, ahead_rest, back_rest, x_all, y_all, y_squares, chunks) = refs[:YS], refs[YS:]
    rows = ys[0].shape[0]
    depth = chunks.shape[0]
    high = rows // depth
    z, y, x, c = place_ref[0], place_ref[1], place_ref[2], place_ref[3]
    for k in range(XS):
        at = lax.rem(x + XS - k, XS) * CORES
        block = slice(k * rows, (k + 1) * rows)
        x_all[at + c] = x_here[block, :]
        x_all[at + 1 - c] = x_there[block, :]
    for k in range(YS):
        at = pl.multiple_of(lax.rem(y + YS - k, YS) * rows, rows)
        y_all[pl.ds(at, rows), :] = ys[k][...]
    for k in range(YS):
        block = slice(k * rows, (k + 1) * rows)
        y_squares[:, block] = scale * squares_row(y_all[block, :])
    for k in range(XS * CORES):
        value = x_all[k]
        wide = value.astype(jnp.float32)
        x_squares = scale * jnp.sum(wide * wide, axis=1, keepdims=True)
        cross = lax.dot_general(
            value, y_all[...], (((1,), (1,)), ((), ())), preferred_element_type=jnp.float32
        )
        value = (2.0 * scale) * cross - x_squares - y_squares[...]
        for t in range(depth):
            at = jnp.where(c == 0, lax.rem(t + depth - z, depth), lax.rem(z + depth - t, depth))
            chunks[at, k * high : (k + 1) * high, :] = value[t * high : (t + 1) * high]
    middle = depth // 2
    own[...] = chunks[0]
    ahead[...] = chunks[middle]
    back[...] = chunks[middle + 1]
    for k in range(1, middle):
        ahead_rest[middle - 1 - k] = chunks[k]
    for k in range(middle + 2, depth):
        back_rest[k - middle - 2] = chunks[k]


def joined(parts):
    peak = jnp.max(parts, axis=0)
    return peak + jnp.log(jnp.sum(jnp.exp2(parts - peak), axis=0)) * LOG2E


def on_diagonal(n):
    rows = lax.broadcasted_iota(jnp.int32, (n, n), 0)
    return rows == lax.broadcasted_iota(jnp.int32, (n, n), 1)


def column_of(u, k):
    n = u.shape[1]
    return jnp.sum(jnp.where(on_diagonal(n), u[k : k + 1], 0.0), axis=1, keepdims=True)


def row_of(parts_ref, log_weight):
    v = log_weight - joined(parts_ref[...])
    return jnp.concatenate([v[k : k + 1] for k in range(v.shape[0])], axis=1)


def copy_out(out_ref):
    whole = out_ref[0]
    for k in range(1, out_ref.shape[0]):
        out_ref[k] = whole


def row_sums(a_ref, v, out_ref, n):
    for k in range(a_ref.shape[0] // n):
        value = a_ref[k * n : (k + 1) * n, :]
        if v is not None:
            value = value + v
        peak = jnp.max(value, axis=1, keepdims=True)
        total = jnp.sum(jnp.exp2(value - peak), axis=1, keepdims=True)
        part = peak + jnp.log(total) * LOG2E
        out_ref[0, k : k + 1, :] = jnp.sum(jnp.where(on_diagonal(n), part, 0.0), axis=0, keepdims=True)
    copy_out(out_ref)


def first_rows_kernel(a_ref, out_ref):
    row_sums(a_ref, None, out_ref, out_ref.shape[2])


def rows_kernel(log_weight, a_ref, parts_ref, out_ref):
    row_sums(a_ref, row_of(parts_ref, log_weight), out_ref, out_ref.shape[2])


def all_rows_kernel(log_weight, chunks_ref, parts_ref, a_ref, out_ref):
    blocks, n = out_ref.shape[1:]
    depth = chunks_ref.shape[0]
    high = n // depth
    for z in range(depth):
        for block in range(blocks):
            at = block * n + z * high
            a_ref[at : at + high, :] = chunks_ref[z, block * high : (block + 1) * high, :]
    row_sums(a_ref, row_of(parts_ref, log_weight), out_ref, n)


def columns_kernel(log_weight, a_ref, parts_ref, u_ref, out_ref, shifted):
    u = log_weight - joined(parts_ref[...])
    u_ref[...] = u
    blocks, n = u.shape
    width = a_ref.shape[1]
    peak = None
    for k in range(blocks):
        value = a_ref[k * n : (k + 1) * n, :] + column_of(u, k)
        shifted[k * n : (k + 1) * n, :] = value
        block_peak = jnp.max(value.reshape(n // 8, 8, width), axis=0)
        peak = block_peak if peak is None else jnp.maximum(peak, block_peak)
    peak = jnp.max(peak, axis=0, keepdims=True)
    total = jnp.zeros((8, width), jnp.float32)
    for k in range(blocks):
        value = jnp.exp2(shifted[k * n : (k + 1) * n, :] - peak)
        total = total + jnp.sum(value.reshape(n // 8, 8, width), axis=0)
    part = peak + jnp.log(jnp.sum(total, axis=0, keepdims=True)) * LOG2E
    lanes = out_ref.shape[2]
    for k in range(out_ref.shape[1]):
        out_ref[0, k : k + 1, :] = part[:, k * lanes : (k + 1) * lanes]
    copy_out(out_ref)


def plan_kernel(log_weight, a_ref, u_ref, parts_ref, out_ref):
    v = row_of(parts_ref, log_weight)
    u = u_ref[...] - log_weight
    blocks, n = u.shape
    top = v.astype(jnp.bfloat16).astype(jnp.float32)
    rest = v - top
    middle = rest.astype(jnp.bfloat16).astype(jnp.float32)
    extra = out_ref.shape[1] - n
    row = lax.broadcasted_iota(jnp.int32, (extra, v.shape[1]), 0)
    under = jnp.where(row == 0, top, jnp.where(row == 1, middle, jnp.where(row == 2, rest - middle, 0.0)))
    under = under.astype(jnp.bfloat16)
    for k in range(blocks):
        value = a_ref[k * n : (k + 1) * n, :] + (column_of(u, k) + v)
        out_ref[k, :n, :] = jnp.exp2(value).astype(jnp.bfloat16)
        out_ref[k, n:, :] = under


def target_kernel(unit, place_ref, plan_ref, u_ref, y_ref, out_ref, f_ref, g_ref, total, mass):
    step = pl.program_id(0)
    z, x, c = place_ref[0], place_ref[2], place_ref[3]
    blocks = plan_ref.shape[0]
    n = out_ref.shape[0]

    @pl.when(step == 0)
    def _():
        total[...] = jnp.zeros_like(total)
        mass[...] = jnp.zeros_like(mass)
        f_ref[...] = unit * u_ref[pl.ds(x * CORES + c, 1), :]

    plan = jnp.concatenate([plan_ref[k, :n, :] for k in range(blocks)], axis=1)
    mass[...] += jnp.sum(plan.astype(jnp.float32), axis=1, keepdims=True)
    total[...] += jnp.dot(plan, y_ref[...], preferred_element_type=jnp.float32)

    @pl.when(step == z // XS)
    def _():
        for k in range(CORES):
            v = plan_ref[lax.rem(z, XS) * CORES + k, n:, :].astype(jnp.float32)
            g_ref[:, k * n : (k + 1) * n] = unit * (v[0:1] + v[1:2] + v[2:3])

    @pl.when(step == YS - 1)
    def _():
        out_ref[...] = (total[...] / mass[...]).astype(out_ref.dtype)


def on_device(noise_rows, data_rows):
    rows, features = noise_rows.shape
    tokens = rows * lax.axis_size("noise")
    depth = lax.axis_size("dp")
    me, z = lax.axis_index("noise"), lax.axis_index("dp")
    place = jnp.stack([z, me // (XS * CORES), me // CORES % XS, me % CORES]).astype(jnp.int32)
    epsilon = 0.7 / math.sqrt(D)
    log_weight = -math.log2(tokens)
    f32 = jnp.float32

    group = XS * CORES
    y_groups = [[y * group + k for y in range(YS)] for k in range(group)]
    x_groups = [[y * group + k for k in range(group)] for y in range(YS)]

    def swap(value, groups):
        return lax.all_to_all(value, "noise", 0, 0, axis_index_groups=groups, tiled=True)

    xs, ys = lax.optimization_barrier((gather4(noise_rows, dx=1), gather4(data_rows, dy=1)))
    x_here = jnp.concatenate(xs, axis=0)
    x_there = send(x_here, dc=1)
    tall, wide = group * rows, YS * rows
    middle = depth // 2
    chunk = (tall // depth, wide)
    own, ahead, back, ahead_rest, back_rest = pl.pallas_call(
        functools.partial(partial_kernel, LOG2E / (epsilon * D)),
        out_shape=[
            jax.ShapeDtypeStruct(chunk, f32),
            jax.ShapeDtypeStruct(chunk, f32),
            jax.ShapeDtypeStruct(chunk, f32),
            jax.ShapeDtypeStruct((middle - 1,) + chunk, f32),
            jax.ShapeDtypeStruct((middle - 2,) + chunk, f32),
        ],
        in_specs=[SMEM] + [VMEM] * (2 + YS),
        out_specs=[VMEM] * 5,
        scratch_shapes=[
            pltpu.VMEM((group, rows, features), jnp.bfloat16),
            pltpu.VMEM((YS * rows, features), jnp.bfloat16),
            pltpu.VMEM((1, wide), f32),
            pltpu.VMEM((depth,) + chunk, f32),
        ],
        compiler_params=PARAMS,
    )(place, x_here, x_there, *ys)
    late_rows, own = lax.optimization_barrier((data_rows, own))

    for step in range(middle):
        ahead = send_z(ahead, 1)
        if step < middle - 1:
            ahead = ahead + ahead_rest[step]
            back = send_z(back, -1)
            if step < middle - 2:
                back = back + back_rest[step]
    own = own + ahead + back

    gathered = lax.all_gather(own, "dp")
    z_groups = [
        [((y * group) + k) * depth + d for y in range(YS) for d in range(depth)] for k in range(group)
    ]
    sharers = YS * depth
    few = tall // depth
    for step in range(ITERS):
        last = step == ITERS - 1
        lines, n = (group, rows) if last else (1, few)
        row_shape = jax.ShapeDtypeStruct((group, lines, n), f32)
        if step == 0:
            part = pl.pallas_call(
                first_rows_kernel,
                out_shape=row_shape,
                in_specs=[VMEM],
                out_specs=VMEM,
                compiler_params=PARAMS,
            )(own)
        elif not last:
            part = pl.pallas_call(
                functools.partial(rows_kernel, log_weight),
                out_shape=row_shape,
                in_specs=[VMEM] * 2,
                out_specs=VMEM,
                compiler_params=PARAMS,
            )(own, part)
        else:
            a, part = pl.pallas_call(
                functools.partial(all_rows_kernel, log_weight),
                out_shape=[jax.ShapeDtypeStruct((tall, wide), f32), row_shape],
                in_specs=[VMEM] * 2,
                out_specs=[VMEM] * 2,
                compiler_params=PARAMS,
            )(gathered, part)
        part = swap(part, x_groups)
        u, part = pl.pallas_call(
            functools.partial(columns_kernel, log_weight),
            out_shape=[
                jax.ShapeDtypeStruct((lines, n), f32),
                jax.ShapeDtypeStruct((YS if last else sharers, YS, rows), f32),
            ],
            in_specs=[VMEM] * 2,
            out_specs=[VMEM] * 2,
            scratch_shapes=[pltpu.VMEM((lines * n, wide), f32)],
            compiler_params=PARAMS,
        )(a if last else own, part)
        if last:
            part = swap(part, y_groups)
        else:
            part = lax.all_to_all(
                part, ("noise", "dp"), 0, 0, axis_index_groups=z_groups, tiled=True
            )
    plan = pl.pallas_call(
        functools.partial(plan_kernel, log_weight),
        out_shape=jax.ShapeDtypeStruct((group, rows + 16, wide), jnp.bfloat16),
        in_specs=[VMEM] * 3,
        out_specs=VMEM,
        compiler_params=PARAMS,
    )(a, u, part)
    plan = swap(plan, x_groups)

    everything = lax.all_gather(late_rows, "noise", axis=0, tiled=True)
    targets, noise_potential, data_potential = pl.pallas_call(
        functools.partial(target_kernel, epsilon / LOG2E),
        grid=(YS,),
        out_shape=[
            jax.ShapeDtypeStruct((rows, features), jnp.bfloat16),
            jax.ShapeDtypeStruct((1, rows), f32),
            jax.ShapeDtypeStruct((1, CORES * rows), f32),
        ],
        in_specs=[
            SMEM,
            pl.BlockSpec((group, rows + 16, rows), lambda k: (0, 0, k)),
            pl.BlockSpec((group, rows), lambda k: (0, 0)),
            pl.BlockSpec((group * rows, features), lambda k: (k, 0)),
        ],
        out_specs=[
            pl.BlockSpec((rows, features), lambda k: (0, 0)),
            pl.BlockSpec((1, rows), lambda k: (0, 0)),
            pl.BlockSpec((1, CORES * rows), lambda k: (0, 0)),
        ],
        scratch_shapes=[
            pltpu.VMEM((rows, features), f32),
            pltpu.VMEM((rows, 1), f32),
        ],
        compiler_params=PARAMS,
    )(place, plan, u, everything)
    return targets, noise_potential.reshape(rows), data_potential.reshape(CORES * rows)


def solution(mesh):
    return jax.shard_map(
        on_device,
        mesh=mesh,
        in_specs=(P("noise", "dp"), P("noise", "dp")),
        out_specs=(P("noise", "dp"), P("noise"), P("dp")),
        check_vma=False,
    )
```

```python
import functools
import math

import jax
import jax.numpy as jnp
from jax import lax
from jax.experimental import pallas as pl
from jax.experimental.pallas import tpu as pltpu
from jax.sharding import PartitionSpec as P

D = 16384
ITERS = 4
YS, XS, CORES = 4, 4, 2
LOG2E = math.log2(math.e)
VMEM = pl.BlockSpec(memory_space=pltpu.VMEM)
SMEM = pl.BlockSpec(memory_space=pltpu.SMEM)
PARAMS = pltpu.CompilerParams(vmem_limit_bytes=48 * 1024 * 1024)


def noise_pairs(target):
    pairs = []
    for y in range(YS):
        for x in range(XS):
            for c in range(CORES):
                to_y, to_x, to_c = target(y, x, c)
                pairs.append(((y * XS + x) * CORES + c, (to_y * XS + to_x) * CORES + to_c))
    return pairs


def to_other_core(value):
    return lax.ppermute(value, "noise", noise_pairs(lambda y, x, c: (y, x, 1 - c)))


FIRST, SECOND, BOTH = (1, 3), (3, 1), 2
PLACES = ((0, 0), FIRST, SECOND, (BOTH, BOTH))


def swap_x(value, by):
    return lax.ppermute(value, "noise", noise_pairs(lambda y, x, c: (y, x ^ by[c], c)))


def swap_y(value, by):
    return lax.ppermute(value, "noise", noise_pairs(lambda y, x, c: (y ^ by[c], x, c)))


def send_z(value, target):
    size = lax.axis_size("dp")
    pairs = []
    for n in range(YS * XS * CORES):
        pairs += [(n * size + z, n * size + target(z, n % CORES) % size) for z in range(size)]
    return lax.ppermute(value, ("noise", "dp"), pairs)


def z_partner(z, c):
    return z ^ 1 if c == 0 else z + 1 if z % 2 else z - 1


def squares_row(block):
    wide = block.astype(jnp.float32)
    column = jnp.sum(wide * wide, axis=1, keepdims=True)
    n = block.shape[0]
    row_at = lax.broadcasted_iota(jnp.int32, (n, n), 0)
    column_at = lax.broadcasted_iota(jnp.int32, (n, n), 1)
    return jnp.sum(jnp.where(row_at == column_at, column, 0.0), axis=0, keepdims=True)


def partial_kernel(scale, place_ref, *refs):
    here, there, ys = refs[:2], refs[2:4], refs[4:6]
    keep, give, x_all, y_all, y_squares, chunks = refs[6:]
    rows = here[0].shape[0] // 2
    depth = chunks.shape[0]
    high = rows // depth
    z, y, x, c = place_ref[0], place_ref[1], place_ref[2], place_ref[3]
    for k, (first, second) in enumerate(PLACES):
        block = slice(k % 2 * rows, (k % 2 + 1) * rows)
        mine, other = jnp.where(c == 0, first, second), jnp.where(c == 0, second, first)
        x_all[lax.bitwise_xor(x, mine) * CORES + c] = here[k // 2][block, :]
        x_all[lax.bitwise_xor(x, other) * CORES + 1 - c] = there[k // 2][block, :]
        at = pl.multiple_of(lax.bitwise_xor(y, mine) * rows, rows)
        y_all[pl.ds(at, rows), :] = ys[k // 2][block, :]
    for k in range(YS):
        block = slice(k * rows, (k + 1) * rows)
        y_squares[:, block] = scale * squares_row(y_all[block, :])
    up = jnp.where(c == 0, lax.rem(z, 2) == 0, lax.rem(z, 2) == 1)
    partner = lax.rem(z + jnp.where(up, 1, depth - 1), depth)
    places = []
    for t in range(depth):
        same = lax.rem(z + t, 2) == 0
        base = jnp.where(same, z, partner)
        ahead = jnp.where(c == 0, lax.rem(t + depth - base, depth), lax.rem(base + depth - t, depth))
        places.append(ahead // 2 + jnp.where(same, 0, depth // 2))
    for k in range(XS * CORES):
        value = x_all[k]
        wide = value.astype(jnp.float32)
        x_squares = scale * jnp.sum(wide * wide, axis=1, keepdims=True)
        cross = lax.dot_general(
            value, y_all[...], (((1,), (1,)), ((), ())), preferred_element_type=jnp.float32
        )
        value = (2.0 * scale) * cross - x_squares - y_squares[...]
        for t in range(depth):
            chunks[places[t], k * high : (k + 1) * high, :] = value[t * high : (t + 1) * high]
    for k in range(depth // 2):
        keep[k] = chunks[k]
        give[k] = chunks[depth // 2 + k]


def pair_kernel(keep, got, own, ahead, back, ahead_rest, back_rest):
    own[...] = keep[0] + got[0]
    middle = keep.shape[0] // 2
    ahead[...] = keep[middle] + got[middle]
    back[...] = keep[middle + 1] + got[middle + 1]
    for k in range(1, middle):
        ahead_rest[middle - 1 - k] = keep[k] + got[k]
    for k in range(middle + 2, keep.shape[0]):
        back_rest[k - middle - 2] = keep[k] + got[k]


def joined(parts):
    peak = jnp.max(parts, axis=0)
    return peak + jnp.log(jnp.sum(jnp.exp2(parts - peak), axis=0)) * LOG2E


def on_diagonal(n):
    rows = lax.broadcasted_iota(jnp.int32, (n, n), 0)
    return rows == lax.broadcasted_iota(jnp.int32, (n, n), 1)


def column_of(u, k):
    n = u.shape[1]
    return jnp.sum(jnp.where(on_diagonal(n), u[k : k + 1], 0.0), axis=1, keepdims=True)


def row_of(parts_ref, log_weight):
    v = log_weight - joined(parts_ref[...])
    return jnp.concatenate([v[k : k + 1] for k in range(v.shape[0])], axis=1)


def copy_out(out_ref):
    whole = out_ref[0]
    for k in range(1, out_ref.shape[0]):
        out_ref[k] = whole


def row_sums(a_ref, v, out_ref, n):
    for k in range(a_ref.shape[0] // n):
        value = a_ref[k * n : (k + 1) * n, :]
        if v is not None:
            value = value + v
        peak = jnp.max(value, axis=1, keepdims=True)
        total = jnp.sum(jnp.exp2(value - peak), axis=1, keepdims=True)
        part = peak + jnp.log(total) * LOG2E
        out_ref[0, k : k + 1, :] = jnp.sum(jnp.where(on_diagonal(n), part, 0.0), axis=0, keepdims=True)
    copy_out(out_ref)


def first_rows_kernel(a_ref, out_ref):
    row_sums(a_ref, None, out_ref, out_ref.shape[2])


def rows_kernel(log_weight, a_ref, parts_ref, out_ref):
    row_sums(a_ref, row_of(parts_ref, log_weight), out_ref, out_ref.shape[2])


def all_rows_kernel(log_weight, chunks_ref, parts_ref, a_ref, out_ref):
    blocks, n = out_ref.shape[1:]
    depth = chunks_ref.shape[0]
    high = n // depth
    for z in range(depth):
        for block in range(blocks):
            at = block * n + z * high
            a_ref[at : at + high, :] = chunks_ref[z, block * high : (block + 1) * high, :]
    row_sums(a_ref, row_of(parts_ref, log_weight), out_ref, n)


def columns_kernel(log_weight, a_ref, parts_ref, u_ref, out_ref, shifted):
    u = log_weight - joined(parts_ref[...])
    u_ref[...] = u
    blocks, n = u.shape
    width = a_ref.shape[1]
    peak = None
    for k in range(blocks):
        value = a_ref[k * n : (k + 1) * n, :] + column_of(u, k)
        shifted[k * n : (k + 1) * n, :] = value
        block_peak = jnp.max(value.reshape(n // 8, 8, width), axis=0)
        peak = block_peak if peak is None else jnp.maximum(peak, block_peak)
    peak = jnp.max(peak, axis=0, keepdims=True)
    total = jnp.zeros((8, width), jnp.float32)
    for k in range(blocks):
        value = jnp.exp2(shifted[k * n : (k + 1) * n, :] - peak)
        total = total + jnp.sum(value.reshape(n // 8, 8, width), axis=0)
    part = peak + jnp.log(jnp.sum(total, axis=0, keepdims=True)) * LOG2E
    lanes = out_ref.shape[2]
    for k in range(out_ref.shape[1]):
        out_ref[0, k : k + 1, :] = part[:, k * lanes : (k + 1) * lanes]
    copy_out(out_ref)


def join_kernel(parts_ref, out_ref):
    out_ref[0] = joined(parts_ref[...])
    copy_out(out_ref)


def plan_kernel(log_weight, a_ref, u_ref, parts_ref, out_ref):
    v = row_of(parts_ref, log_weight)
    u = u_ref[...] - log_weight
    blocks, n = u.shape
    top = v.astype(jnp.bfloat16).astype(jnp.float32)
    rest = v - top
    middle = rest.astype(jnp.bfloat16).astype(jnp.float32)
    extra = out_ref.shape[1] - n
    row = lax.broadcasted_iota(jnp.int32, (extra, v.shape[1]), 0)
    under = jnp.where(row == 0, top, jnp.where(row == 1, middle, jnp.where(row == 2, rest - middle, 0.0)))
    under = under.astype(jnp.bfloat16)
    for k in range(blocks):
        value = a_ref[k * n : (k + 1) * n, :] + (column_of(u, k) + v)
        out_ref[k, :n, :] = jnp.exp2(value).astype(jnp.bfloat16)
        out_ref[k, n:, :] = under


def target_kernel(unit, place_ref, plan_ref, u_ref, y_ref, out_ref, f_ref, g_ref, total, mass):
    step = pl.program_id(0)
    z, x, c = place_ref[0], place_ref[2], place_ref[3]
    blocks = plan_ref.shape[0]
    n = out_ref.shape[0]

    @pl.when(step == 0)
    def _():
        total[...] = jnp.zeros_like(total)
        mass[...] = jnp.zeros_like(mass)
        f_ref[...] = unit * u_ref[pl.ds(x * CORES + c, 1), :]

    plan = jnp.concatenate([plan_ref[k, :n, :] for k in range(blocks)], axis=1)
    mass[...] += jnp.sum(plan.astype(jnp.float32), axis=1, keepdims=True)
    total[...] += jnp.dot(plan, y_ref[...], preferred_element_type=jnp.float32)

    @pl.when(step == z // XS)
    def _():
        for k in range(CORES):
            v = plan_ref[lax.rem(z, XS) * CORES + k, n:, :].astype(jnp.float32)
            g_ref[:, k * n : (k + 1) * n] = unit * (v[0:1] + v[1:2] + v[2:3])

    @pl.when(step == YS - 1)
    def _():
        out_ref[...] = (total[...] / mass[...]).astype(out_ref.dtype)


def on_device(noise_rows, data_rows):
    rows, features = noise_rows.shape
    tokens = rows * lax.axis_size("noise")
    depth = lax.axis_size("dp")
    me, z = lax.axis_index("noise"), lax.axis_index("dp")
    place = jnp.stack([z, me // (XS * CORES), me // CORES % XS, me % CORES]).astype(jnp.int32)
    epsilon = 0.7 / math.sqrt(D)
    log_weight = -math.log2(tokens)
    f32 = jnp.float32

    group = XS * CORES
    y_groups = [[y * group + k for y in range(YS)] for k in range(group)]
    x_groups = [[y * group + k for k in range(group)] for y in range(YS)]

    def swap(value, groups):
        return lax.all_to_all(value, "noise", 0, 0, axis_index_groups=groups, tiled=True)

    x_near = jnp.concatenate([noise_rows, swap_x(noise_rows, FIRST)], axis=0)
    y_near = jnp.concatenate([data_rows, swap_y(data_rows, FIRST)], axis=0)
    x_near, y_near = lax.optimization_barrier((x_near, y_near))
    x_far, y_far = swap_x(x_near, SECOND), swap_y(y_near, SECOND)
    x_far, y_far, late_rows = lax.optimization_barrier((x_far, y_far, data_rows))
    everything = lax.all_gather(late_rows, "noise", axis=0, tiled=True)
    tall, wide = group * rows, YS * rows
    half = depth // 2
    middle = half // 2
    chunk = (tall // depth, wide)
    keep, give = pl.pallas_call(
        functools.partial(partial_kernel, LOG2E / (epsilon * D)),
        out_shape=[jax.ShapeDtypeStruct((half,) + chunk, f32)] * 2,
        in_specs=[SMEM] + [VMEM] * 6,
        out_specs=[VMEM] * 2,
        scratch_shapes=[
            pltpu.VMEM((group, rows, features), jnp.bfloat16),
            pltpu.VMEM((YS * rows, features), jnp.bfloat16),
            pltpu.VMEM((1, wide), f32),
            pltpu.VMEM((depth,) + chunk, f32),
        ],
        compiler_params=PARAMS,
    )(place, x_near, x_far, to_other_core(x_near), to_other_core(x_far), y_near, y_far)

    got = send_z(give, z_partner)
    own, ahead, back, ahead_rest, back_rest = pl.pallas_call(
        pair_kernel,
        out_shape=[
            jax.ShapeDtypeStruct(chunk, f32),
            jax.ShapeDtypeStruct(chunk, f32),
            jax.ShapeDtypeStruct(chunk, f32),
            jax.ShapeDtypeStruct((middle - 1,) + chunk, f32),
            jax.ShapeDtypeStruct((middle - 2,) + chunk, f32),
        ],
        in_specs=[VMEM] * 2,
        out_specs=[VMEM] * 5,
        compiler_params=PARAMS,
    )(keep, got)
    for step in range(middle):
        ahead = send_z(ahead, lambda z, c: z + 2 if c == 0 else z - 2)
        if step < middle - 1:
            ahead = ahead + ahead_rest[step]
            back = send_z(back, lambda z, c: z - 2 if c == 0 else z + 2)
            if step < middle - 2:
                back = back + back_rest[step]
    own = own + ahead + back

    everything, own = lax.optimization_barrier((everything, own))
    gathered = lax.all_gather(own, "dp")
    few = tall // depth
    for step in range(ITERS):
        last = step == ITERS - 1
        lines, n = (group, rows) if last else (1, few)
        row_shape = jax.ShapeDtypeStruct((group, lines, n), f32)
        if step == 0:
            part = pl.pallas_call(
                first_rows_kernel,
                out_shape=row_shape,
                in_specs=[VMEM],
                out_specs=VMEM,
                compiler_params=PARAMS,
            )(own)
        elif not last:
            part = pl.pallas_call(
                functools.partial(rows_kernel, log_weight),
                out_shape=row_shape,
                in_specs=[VMEM] * 2,
                out_specs=VMEM,
                compiler_params=PARAMS,
            )(own, part)
        else:
            a, part = pl.pallas_call(
                functools.partial(all_rows_kernel, log_weight),
                out_shape=[jax.ShapeDtypeStruct((tall, wide), f32), row_shape],
                in_specs=[VMEM] * 2,
                out_specs=[VMEM] * 2,
                compiler_params=PARAMS,
            )(gathered, part)
        part = swap(part, x_groups)
        u, part = pl.pallas_call(
            functools.partial(columns_kernel, log_weight),
            out_shape=[
                jax.ShapeDtypeStruct((lines, n), f32),
                jax.ShapeDtypeStruct((YS if last else depth, YS, rows), f32),
            ],
            in_specs=[VMEM] * 2,
            out_specs=[VMEM] * 2,
            scratch_shapes=[pltpu.VMEM((lines * n, wide), f32)],
            compiler_params=PARAMS,
        )(a if last else own, part)
        if not last:
            part = pl.pallas_call(
                join_kernel,
                out_shape=jax.ShapeDtypeStruct((YS, YS, rows), f32),
                in_specs=[VMEM],
                out_specs=VMEM,
                compiler_params=PARAMS,
            )(lax.all_to_all(part, "dp", 0, 0, tiled=True))
        part = swap(part, y_groups)
    plan = pl.pallas_call(
        functools.partial(plan_kernel, log_weight),
        out_shape=jax.ShapeDtypeStruct((group, rows + 16, wide), jnp.bfloat16),
        in_specs=[VMEM] * 3,
        out_specs=VMEM,
        compiler_params=PARAMS,
    )(a, u, part)
    plan = swap(plan, x_groups)

    targets, noise_potential, data_potential = pl.pallas_call(
        functools.partial(target_kernel, epsilon / LOG2E),
        grid=(YS,),
        out_shape=[
            jax.ShapeDtypeStruct((rows, features), jnp.bfloat16),
            jax.ShapeDtypeStruct((1, rows), f32),
            jax.ShapeDtypeStruct((1, CORES * rows), f32),
        ],
        in_specs=[
            SMEM,
            pl.BlockSpec((group, rows + 16, rows), lambda k: (0, 0, k)),
            pl.BlockSpec((group, rows), lambda k: (0, 0)),
            pl.BlockSpec((group * rows, features), lambda k: (k, 0)),
        ],
        out_specs=[
            pl.BlockSpec((rows, features), lambda k: (0, 0)),
            pl.BlockSpec((1, rows), lambda k: (0, 0)),
            pl.BlockSpec((1, CORES * rows), lambda k: (0, 0)),
        ],
        scratch_shapes=[
            pltpu.VMEM((rows, features), f32),
            pltpu.VMEM((rows, 1), f32),
        ],
        compiler_params=PARAMS,
    )(place, plan, u, everything)
    return targets, noise_potential.reshape(rows), data_potential.reshape(CORES * rows)


def solution(mesh):
    return jax.shard_map(
        on_device,
        mesh=mesh,
        in_specs=(P("noise", "dp"), P("noise", "dp")),
        out_specs=(P("noise", "dp"), P("noise"), P("dp")),
        check_vma=False,
    )
```

```python
import functools
import math

import jax
import jax.numpy as jnp
from jax import lax
from jax.experimental import pallas as pl
from jax.experimental.pallas import tpu as pltpu
from jax.sharding import PartitionSpec as P

D = 16384
ITERS = 4
YS, XS, CORES = 4, 4, 2
LOG2E = math.log2(math.e)
VMEM = pl.BlockSpec(memory_space=pltpu.VMEM)
SMEM = pl.BlockSpec(memory_space=pltpu.SMEM)
PARAMS = pltpu.CompilerParams(vmem_limit_bytes=48 * 1024 * 1024)


def noise_pairs(target):
    pairs = []
    for y in range(YS):
        for x in range(XS):
            for c in range(CORES):
                to_y, to_x, to_c = target(y, x, c)
                pairs.append(((y * XS + x) * CORES + c, (to_y * XS + to_x) * CORES + to_c))
    return pairs


def to_other_core(value):
    return lax.ppermute(value, "noise", noise_pairs(lambda y, x, c: (y, x, 1 - c)))


FIRST, SECOND, BOTH = (1, 3), (3, 1), 2
PLACES = ((0, 0), FIRST, SECOND, (BOTH, BOTH))


def swap_x(value, by):
    return lax.ppermute(value, "noise", noise_pairs(lambda y, x, c: (y, x ^ by[c], c)))


def swap_y(value, by):
    return lax.ppermute(value, "noise", noise_pairs(lambda y, x, c: (y ^ by[c], x, c)))


def send_z(value, target):
    size = lax.axis_size("dp")
    pairs = []
    for n in range(YS * XS * CORES):
        pairs += [(n * size + z, n * size + target(z, n % CORES) % size) for z in range(size)]
    return lax.ppermute(value, ("noise", "dp"), pairs)


def z_partner(z, c):
    return z ^ 1 if c == 0 else z + 1 if z % 2 else z - 1


def squares_row(block):
    wide = block.astype(jnp.float32)
    column = jnp.sum(wide * wide, axis=1, keepdims=True)
    n = block.shape[0]
    row_at = lax.broadcasted_iota(jnp.int32, (n, n), 0)
    column_at = lax.broadcasted_iota(jnp.int32, (n, n), 1)
    return jnp.sum(jnp.where(row_at == column_at, column, 0.0), axis=0, keepdims=True)


def partial_kernel(scale, place_ref, *refs):
    here, there, ys = refs[:2], refs[2:4], refs[4:6]
    keep, give, x_all, y_all, y_squares, chunks = refs[6:]
    rows = here[0].shape[0] // 2
    depth = chunks.shape[0]
    high = rows // depth
    z, y, x, c = place_ref[0], place_ref[1], place_ref[2], place_ref[3]
    for k, (first, second) in enumerate(PLACES):
        block = slice(k % 2 * rows, (k % 2 + 1) * rows)
        mine, other = jnp.where(c == 0, first, second), jnp.where(c == 0, second, first)
        x_all[lax.bitwise_xor(x, mine) * CORES + c] = here[k // 2][block, :]
        x_all[lax.bitwise_xor(x, other) * CORES + 1 - c] = there[k // 2][block, :]
        at = pl.multiple_of(lax.bitwise_xor(y, mine) * rows, rows)
        y_all[pl.ds(at, rows), :] = ys[k // 2][block, :]
    for k in range(YS):
        block = slice(k * rows, (k + 1) * rows)
        y_squares[:, block] = scale * squares_row(y_all[block, :])
    partner = lax.rem(z + jnp.where(lax.rem(z + c, 2) == 0, 1, depth - 1), depth)
    places = []
    for t in range(depth):
        same = lax.rem(z + t, 2) == 0
        base = jnp.where(same, z, partner)
        ahead = jnp.where(c == 0, lax.rem(t + depth - base, depth), lax.rem(base + depth - t, depth))
        places.append(ahead // 2 + jnp.where(same, 0, depth // 2))
    for k in range(XS * CORES):
        value = x_all[k]
        wide = value.astype(jnp.float32)
        x_squares = scale * jnp.sum(wide * wide, axis=1, keepdims=True)
        cross = lax.dot_general(
            value, y_all[...], (((1,), (1,)), ((), ())), preferred_element_type=jnp.float32
        )
        value = (2.0 * scale) * cross - x_squares - y_squares[...]
        for t in range(depth):
            chunks[places[t], k * high : (k + 1) * high, :] = value[t * high : (t + 1) * high]
    for k in range(depth // 2):
        keep[k] = chunks[k]
        give[k] = chunks[depth // 2 + k]


def pair_kernel(keep, got, own, ahead, back, ahead_rest, back_rest):
    own[...] = keep[0] + got[0]
    middle = keep.shape[0] // 2
    ahead[...] = keep[middle] + got[middle]
    back[...] = keep[middle + 1] + got[middle + 1]
    for k in range(1, middle):
        ahead_rest[middle - 1 - k] = keep[k] + got[k]
    for k in range(middle + 2, keep.shape[0]):
        back_rest[k - middle - 2] = keep[k] + got[k]


def joined(parts):
    peak = jnp.max(parts, axis=0)
    return peak + jnp.log(jnp.sum(jnp.exp2(parts - peak), axis=0)) * LOG2E


def on_diagonal(n):
    rows = lax.broadcasted_iota(jnp.int32, (n, n), 0)
    return rows == lax.broadcasted_iota(jnp.int32, (n, n), 1)


def column_of(u, k):
    n = u.shape[1]
    return jnp.sum(jnp.where(on_diagonal(n), u[k : k + 1], 0.0), axis=1, keepdims=True)


def row_of(parts_ref, log_weight):
    v = log_weight - joined(parts_ref[...])
    return jnp.concatenate([v[k : k + 1] for k in range(v.shape[0])], axis=1)


def copy_out(out_ref):
    whole = out_ref[0]
    for k in range(1, out_ref.shape[0]):
        out_ref[k] = whole


def row_sums(a_ref, v, out_ref, n):
    for k in range(a_ref.shape[0] // n):
        value = a_ref[k * n : (k + 1) * n, :]
        if v is not None:
            value = value + v
        peak = jnp.max(value, axis=1, keepdims=True)
        total = jnp.sum(jnp.exp2(value - peak), axis=1, keepdims=True)
        part = peak + jnp.log(total) * LOG2E
        out_ref[0, k : k + 1, :] = jnp.sum(jnp.where(on_diagonal(n), part, 0.0), axis=0, keepdims=True)
    copy_out(out_ref)


def first_rows_kernel(a_ref, out_ref):
    row_sums(a_ref, None, out_ref, out_ref.shape[2])


def rows_kernel(log_weight, a_ref, parts_ref, out_ref):
    row_sums(a_ref, row_of(parts_ref, log_weight), out_ref, out_ref.shape[2])


def all_rows_kernel(log_weight, place_ref, pairs_ref, parts_ref, a_ref, out_ref):
    blocks, n = out_ref.shape[1:]
    depth = 2 * pairs_ref.shape[0]
    high = n // depth
    z = place_ref[0]
    for k in range(depth // 2):
        source = 2 * k + lax.rem(z, 2)
        partner = lax.bitwise_xor(source, 1)
        for half, t in enumerate((source, partner)):
            for block in range(blocks):
                at = pl.multiple_of(block * n + t * high, high)
                rows = pairs_ref[k, half * blocks * high + block * high : half * blocks * high + (block + 1) * high, :]
                a_ref[pl.ds(at, high), :] = rows
    row_sums(a_ref, row_of(parts_ref, log_weight), out_ref, n)


def columns_kernel(log_weight, a_ref, parts_ref, u_ref, out_ref, shifted):
    u = log_weight - joined(parts_ref[...])
    u_ref[...] = u
    blocks, n = u.shape
    width = a_ref.shape[1]
    peak = None
    for k in range(blocks):
        value = a_ref[k * n : (k + 1) * n, :] + column_of(u, k)
        shifted[k * n : (k + 1) * n, :] = value
        block_peak = jnp.max(value.reshape(n // 8, 8, width), axis=0)
        peak = block_peak if peak is None else jnp.maximum(peak, block_peak)
    peak = jnp.max(peak, axis=0, keepdims=True)
    total = jnp.zeros((8, width), jnp.float32)
    for k in range(blocks):
        value = jnp.exp2(shifted[k * n : (k + 1) * n, :] - peak)
        total = total + jnp.sum(value.reshape(n // 8, 8, width), axis=0)
    part = peak + jnp.log(jnp.sum(total, axis=0, keepdims=True)) * LOG2E
    lanes = out_ref.shape[2]
    for k in range(out_ref.shape[1]):
        out_ref[0, k : k + 1, :] = part[:, k * lanes : (k + 1) * lanes]
    copy_out(out_ref)


def plan_kernel(log_weight, a_ref, u_ref, parts_ref, out_ref):
    v = row_of(parts_ref, log_weight)
    u = u_ref[...] - log_weight
    blocks, n = u.shape
    top = v.astype(jnp.bfloat16).astype(jnp.float32)
    rest = v - top
    middle = rest.astype(jnp.bfloat16).astype(jnp.float32)
    extra = out_ref.shape[1] - n
    row = lax.broadcasted_iota(jnp.int32, (extra, v.shape[1]), 0)
    under = jnp.where(row == 0, top, jnp.where(row == 1, middle, jnp.where(row == 2, rest - middle, 0.0)))
    under = under.astype(jnp.bfloat16)
    for k in range(blocks):
        value = a_ref[k * n : (k + 1) * n, :] + (column_of(u, k) + v)
        out_ref[k, :n, :] = jnp.exp2(value).astype(jnp.bfloat16)
        out_ref[k, n:, :] = under


def target_kernel(unit, place_ref, plan_ref, u_ref, y_ref, out_ref, f_ref, g_ref, total, mass):
    step = pl.program_id(0)
    z, x, c = place_ref[0], place_ref[2], place_ref[3]
    blocks = plan_ref.shape[0]
    n = out_ref.shape[0]

    @pl.when(step == 0)
    def _():
        total[...] = jnp.zeros_like(total)
        mass[...] = jnp.zeros_like(mass)
        f_ref[...] = unit * u_ref[pl.ds(x * CORES + c, 1), :]

    plan = jnp.concatenate([plan_ref[k, :n, :] for k in range(blocks)], axis=1)
    mass[...] += jnp.sum(plan.astype(jnp.float32), axis=1, keepdims=True)
    total[...] += jnp.dot(plan, y_ref[...], preferred_element_type=jnp.float32)

    @pl.when(step == z // XS)
    def _():
        for k in range(CORES):
            v = plan_ref[lax.rem(z, XS) * CORES + k, n:, :].astype(jnp.float32)
            g_ref[:, k * n : (k + 1) * n] = unit * (v[0:1] + v[1:2] + v[2:3])

    @pl.when(step == YS - 1)
    def _():
        out_ref[...] = (total[...] / mass[...]).astype(out_ref.dtype)


def on_device(noise_rows, data_rows):
    rows, features = noise_rows.shape
    tokens = rows * lax.axis_size("noise")
    depth = lax.axis_size("dp")
    me, z = lax.axis_index("noise"), lax.axis_index("dp")
    place = jnp.stack([z, me // (XS * CORES), me // CORES % XS, me % CORES]).astype(jnp.int32)
    epsilon = 0.7 / math.sqrt(D)
    log_weight = -math.log2(tokens)
    f32 = jnp.float32

    group = XS * CORES
    y_groups = [[y * group + k for y in range(YS)] for k in range(group)]
    x_groups = [[y * group + k for k in range(group)] for y in range(YS)]

    def swap(value, groups):
        return lax.all_to_all(value, "noise", 0, 0, axis_index_groups=groups, tiled=True)

    x_near = jnp.concatenate([noise_rows, swap_x(noise_rows, FIRST)], axis=0)
    y_near = jnp.concatenate([data_rows, swap_y(data_rows, FIRST)], axis=0)
    x_near, y_near = lax.optimization_barrier((x_near, y_near))
    x_far, y_far = swap_x(x_near, SECOND), swap_y(y_near, SECOND)
    x_far, y_far, x_there, late_rows = lax.optimization_barrier(
        (x_far, y_far, to_other_core(x_near), data_rows)
    )
    everything = lax.all_gather(late_rows, "noise", axis=0, tiled=True)
    tall, wide = group * rows, YS * rows
    half = depth // 2
    middle = half // 2
    chunk = (tall // depth, wide)
    keep, give = pl.pallas_call(
        functools.partial(partial_kernel, LOG2E / (epsilon * D)),
        out_shape=[jax.ShapeDtypeStruct((half,) + chunk, f32)] * 2,
        in_specs=[SMEM] + [VMEM] * 6,
        out_specs=[VMEM] * 2,
        scratch_shapes=[
            pltpu.VMEM((group, rows, features), jnp.bfloat16),
            pltpu.VMEM((YS * rows, features), jnp.bfloat16),
            pltpu.VMEM((1, wide), f32),
            pltpu.VMEM((depth,) + chunk, f32),
        ],
        compiler_params=PARAMS,
    )(place, x_near, x_far, x_there, to_other_core(x_far), y_near, y_far)

    got = send_z(give, z_partner)
    own, ahead, back, ahead_rest, back_rest = pl.pallas_call(
        pair_kernel,
        out_shape=[
            jax.ShapeDtypeStruct(chunk, f32),
            jax.ShapeDtypeStruct(chunk, f32),
            jax.ShapeDtypeStruct(chunk, f32),
            jax.ShapeDtypeStruct((middle - 1,) + chunk, f32),
            jax.ShapeDtypeStruct((middle - 2,) + chunk, f32),
        ],
        in_specs=[VMEM] * 2,
        out_specs=[VMEM] * 5,
        compiler_params=PARAMS,
    )(keep, got)
    for step in range(middle):
        ahead = send_z(ahead, lambda z, c: z + 2 if c == 0 else z - 2)
        if step < middle - 1:
            ahead = ahead + ahead_rest[step]
            back = send_z(back, lambda z, c: z - 2 if c == 0 else z + 2)
            if step < middle - 2:
                back = back + back_rest[step]
    own = own + ahead + back

    pair = jnp.concatenate([own, send_z(own, lambda z, c: z ^ 1)], axis=0)
    everything, sent_pair = lax.optimization_barrier((everything, pair))
    gathered = lax.all_gather(
        sent_pair, "dp", axis_index_groups=[list(range(k, depth, 2)) for k in range(2)]
    )
    z_groups = [
        [((y * group) + k) * depth + d for y in range(YS) for d in range(parity, depth, 2)]
        for k in range(group)
        for parity in range(2)
    ]
    few = 2 * tall // depth
    row_shape = jax.ShapeDtypeStruct((group, 1, few), f32)
    part = pl.pallas_call(
        first_rows_kernel,
        out_shape=row_shape,
        in_specs=[VMEM],
        out_specs=VMEM,
        compiler_params=PARAMS,
    )(pair)
    for step in range(ITERS):
        first = step == 0
        lines, n = (1, few) if first else (group, rows)
        row_shape = jax.ShapeDtypeStruct((group, lines, n), f32)
        if step == 1:
            a, part = pl.pallas_call(
                functools.partial(all_rows_kernel, log_weight),
                out_shape=[jax.ShapeDtypeStruct((tall, wide), f32), row_shape],
                in_specs=[SMEM] + [VMEM] * 2,
                out_specs=[VMEM] * 2,
                compiler_params=PARAMS,
            )(place, gathered, part)
        elif step > 1:
            part = pl.pallas_call(
                functools.partial(rows_kernel, log_weight),
                out_shape=row_shape,
                in_specs=[VMEM] * 2,
                out_specs=VMEM,
                compiler_params=PARAMS,
            )(a, part)
        part = swap(part, x_groups)
        u, part = pl.pallas_call(
            functools.partial(columns_kernel, log_weight),
            out_shape=[
                jax.ShapeDtypeStruct((lines, n), f32),
                jax.ShapeDtypeStruct((YS * half if first else YS, YS, rows), f32),
            ],
            in_specs=[VMEM] * 2,
            out_specs=[VMEM] * 2,
            scratch_shapes=[pltpu.VMEM((lines * n, wide), f32)],
            compiler_params=PARAMS,
        )(pair if first else a, part)
        if first:
            part = lax.all_to_all(
                part, ("noise", "dp"), 0, 0, axis_index_groups=z_groups, tiled=True
            )
        else:
            part = swap(part, y_groups)
    plan = pl.pallas_call(
        functools.partial(plan_kernel, log_weight),
        out_shape=jax.ShapeDtypeStruct((group, rows + 16, wide), jnp.bfloat16),
        in_specs=[VMEM] * 3,
        out_specs=VMEM,
        compiler_params=PARAMS,
    )(a, u, part)
    plan = swap(plan, x_groups)

    targets, noise_potential, data_potential = pl.pallas_call(
        functools.partial(target_kernel, epsilon / LOG2E),
        grid=(YS,),
        out_shape=[
            jax.ShapeDtypeStruct((rows, features), jnp.bfloat16),
            jax.ShapeDtypeStruct((1, rows), f32),
            jax.ShapeDtypeStruct((1, CORES * rows), f32),
        ],
        in_specs=[
            SMEM,
            pl.BlockSpec((group, rows + 16, rows), lambda k: (0, 0, k)),
            pl.BlockSpec((group, rows), lambda k: (0, 0)),
            pl.BlockSpec((group * rows, features), lambda k: (k, 0)),
        ],
        out_specs=[
            pl.BlockSpec((rows, features), lambda k: (0, 0)),
            pl.BlockSpec((1, rows), lambda k: (0, 0)),
            pl.BlockSpec((1, CORES * rows), lambda k: (0, 0)),
        ],
        scratch_shapes=[
            pltpu.VMEM((rows, features), f32),
            pltpu.VMEM((rows, 1), f32),
        ],
        compiler_params=PARAMS,
    )(place, plan, u, everything)
    return targets, noise_potential.reshape(rows), data_potential.reshape(CORES * rows)


def solution(mesh):
    return jax.shard_map(
        on_device,
        mesh=mesh,
        in_specs=(P("noise", "dp"), P("noise", "dp")),
        out_specs=(P("noise", "dp"), P("noise"), P("dp")),
        check_vma=False,
    )
```

```python
import functools
import math

import jax
import jax.numpy as jnp
from jax import lax
from jax.experimental import pallas as pl
from jax.experimental.pallas import tpu as pltpu
from jax.sharding import PartitionSpec as P

D = 16384
ITERS = 4
EARLY = 2
YS, XS, CORES = 4, 4, 2
LOG2E = math.log2(math.e)
VMEM = pl.BlockSpec(memory_space=pltpu.VMEM)
SMEM = pl.BlockSpec(memory_space=pltpu.SMEM)
PARAMS = pltpu.CompilerParams(vmem_limit_bytes=48 * 1024 * 1024)


def noise_pairs(target):
    pairs = []
    for y in range(YS):
        for x in range(XS):
            for c in range(CORES):
                to_y, to_x, to_c = target(y, x, c)
                pairs.append(((y * XS + x) * CORES + c, (to_y * XS + to_x) * CORES + to_c))
    return pairs


def to_other_core(value):
    return lax.ppermute(value, "noise", noise_pairs(lambda y, x, c: (y, x, 1 - c)))


FIRST, SECOND, BOTH = (1, 3), (3, 1), 2
PLACES = ((0, 0), FIRST, SECOND, (BOTH, BOTH))


def swap_x(value, by):
    return lax.ppermute(value, "noise", noise_pairs(lambda y, x, c: (y, x ^ by[c], c)))


def swap_y(value, by):
    return lax.ppermute(value, "noise", noise_pairs(lambda y, x, c: (y ^ by[c], x, c)))


def send_z(value, target):
    size = lax.axis_size("dp")
    pairs = []
    for n in range(YS * XS * CORES):
        pairs += [(n * size + z, n * size + target(z, n % CORES) % size) for z in range(size)]
    return lax.ppermute(value, ("noise", "dp"), pairs)


def z_partner(z, c):
    return z ^ 1 if c == 0 else z + 1 if z % 2 else z - 1


def squares_row(block):
    wide = block.astype(jnp.float32)
    column = jnp.sum(wide * wide, axis=1, keepdims=True)
    n = block.shape[0]
    row_at = lax.broadcasted_iota(jnp.int32, (n, n), 0)
    column_at = lax.broadcasted_iota(jnp.int32, (n, n), 1)
    return jnp.sum(jnp.where(row_at == column_at, column, 0.0), axis=0, keepdims=True)


def partial_kernel(scale, place_ref, *refs):
    here, there, ys = refs[:2], refs[2:4], refs[4:6]
    keep, give, x_all, y_all, y_squares, chunks = refs[6:]
    rows = here[0].shape[0] // 2
    depth = chunks.shape[0]
    high = rows // depth
    z, y, x, c = place_ref[0], place_ref[1], place_ref[2], place_ref[3]
    for k, (first, second) in enumerate(PLACES):
        block = slice(k % 2 * rows, (k % 2 + 1) * rows)
        mine, other = jnp.where(c == 0, first, second), jnp.where(c == 0, second, first)
        x_all[lax.bitwise_xor(x, mine) * CORES + c] = here[k // 2][block, :]
        x_all[lax.bitwise_xor(x, other) * CORES + 1 - c] = there[k // 2][block, :]
        at = pl.multiple_of(lax.bitwise_xor(y, mine) * rows, rows)
        y_all[pl.ds(at, rows), :] = ys[k // 2][block, :]
    for k in range(YS):
        block = slice(k * rows, (k + 1) * rows)
        y_squares[:, block] = scale * squares_row(y_all[block, :])
    up = jnp.where(c == 0, lax.rem(z, 2) == 0, lax.rem(z, 2) == 1)
    partner = lax.rem(z + jnp.where(up, 1, depth - 1), depth)
    places = []
    for t in range(depth):
        same = lax.rem(z + t, 2) == 0
        base = jnp.where(same, z, partner)
        ahead = jnp.where(c == 0, lax.rem(t + depth - base, depth), lax.rem(base + depth - t, depth))
        places.append(ahead // 2 + jnp.where(same, 0, depth // 2))
    for k in range(XS * CORES):
        value = x_all[k]
        wide = value.astype(jnp.float32)
        x_squares = scale * jnp.sum(wide * wide, axis=1, keepdims=True)
        cross = lax.dot_general(
            value, y_all[...], (((1,), (1,)), ((), ())), preferred_element_type=jnp.float32
        )
        value = (2.0 * scale) * cross - x_squares - y_squares[...]
        for t in range(depth):
            chunks[places[t], k * high : (k + 1) * high, :] = value[t * high : (t + 1) * high]
    for k in range(depth // 2):
        keep[k] = chunks[k]
        give[k] = chunks[depth // 2 + k]


def pair_kernel(keep, got, own, ahead, back, ahead_rest, back_rest):
    own[...] = keep[0] + got[0]
    middle = keep.shape[0] // 2
    ahead[...] = keep[middle] + got[middle]
    back[...] = keep[middle + 1] + got[middle + 1]
    for k in range(1, middle):
        ahead_rest[middle - 1 - k] = keep[k] + got[k]
    for k in range(middle + 2, keep.shape[0]):
        back_rest[k - middle - 2] = keep[k] + got[k]


def joined(parts):
    peak = jnp.max(parts, axis=0)
    return peak + jnp.log(jnp.sum(jnp.exp2(parts - peak), axis=0)) * LOG2E


def on_diagonal(n):
    rows = lax.broadcasted_iota(jnp.int32, (n, n), 0)
    return rows == lax.broadcasted_iota(jnp.int32, (n, n), 1)


def column_of(u, k):
    n = u.shape[1]
    return jnp.sum(jnp.where(on_diagonal(n), u[k : k + 1], 0.0), axis=1, keepdims=True)


def row_of(parts_ref, log_weight):
    v = log_weight - joined(parts_ref[...])
    return jnp.concatenate([v[k : k + 1] for k in range(v.shape[0])], axis=1)


def copy_out(out_ref):
    whole = out_ref[0]
    for k in range(1, out_ref.shape[0]):
        out_ref[k] = whole


def row_sums(a_ref, v, out_ref, n):
    for k in range(a_ref.shape[0] // n):
        value = a_ref[k * n : (k + 1) * n, :]
        if v is not None:
            value = value + v
        peak = jnp.max(value, axis=1, keepdims=True)
        total = jnp.sum(jnp.exp2(value - peak), axis=1, keepdims=True)
        part = peak + jnp.log(total) * LOG2E
        out_ref[0, k : k + 1, :] = jnp.sum(jnp.where(on_diagonal(n), part, 0.0), axis=0, keepdims=True)
    copy_out(out_ref)


def first_rows_kernel(a_ref, out_ref):
    row_sums(a_ref, None, out_ref, out_ref.shape[2])


def rows_kernel(log_weight, a_ref, parts_ref, out_ref):
    row_sums(a_ref, row_of(parts_ref, log_weight), out_ref, out_ref.shape[2])


def all_rows_kernel(log_weight, chunks_ref, parts_ref, a_ref, out_ref):
    blocks, n = out_ref.shape[1:]
    depth = chunks_ref.shape[0]
    high = n // depth
    for z in range(depth):
        for block in range(blocks):
            at = block * n + z * high
            a_ref[at : at + high, :] = chunks_ref[z, block * high : (block + 1) * high, :]
    row_sums(a_ref, row_of(parts_ref, log_weight), out_ref, n)


def columns_kernel(log_weight, a_ref, parts_ref, u_ref, out_ref, shifted):
    u = log_weight - joined(parts_ref[...])
    u_ref[...] = u
    blocks, n = u.shape
    width = a_ref.shape[1]
    peak = None
    for k in range(blocks):
        value = a_ref[k * n : (k + 1) * n, :] + column_of(u, k)
        shifted[k * n : (k + 1) * n, :] = value
        block_peak = jnp.max(value.reshape(n // 8, 8, width), axis=0)
        peak = block_peak if peak is None else jnp.maximum(peak, block_peak)
    peak = jnp.max(peak, axis=0, keepdims=True)
    total = jnp.zeros((8, width), jnp.float32)
    for k in range(blocks):
        value = jnp.exp2(shifted[k * n : (k + 1) * n, :] - peak)
        total = total + jnp.sum(value.reshape(n // 8, 8, width), axis=0)
    part = peak + jnp.log(jnp.sum(total, axis=0, keepdims=True)) * LOG2E
    lanes = out_ref.shape[2]
    for k in range(out_ref.shape[1]):
        out_ref[0, k : k + 1, :] = part[:, k * lanes : (k + 1) * lanes]
    copy_out(out_ref)


def plan_kernel(log_weight, a_ref, u_ref, parts_ref, out_ref):
    v = row_of(parts_ref, log_weight)
    u = u_ref[...] - log_weight
    blocks, n = u.shape
    top = v.astype(jnp.bfloat16).astype(jnp.float32)
    rest = v - top
    middle = rest.astype(jnp.bfloat16).astype(jnp.float32)
    extra = out_ref.shape[1] - n
    row = lax.broadcasted_iota(jnp.int32, (extra, v.shape[1]), 0)
    under = jnp.where(row == 0, top, jnp.where(row == 1, middle, jnp.where(row == 2, rest - middle, 0.0)))
    under = under.astype(jnp.bfloat16)
    for k in range(blocks):
        value = a_ref[k * n : (k + 1) * n, :] + (column_of(u, k) + v)
        out_ref[k, :n, :] = jnp.exp2(value).astype(jnp.bfloat16)
        out_ref[k, n:, :] = under


def target_kernel(unit, place_ref, plan_ref, u_ref, y_ref, out_ref, f_ref, g_ref, total, mass):
    step = pl.program_id(0)
    z, x, c = place_ref[0], place_ref[2], place_ref[3]
    blocks = plan_ref.shape[0]
    n = out_ref.shape[0]

    @pl.when(step == 0)
    def _():
        total[...] = jnp.zeros_like(total)
        mass[...] = jnp.zeros_like(mass)
        f_ref[...] = unit * u_ref[pl.ds(x * CORES + c, 1), :]

    plan = jnp.concatenate([plan_ref[k, :n, :] for k in range(blocks)], axis=1)
    mass[...] += jnp.sum(plan.astype(jnp.float32), axis=1, keepdims=True)
    total[...] += jnp.dot(plan, y_ref[...], preferred_element_type=jnp.float32)

    @pl.when(step == z // XS)
    def _():
        for k in range(CORES):
            v = plan_ref[lax.rem(z, XS) * CORES + k, n:, :].astype(jnp.float32)
            g_ref[:, k * n : (k + 1) * n] = unit * (v[0:1] + v[1:2] + v[2:3])

    @pl.when(step == YS - 1)
    def _():
        out_ref[...] = (total[...] / mass[...]).astype(out_ref.dtype)


def on_device(noise_rows, data_rows):
    rows, features = noise_rows.shape
    tokens = rows * lax.axis_size("noise")
    depth = lax.axis_size("dp")
    me, z = lax.axis_index("noise"), lax.axis_index("dp")
    place = jnp.stack([z, me // (XS * CORES), me // CORES % XS, me % CORES]).astype(jnp.int32)
    epsilon = 0.7 / math.sqrt(D)
    log_weight = -math.log2(tokens)
    f32 = jnp.float32

    group = XS * CORES
    y_groups = [[y * group + k for y in range(YS)] for k in range(group)]
    x_groups = [[y * group + k for k in range(group)] for y in range(YS)]

    def swap(value, groups):
        return lax.all_to_all(value, "noise", 0, 0, axis_index_groups=groups, tiled=True)

    x_near = jnp.concatenate([noise_rows, swap_x(noise_rows, FIRST)], axis=0)
    y_near = jnp.concatenate([data_rows, swap_y(data_rows, FIRST)], axis=0)
    x_near, y_near = lax.optimization_barrier((x_near, y_near))
    x_far, y_far = swap_x(x_near, SECOND), swap_y(y_near, SECOND)
    x_far, y_far, x_there, late_rows = lax.optimization_barrier(
        (x_far, y_far, to_other_core(x_near), data_rows)
    )
    everything = lax.all_gather(late_rows, "noise", axis=0, tiled=True)
    tall, wide = group * rows, YS * rows
    half = depth // 2
    middle = half // 2
    chunk = (tall // depth, wide)
    keep, give = pl.pallas_call(
        functools.partial(partial_kernel, LOG2E / (epsilon * D)),
        out_shape=[jax.ShapeDtypeStruct((half,) + chunk, f32)] * 2,
        in_specs=[SMEM] + [VMEM] * 6,
        out_specs=[VMEM] * 2,
        scratch_shapes=[
            pltpu.VMEM((group, rows, features), jnp.bfloat16),
            pltpu.VMEM((YS * rows, features), jnp.bfloat16),
            pltpu.VMEM((1, wide), f32),
            pltpu.VMEM((depth,) + chunk, f32),
        ],
        compiler_params=PARAMS,
    )(place, x_near, x_far, x_there, to_other_core(x_far), y_near, y_far)

    got = send_z(give, z_partner)
    own, ahead, back, ahead_rest, back_rest = pl.pallas_call(
        pair_kernel,
        out_shape=[
            jax.ShapeDtypeStruct(chunk, f32),
            jax.ShapeDtypeStruct(chunk, f32),
            jax.ShapeDtypeStruct(chunk, f32),
            jax.ShapeDtypeStruct((middle - 1,) + chunk, f32),
            jax.ShapeDtypeStruct((middle - 2,) + chunk, f32),
        ],
        in_specs=[VMEM] * 2,
        out_specs=[VMEM] * 5,
        compiler_params=PARAMS,
    )(keep, got)
    for step in range(middle):
        ahead = send_z(ahead, lambda z, c: z + 2 if c == 0 else z - 2)
        if step < middle - 1:
            ahead = ahead + ahead_rest[step]
            back = send_z(back, lambda z, c: z - 2 if c == 0 else z + 2)
            if step < middle - 2:
                back = back + back_rest[step]
    own = own + ahead + back

    everything, own = lax.optimization_barrier((everything, own))
    gathered = lax.all_gather(own, "dp")
    z_groups = [
        [((y * group) + k) * depth + d for y in range(YS) for d in range(depth)] for k in range(group)
    ]
    few = tall // depth
    for step in range(ITERS):
        early = step < EARLY
        lines, n = (1, few) if early else (group, rows)
        row_shape = jax.ShapeDtypeStruct((group, lines, n), f32)
        if step == 0:
            part = pl.pallas_call(
                first_rows_kernel,
                out_shape=row_shape,
                in_specs=[VMEM],
                out_specs=VMEM,
                compiler_params=PARAMS,
            )(own)
        elif step == EARLY:
            a, part = pl.pallas_call(
                functools.partial(all_rows_kernel, log_weight),
                out_shape=[jax.ShapeDtypeStruct((tall, wide), f32), row_shape],
                in_specs=[VMEM] * 2,
                out_specs=[VMEM] * 2,
                compiler_params=PARAMS,
            )(gathered, part)
        else:
            part = pl.pallas_call(
                functools.partial(rows_kernel, log_weight),
                out_shape=row_shape,
                in_specs=[VMEM] * 2,
                out_specs=VMEM,
                compiler_params=PARAMS,
            )(own if early else a, part)
        part = swap(part, x_groups)
        u, part = pl.pallas_call(
            functools.partial(columns_kernel, log_weight),
            out_shape=[
                jax.ShapeDtypeStruct((lines, n), f32),
                jax.ShapeDtypeStruct((YS * depth if early else YS, YS, rows), f32),
            ],
            in_specs=[VMEM] * 2,
            out_specs=[VMEM] * 2,
            scratch_shapes=[pltpu.VMEM((lines * n, wide), f32)],
            compiler_params=PARAMS,
        )(own if early else a, part)
        if early:
            part = lax.all_to_all(
                part, ("noise", "dp"), 0, 0, axis_index_groups=z_groups, tiled=True
            )
        else:
            part = swap(part, y_groups)
    plan = pl.pallas_call(
        functools.partial(plan_kernel, log_weight),
        out_shape=jax.ShapeDtypeStruct((group, rows + 16, wide), jnp.bfloat16),
        in_specs=[VMEM] * 3,
        out_specs=VMEM,
        compiler_params=PARAMS,
    )(a, u, part)
    plan = swap(plan, x_groups)

    targets, noise_potential, data_potential = pl.pallas_call(
        functools.partial(target_kernel, epsilon / LOG2E),
        grid=(YS,),
        out_shape=[
            jax.ShapeDtypeStruct((rows, features), jnp.bfloat16),
            jax.ShapeDtypeStruct((1, rows), f32),
            jax.ShapeDtypeStruct((1, CORES * rows), f32),
        ],
        in_specs=[
            SMEM,
            pl.BlockSpec((group, rows + 16, rows), lambda k: (0, 0, k)),
            pl.BlockSpec((group, rows), lambda k: (0, 0)),
            pl.BlockSpec((group * rows, features), lambda k: (k, 0)),
        ],
        out_specs=[
            pl.BlockSpec((rows, features), lambda k: (0, 0)),
            pl.BlockSpec((1, rows), lambda k: (0, 0)),
            pl.BlockSpec((1, CORES * rows), lambda k: (0, 0)),
        ],
        scratch_shapes=[
            pltpu.VMEM((rows, features), f32),
            pltpu.VMEM((rows, 1), f32),
        ],
        compiler_params=PARAMS,
    )(place, plan, u, everything)
    return targets, noise_potential.reshape(rows), data_potential.reshape(CORES * rows)


def solution(mesh):
    return jax.shard_map(
        on_device,
        mesh=mesh,
        in_specs=(P("noise", "dp"), P("noise", "dp")),
        out_specs=(P("noise", "dp"), P("noise"), P("dp")),
        check_vma=False,
    )
```

```python
import functools
import math

import jax
import jax.numpy as jnp
from jax import lax
from jax.experimental import pallas as pl
from jax.experimental.pallas import tpu as pltpu
from jax.sharding import PartitionSpec as P

D = 16384
ITERS = 4
EARLY = 2
YS, XS, CORES = 4, 4, 2
LOG2E = math.log2(math.e)
VMEM = pl.BlockSpec(memory_space=pltpu.VMEM)
SMEM = pl.BlockSpec(memory_space=pltpu.SMEM)
PARAMS = pltpu.CompilerParams(vmem_limit_bytes=48 * 1024 * 1024)


def noise_pairs(target):
    pairs = []
    for y in range(YS):
        for x in range(XS):
            for c in range(CORES):
                to_y, to_x, to_c = target(y, x, c)
                pairs.append(((y * XS + x) * CORES + c, (to_y * XS + to_x) * CORES + to_c))
    return pairs


def to_other_core(value):
    return lax.ppermute(value, "noise", noise_pairs(lambda y, x, c: (y, x, 1 - c)))


FIRST, SECOND, BOTH = (1, 3), (3, 1), 2
PLACES = ((0, 0), FIRST, SECOND, (BOTH, BOTH))


def swap_x(value, by):
    return lax.ppermute(value, "noise", noise_pairs(lambda y, x, c: (y, x ^ by[c], c)))


def swap_y(value, by):
    return lax.ppermute(value, "noise", noise_pairs(lambda y, x, c: (y ^ by[c], x, c)))


def send_z(value, target):
    size = lax.axis_size("dp")
    pairs = []
    for n in range(YS * XS * CORES):
        pairs += [(n * size + z, n * size + target(z, n % CORES) % size) for z in range(size)]
    return lax.ppermute(value, ("noise", "dp"), pairs)


def z_partner(z, c):
    return z ^ 1 if c == 0 else z + 1 if z % 2 else z - 1


def squares_row(block):
    wide = block.astype(jnp.float32)
    column = jnp.sum(wide * wide, axis=1, keepdims=True)
    n = block.shape[0]
    row_at = lax.broadcasted_iota(jnp.int32, (n, n), 0)
    column_at = lax.broadcasted_iota(jnp.int32, (n, n), 1)
    return jnp.sum(jnp.where(row_at == column_at, column, 0.0), axis=0, keepdims=True)


def partial_kernel(scale, place_ref, *refs):
    here, there, ys = refs[:2], refs[2:4], refs[4:6]
    keep, give, x_all, y_all, y_squares, chunks = refs[6:]
    rows = here[0].shape[0] // 2
    depth = chunks.shape[0]
    high = rows // depth
    z, y, x, c = place_ref[0], place_ref[1], place_ref[2], place_ref[3]
    for k, (first, second) in enumerate(PLACES):
        block = slice(k % 2 * rows, (k % 2 + 1) * rows)
        mine, other = jnp.where(c == 0, first, second), jnp.where(c == 0, second, first)
        at = pl.multiple_of((lax.bitwise_xor(x, mine) * CORES + c) * rows, rows)
        x_all[pl.ds(at, rows), :] = here[k // 2][block, :]
        at = pl.multiple_of((lax.bitwise_xor(x, other) * CORES + 1 - c) * rows, rows)
        x_all[pl.ds(at, rows), :] = there[k // 2][block, :]
        at = pl.multiple_of(lax.bitwise_xor(y, mine) * rows, rows)
        y_all[pl.ds(at, rows), :] = ys[k // 2][block, :]
    for k in range(YS):
        block = slice(k * rows, (k + 1) * rows)
        y_squares[:, block] = scale * squares_row(y_all[block, :])
    up = jnp.where(c == 0, lax.rem(z, 2) == 0, lax.rem(z, 2) == 1)
    partner = lax.rem(z + jnp.where(up, 1, depth - 1), depth)
    places = []
    for t in range(depth):
        same = lax.rem(z + t, 2) == 0
        base = jnp.where(same, z, partner)
        ahead = jnp.where(c == 0, lax.rem(t + depth - base, depth), lax.rem(base + depth - t, depth))
        places.append(ahead // 2 + jnp.where(same, 0, depth // 2))
    tall = 4 * rows
    for k in range(XS * CORES // 4):
        value = x_all[k * tall : (k + 1) * tall, :]
        wide = value.astype(jnp.float32)
        x_squares = scale * jnp.sum(wide * wide, axis=1, keepdims=True)
        cross = lax.dot_general(
            value, y_all[...], (((1,), (1,)), ((), ())), preferred_element_type=jnp.float32
        )
        value = (2.0 * scale) * cross - x_squares - y_squares[...]
        for i in range(4 * depth):
            block = k * 4 + i // depth
            chunks[places[i % depth], block * high : (block + 1) * high, :] = value[i * high : (i + 1) * high]
    for k in range(depth // 2):
        keep[k] = chunks[k]
        give[k] = chunks[depth // 2 + k]


def pair_kernel(keep, got, own, ahead, back, ahead_rest, back_rest):
    own[...] = keep[0] + got[0]
    middle = keep.shape[0] // 2
    ahead[...] = keep[middle] + got[middle]
    back[...] = keep[middle + 1] + got[middle + 1]
    for k in range(1, middle):
        ahead_rest[middle - 1 - k] = keep[k] + got[k]
    for k in range(middle + 2, keep.shape[0]):
        back_rest[k - middle - 2] = keep[k] + got[k]


def joined(parts):
    peak = jnp.max(parts, axis=0)
    return peak + jnp.log(jnp.sum(jnp.exp2(parts - peak), axis=0)) * LOG2E


def on_diagonal(n):
    rows = lax.broadcasted_iota(jnp.int32, (n, n), 0)
    return rows == lax.broadcasted_iota(jnp.int32, (n, n), 1)


def column_of(u, k):
    n = u.shape[1]
    return jnp.sum(jnp.where(on_diagonal(n), u[k : k + 1], 0.0), axis=1, keepdims=True)


def row_of(parts_ref, log_weight):
    v = log_weight - joined(parts_ref[...])
    return jnp.concatenate([v[k : k + 1] for k in range(v.shape[0])], axis=1)


def copy_out(out_ref):
    whole = out_ref[0]
    for k in range(1, out_ref.shape[0]):
        out_ref[k] = whole


def row_sums(a_ref, v, out_ref, n):
    for k in range(a_ref.shape[0] // n):
        value = a_ref[k * n : (k + 1) * n, :]
        if v is not None:
            value = value + v
        peak = jnp.max(value, axis=1, keepdims=True)
        total = jnp.sum(jnp.exp2(value - peak), axis=1, keepdims=True)
        part = peak + jnp.log(total) * LOG2E
        out_ref[0, k : k + 1, :] = jnp.sum(jnp.where(on_diagonal(n), part, 0.0), axis=0, keepdims=True)
    copy_out(out_ref)


def first_rows_kernel(a_ref, out_ref):
    row_sums(a_ref, None, out_ref, out_ref.shape[2])


def rows_kernel(log_weight, a_ref, parts_ref, out_ref):
    row_sums(a_ref, row_of(parts_ref, log_weight), out_ref, out_ref.shape[2])


def columns_kernel(log_weight, a_ref, parts_ref, out_ref, shifted):
    u = log_weight - joined(parts_ref[...])
    blocks, n = u.shape
    width = a_ref.shape[1]
    peak = None
    for k in range(blocks):
        value = a_ref[k * n : (k + 1) * n, :] + column_of(u, k)
        shifted[k * n : (k + 1) * n, :] = value
        block_peak = jnp.max(value.reshape(n // 8, 8, width), axis=0)
        peak = block_peak if peak is None else jnp.maximum(peak, block_peak)
    peak = jnp.max(peak, axis=0, keepdims=True)
    total = jnp.zeros((8, width), jnp.float32)
    for k in range(blocks):
        value = jnp.exp2(shifted[k * n : (k + 1) * n, :] - peak)
        total = total + jnp.sum(value.reshape(n // 8, 8, width), axis=0)
    part = peak + jnp.log(jnp.sum(total, axis=0, keepdims=True)) * LOG2E
    lanes = out_ref.shape[2]
    for k in range(out_ref.shape[1]):
        out_ref[0, k : k + 1, :] = part[:, k * lanes : (k + 1) * lanes]
    copy_out(out_ref)


def join_kernel(parts_ref, out_ref):
    out_ref[0] = joined(parts_ref[...])
    copy_out(out_ref)


def half_steps(log_weight, a_ref, v, u_ref, l_ref):
    rows, columns = a_ref.shape
    lanes = u_ref.shape[1]
    copies, high, width = l_ref.shape

    @pl.loop(0, rows // 8, step=2)
    def _(base):
        for i in range(2):
            at = pl.ds(pl.multiple_of((base + i) * 8, 8), 8)
            value = a_ref[at, :] + v
            peak = jnp.max(value, axis=1, keepdims=True)
            total = jnp.sum(jnp.exp2(value - peak), axis=1, keepdims=True)
            u = log_weight - (peak + jnp.log(total) * LOG2E)
            u_ref[at, :] = jnp.broadcast_to(u, (8, lanes))

    for k in range(high):
        for i in range(width // lanes):
            at = pl.ds(k * width + i * lanes, lanes)
            value = a_ref[:, at] + u_ref[...]
            peak = jnp.max(value, axis=0, keepdims=True)
            total = jnp.sum(jnp.exp2(value - peak), axis=0, keepdims=True)
            l_ref[0, k : k + 1, i * lanes : (i + 1) * lanes] = peak + jnp.log(total) * LOG2E
    whole = l_ref[0]
    for k in range(1, copies):
        l_ref[k] = whole


def whole_rows_kernel(log_weight, pieces_ref, parts_ref, a_ref, u_ref, l_ref):
    depth, blocks, high, width = pieces_ref.shape
    n = width // YS
    v = log_weight - parts_ref[...]
    for z in range(depth):
        for y in range(YS):
            for k in range(blocks):
                at = (y * blocks + k) * n
                a_ref[z * high : (z + 1) * high, at : at + n] = pieces_ref[z, k, :, y * n : (y + 1) * n]
    v = jnp.concatenate([v[k, y : y + 1] for y in range(YS) for k in range(blocks)], axis=1)
    half_steps(log_weight, a_ref, v, u_ref, l_ref)


def next_kernel(log_weight, a_ref, parts_ref, u_ref, l_ref):
    v = log_weight - joined(parts_ref[...])
    v = jnp.concatenate([v[k : k + 1] for k in range(v.shape[0])], axis=1)
    half_steps(log_weight, a_ref, v, u_ref, l_ref)


def target_kernel(log_weight, unit, steps, a_ref, u_ref, parts_ref, y_ref, out_ref, f_ref, g_ref, total, mass):
    step = pl.program_id(0)
    lines = g_ref.shape[0] // steps

    @pl.when(step == 0)
    def _():
        total[...] = jnp.zeros_like(total)
        mass[...] = jnp.zeros_like(mass)
        u = u_ref[...]
        f_ref[...] = unit * jnp.sum(jnp.where(on_diagonal(u.shape[0]), u, 0.0), axis=0, keepdims=True)
        g_ref[...] = log_weight - joined(parts_ref[...])

    v = jnp.concatenate([g_ref[pl.ds(step * lines + k, 1), :] for k in range(lines)], axis=1)
    u = u_ref[:, :1]
    plan = jnp.exp2((u - log_weight + v) + a_ref[...]).astype(jnp.bfloat16)
    mass[...] += jnp.sum(plan.astype(jnp.float32), axis=1, keepdims=True)
    total[...] += jnp.dot(plan, y_ref[...], preferred_element_type=jnp.float32)

    @pl.when(step == steps - 1)
    def _():
        out_ref[...] = (total[...] / mass[...]).astype(out_ref.dtype)
        g_ref[...] = unit * g_ref[...]


def on_device(noise_rows, data_rows):
    rows, features = noise_rows.shape
    tokens = rows * lax.axis_size("noise")
    depth = lax.axis_size("dp")
    me, z = lax.axis_index("noise"), lax.axis_index("dp")
    place = jnp.stack([z, me // (XS * CORES), me // CORES % XS, me % CORES]).astype(jnp.int32)
    epsilon = 0.7 / math.sqrt(D)
    log_weight = -math.log2(tokens)
    f32 = jnp.float32

    group = XS * CORES
    y_groups = [[y * group + k for y in range(YS)] for k in range(group)]
    x_groups = [[y * group + k for k in range(group)] for y in range(YS)]

    def swap(value, groups):
        return lax.all_to_all(value, "noise", 0, 0, axis_index_groups=groups, tiled=True)

    x_near = jnp.concatenate([noise_rows, swap_x(noise_rows, FIRST)], axis=0)
    y_near = jnp.concatenate([data_rows, swap_y(data_rows, FIRST)], axis=0)
    x_near, y_near = lax.optimization_barrier((x_near, y_near))
    x_far, y_far = swap_x(x_near, SECOND), swap_y(y_near, SECOND)
    x_far, y_far, x_there, late_rows = lax.optimization_barrier(
        (x_far, y_far, to_other_core(x_near), data_rows)
    )
    everything = lax.all_gather(late_rows, "noise", axis=0, tiled=True)
    tall, wide = group * rows, YS * rows
    half = depth // 2
    middle = half // 2
    chunk = (tall // depth, wide)
    keep, give = pl.pallas_call(
        functools.partial(partial_kernel, LOG2E / (epsilon * D)),
        out_shape=[jax.ShapeDtypeStruct((half,) + chunk, f32)] * 2,
        in_specs=[SMEM] + [VMEM] * 6,
        out_specs=[VMEM] * 2,
        scratch_shapes=[
            pltpu.VMEM((group * rows, features), jnp.bfloat16),
            pltpu.VMEM((YS * rows, features), jnp.bfloat16),
            pltpu.VMEM((1, wide), f32),
            pltpu.VMEM((depth,) + chunk, f32),
        ],
        compiler_params=PARAMS,
    )(place, x_near, x_far, x_there, to_other_core(x_far), y_near, y_far)

    got = send_z(give, z_partner)
    own, ahead, back, ahead_rest, back_rest = pl.pallas_call(
        pair_kernel,
        out_shape=[
            jax.ShapeDtypeStruct(chunk, f32),
            jax.ShapeDtypeStruct(chunk, f32),
            jax.ShapeDtypeStruct(chunk, f32),
            jax.ShapeDtypeStruct((middle - 1,) + chunk, f32),
            jax.ShapeDtypeStruct((middle - 2,) + chunk, f32),
        ],
        in_specs=[VMEM] * 2,
        out_specs=[VMEM] * 5,
        compiler_params=PARAMS,
    )(keep, got)
    for step in range(middle):
        ahead = send_z(ahead, lambda z, c: z + 2 if c == 0 else z - 2)
        if step < middle - 1:
            ahead = ahead + ahead_rest[step]
            back = send_z(back, lambda z, c: z - 2 if c == 0 else z + 2)
            if step < middle - 2:
                back = back + back_rest[step]
    own = own + ahead + back

    pieces = swap(own.reshape(group, rows // depth, wide), x_groups)
    everything, pieces = lax.optimization_barrier((everything, pieces))
    gathered = lax.all_gather(pieces, "dp")
    z_groups = [
        [((y * group) + k) * depth + d for y in range(YS) for d in range(depth)] for k in range(group)
    ]
    few = tall // depth
    row_shape = jax.ShapeDtypeStruct((group, 1, few), f32)
    for step in range(EARLY):
        if step == 0:
            part = pl.pallas_call(
                first_rows_kernel,
                out_shape=row_shape,
                in_specs=[VMEM],
                out_specs=VMEM,
                compiler_params=PARAMS,
            )(own)
        else:
            part = pl.pallas_call(
                functools.partial(rows_kernel, log_weight),
                out_shape=row_shape,
                in_specs=[VMEM] * 2,
                out_specs=VMEM,
                compiler_params=PARAMS,
            )(own, part)
        part = swap(part, x_groups)
        part = pl.pallas_call(
            functools.partial(columns_kernel, log_weight),
            out_shape=jax.ShapeDtypeStruct((YS * depth, YS, rows), f32),
            in_specs=[VMEM] * 2,
            out_specs=VMEM,
            scratch_shapes=[pltpu.VMEM((few, wide), f32)],
            compiler_params=PARAMS,
        )(own, part)
        part = lax.all_to_all(
            part, ("noise", "dp"), 0, 0, axis_index_groups=z_groups, tiled=True
        )
    part = pl.pallas_call(
        join_kernel,
        out_shape=jax.ShapeDtypeStruct((group, YS, rows), f32),
        in_specs=[VMEM],
        out_specs=VMEM,
        compiler_params=PARAMS,
    )(part)
    part = swap(part, x_groups)

    copies = lax.axis_size("noise")
    high = 8
    block = tokens // high
    u_shape = jax.ShapeDtypeStruct((rows, rows), f32)
    l_shape = jax.ShapeDtypeStruct((copies, high, block), f32)
    for step in range(EARLY, ITERS):
        if step == EARLY:
            a, u, part = pl.pallas_call(
                functools.partial(whole_rows_kernel, log_weight),
                out_shape=[jax.ShapeDtypeStruct((rows, tokens), f32), u_shape, l_shape],
                in_specs=[VMEM] * 2,
                out_specs=[VMEM] * 3,
                compiler_params=PARAMS,
            )(gathered, part)
        else:
            u, part = pl.pallas_call(
                functools.partial(next_kernel, log_weight),
                out_shape=[u_shape, l_shape],
                in_specs=[VMEM] * 2,
                out_specs=[VMEM] * 2,
                compiler_params=PARAMS,
            )(a, part)
        part = lax.all_to_all(part, "noise", 0, 0, tiled=True)

    steps = 4
    targets, noise_potential, data_potential = pl.pallas_call(
        functools.partial(target_kernel, log_weight, epsilon / LOG2E, steps),
        grid=(steps,),
        out_shape=[
            jax.ShapeDtypeStruct((rows, features), jnp.bfloat16),
            jax.ShapeDtypeStruct((1, rows), f32),
            jax.ShapeDtypeStruct((high, block), f32),
        ],
        in_specs=[
            pl.BlockSpec((rows, tokens // steps), lambda k: (0, k)),
            pl.BlockSpec((rows, rows), lambda k: (0, 0)),
            pl.BlockSpec((copies, high, block), lambda k: (0, 0, 0)),
            pl.BlockSpec((tokens // steps, features), lambda k: (k, 0)),
        ],
        out_specs=[
            pl.BlockSpec((rows, features), lambda k: (0, 0)),
            pl.BlockSpec((1, rows), lambda k: (0, 0)),
            pl.BlockSpec((high, block), lambda k: (0, 0)),
        ],
        scratch_shapes=[
            pltpu.VMEM((rows, features), f32),
            pltpu.VMEM((rows, 1), f32),
        ],
        compiler_params=PARAMS,
    )(a, u, part, everything)
    share = tokens // depth
    data_potential = lax.dynamic_slice(
        data_potential, (z * share // block, z * share % block), (1, share)
    )
    return targets, noise_potential.reshape(rows), data_potential.reshape(share)


def solution(mesh):
    return jax.shard_map(
        on_device,
        mesh=mesh,
        in_specs=(P("noise", "dp"), P("noise", "dp")),
        out_specs=(P("noise", "dp"), P("noise"), P("dp")),
        check_vma=False,
    )
```

```python
import functools
import math

import jax
import jax.numpy as jnp
from jax import lax
from jax.experimental import pallas as pl
from jax.experimental.pallas import tpu as pltpu
from jax.sharding import PartitionSpec as P

D = 16384
ITERS = 4
EARLY = 2
YS, XS, CORES = 4, 4, 2
LOG2E = math.log2(math.e)
VMEM = pl.BlockSpec(memory_space=pltpu.VMEM)
SMEM = pl.BlockSpec(memory_space=pltpu.SMEM)
PARAMS = pltpu.CompilerParams(vmem_limit_bytes=48 * 1024 * 1024)


def noise_pairs(target):
    pairs = []
    for y in range(YS):
        for x in range(XS):
            for c in range(CORES):
                to_y, to_x, to_c = target(y, x, c)
                pairs.append(((y * XS + x) * CORES + c, (to_y * XS + to_x) * CORES + to_c))
    return pairs


def to_other_core(value):
    return lax.ppermute(value, "noise", noise_pairs(lambda y, x, c: (y, x, 1 - c)))


FIRST, SECOND, BOTH = (1, 3), (3, 1), 2
PLACES = ((0, 0), FIRST, SECOND, (BOTH, BOTH))


def swap_x(value, by):
    return lax.ppermute(value, "noise", noise_pairs(lambda y, x, c: (y, x ^ by[c], c)))


def swap_y(value, by):
    return lax.ppermute(value, "noise", noise_pairs(lambda y, x, c: (y ^ by[c], x, c)))


def send_z(value, target):
    size = lax.axis_size("dp")
    pairs = []
    for n in range(YS * XS * CORES):
        pairs += [(n * size + z, n * size + target(z, n % CORES) % size) for z in range(size)]
    return lax.ppermute(value, ("noise", "dp"), pairs)


def z_partner(z, c):
    return z ^ 1 if c == 0 else z + 1 if z % 2 else z - 1


def squares_row(block):
    wide = block.astype(jnp.float32)
    column = jnp.sum(wide * wide, axis=1, keepdims=True)
    n = block.shape[0]
    row_at = lax.broadcasted_iota(jnp.int32, (n, n), 0)
    column_at = lax.broadcasted_iota(jnp.int32, (n, n), 1)
    return jnp.sum(jnp.where(row_at == column_at, column, 0.0), axis=0, keepdims=True)


def partial_kernel(scale, place_ref, *refs):
    here, there, ys = refs[:2], refs[2:4], refs[4:6]
    keep, give, y_all, x_all, y_squares, chunks = refs[6:]
    rows = here[0].shape[0] // 2
    depth = chunks.shape[0]
    high = rows // depth
    z, y, x, c = place_ref[0], place_ref[1], place_ref[2], place_ref[3]
    for k, (first, second) in enumerate(PLACES):
        block = slice(k % 2 * rows, (k % 2 + 1) * rows)
        mine, other = jnp.where(c == 0, first, second), jnp.where(c == 0, second, first)
        at = pl.multiple_of((lax.bitwise_xor(x, mine) * CORES + c) * rows, rows)
        x_all[pl.ds(at, rows), :] = here[k // 2][block, :]
        at = pl.multiple_of((lax.bitwise_xor(x, other) * CORES + 1 - c) * rows, rows)
        x_all[pl.ds(at, rows), :] = there[k // 2][block, :]
        at = pl.multiple_of(lax.bitwise_xor(y, mine) * rows, rows)
        y_all[pl.ds(at, rows), :] = ys[k // 2][block, :]
    for k in range(YS):
        block = slice(k * rows, (k + 1) * rows)
        y_squares[:, block] = scale * squares_row(y_all[block, :])
    up = jnp.where(c == 0, lax.rem(z, 2) == 0, lax.rem(z, 2) == 1)
    partner = lax.rem(z + jnp.where(up, 1, depth - 1), depth)
    places = []
    for t in range(depth):
        same = lax.rem(z + t, 2) == 0
        base = jnp.where(same, z, partner)
        ahead = jnp.where(c == 0, lax.rem(t + depth - base, depth), lax.rem(base + depth - t, depth))
        places.append(ahead // 2 + jnp.where(same, 0, depth // 2))
    tall = 4 * rows
    for k in range(XS * CORES // 4):
        value = x_all[k * tall : (k + 1) * tall, :]
        wide = value.astype(jnp.float32)
        x_squares = scale * jnp.sum(wide * wide, axis=1, keepdims=True)
        cross = lax.dot_general(
            value, y_all[...], (((1,), (1,)), ((), ())), preferred_element_type=jnp.float32
        )
        value = (2.0 * scale) * cross - x_squares - y_squares[...]
        for i in range(4 * depth):
            block = k * 4 + i // depth
            chunks[places[i % depth], block * high : (block + 1) * high, :] = value[i * high : (i + 1) * high]
    for k in range(depth // 2):
        keep[k] = chunks[k]
        give[k] = chunks[depth // 2 + k]


def pair_kernel(keep, got, *outs):
    for k, out in enumerate(outs):
        out[...] = keep[k] + got[k]


def joined(parts):
    peak = jnp.max(parts, axis=0)
    return peak + jnp.log(jnp.sum(jnp.exp2(parts - peak), axis=0)) * LOG2E


def on_diagonal(n):
    rows = lax.broadcasted_iota(jnp.int32, (n, n), 0)
    return rows == lax.broadcasted_iota(jnp.int32, (n, n), 1)


def column_of(u, k):
    n = u.shape[1]
    return jnp.sum(jnp.where(on_diagonal(n), u[k : k + 1], 0.0), axis=1, keepdims=True)


def row_of(parts_ref, log_weight):
    v = log_weight - joined(parts_ref[...])
    return jnp.concatenate([v[k : k + 1] for k in range(v.shape[0])], axis=1)


def copy_out(out_ref):
    whole = out_ref[0]
    for k in range(1, out_ref.shape[0]):
        out_ref[k] = whole


def row_sums(a_ref, v, out_ref, n):
    for k in range(a_ref.shape[0] // n):
        value = a_ref[k * n : (k + 1) * n, :]
        if v is not None:
            value = value + v
        peak = jnp.max(value, axis=1, keepdims=True)
        total = jnp.sum(jnp.exp2(value - peak), axis=1, keepdims=True)
        part = peak + jnp.log(total) * LOG2E
        out_ref[0, k : k + 1, :] = jnp.sum(jnp.where(on_diagonal(n), part, 0.0), axis=0, keepdims=True)
    copy_out(out_ref)


def first_rows_kernel(a_ref, out_ref):
    row_sums(a_ref, None, out_ref, out_ref.shape[2])


def rows_kernel(log_weight, a_ref, parts_ref, out_ref):
    row_sums(a_ref, row_of(parts_ref, log_weight), out_ref, out_ref.shape[2])


def columns_kernel(log_weight, a_ref, parts_ref, out_ref, shifted):
    u = log_weight - joined(parts_ref[...])
    blocks, n = u.shape
    width = a_ref.shape[1]
    peak = None
    for k in range(blocks):
        value = a_ref[k * n : (k + 1) * n, :] + column_of(u, k)
        shifted[k * n : (k + 1) * n, :] = value
        block_peak = jnp.max(value.reshape(n // 8, 8, width), axis=0)
        peak = block_peak if peak is None else jnp.maximum(peak, block_peak)
    peak = jnp.max(peak, axis=0, keepdims=True)
    total = jnp.zeros((8, width), jnp.float32)
    for k in range(blocks):
        value = jnp.exp2(shifted[k * n : (k + 1) * n, :] - peak)
        total = total + jnp.sum(value.reshape(n // 8, 8, width), axis=0)
    part = peak + jnp.log(jnp.sum(total, axis=0, keepdims=True)) * LOG2E
    lanes = out_ref.shape[2]
    for k in range(out_ref.shape[1]):
        out_ref[0, k : k + 1, :] = part[:, k * lanes : (k + 1) * lanes]
    copy_out(out_ref)


def join_kernel(parts_ref, out_ref):
    out_ref[0] = joined(parts_ref[...])
    copy_out(out_ref)


def half_steps(log_weight, a_ref, v, u_ref, l_ref):
    rows, columns = a_ref.shape
    lanes = u_ref.shape[1]
    copies, high, width = l_ref.shape

    @pl.loop(0, rows // 8, step=2)
    def _(base):
        for i in range(2):
            at = pl.ds(pl.multiple_of((base + i) * 8, 8), 8)
            value = a_ref[at, :] + v
            peak = jnp.max(value, axis=1, keepdims=True)
            total = jnp.sum(jnp.exp2(value - peak), axis=1, keepdims=True)
            u = log_weight - (peak + jnp.log(total) * LOG2E)
            u_ref[at, :] = jnp.broadcast_to(u, (8, lanes))

    for k in range(high):
        for i in range(width // lanes):
            at = pl.ds(k * width + i * lanes, lanes)
            value = a_ref[:, at] + u_ref[...]
            peak = jnp.max(value, axis=0, keepdims=True)
            total = jnp.sum(jnp.exp2(value - peak), axis=0, keepdims=True)
            l_ref[0, k : k + 1, i * lanes : (i + 1) * lanes] = peak + jnp.log(total) * LOG2E
    whole = l_ref[0]
    for k in range(1, copies):
        l_ref[k] = whole


def whole_rows_kernel(log_weight, pieces_ref, parts_ref, a_ref, u_ref, l_ref):
    depth, blocks, high, width = pieces_ref.shape
    n = width // YS
    v = log_weight - parts_ref[...]
    for z in range(depth):
        for y in range(YS):
            for k in range(blocks):
                at = (y * blocks + k) * n
                a_ref[z * high : (z + 1) * high, at : at + n] = pieces_ref[z, k, :, y * n : (y + 1) * n]
    v = jnp.concatenate([v[k, y : y + 1] for y in range(YS) for k in range(blocks)], axis=1)
    half_steps(log_weight, a_ref, v, u_ref, l_ref)


def next_kernel(log_weight, a_ref, parts_ref, u_ref, l_ref):
    v = log_weight - joined(parts_ref[...])
    v = jnp.concatenate([v[k : k + 1] for k in range(v.shape[0])], axis=1)
    half_steps(log_weight, a_ref, v, u_ref, l_ref)


def target_kernel(
    log_weight, unit, steps, place_ref, a_ref, u_ref, parts_ref, y_ref, out_ref, f_ref, g_ref, total, mass, v_ref
):
    step = pl.program_id(0)
    lines = v_ref.shape[0] // steps

    @pl.when(step == 0)
    def _():
        total[...] = jnp.zeros_like(total)
        mass[...] = jnp.zeros_like(mass)
        u = u_ref[...]
        f_ref[...] = unit * jnp.sum(jnp.where(on_diagonal(u.shape[0]), u, 0.0), axis=0, keepdims=True)
        v_ref[...] = log_weight - joined(parts_ref[...])
        share = g_ref.shape[1]
        z = place_ref[0]
        line = v_ref[pl.ds(z // 2, 1), :]
        g_ref[...] = unit * jnp.where(lax.rem(z, 2) == 0, line[:, :share], line[:, share:])

    v = jnp.concatenate([v_ref[pl.ds(step * lines + k, 1), :] for k in range(lines)], axis=1)
    u = u_ref[:, :1]
    plan = jnp.exp2((u - log_weight + v) + a_ref[...]).astype(jnp.bfloat16)
    mass[...] += jnp.sum(plan.astype(jnp.float32), axis=1, keepdims=True)
    y = y_ref[...].reshape(plan.shape[1], y_ref.shape[2])
    total[...] += jnp.dot(plan, y, preferred_element_type=jnp.float32)

    @pl.when(step == steps - 1)
    def _():
        out_ref[...] = (total[...] / mass[...]).astype(out_ref.dtype)


def on_device(noise_rows, data_rows):
    rows, features = noise_rows.shape
    tokens = rows * lax.axis_size("noise")
    depth = lax.axis_size("dp")
    me, z = lax.axis_index("noise"), lax.axis_index("dp")
    place = jnp.stack([z, me // (XS * CORES), me // CORES % XS, me % CORES]).astype(jnp.int32)
    epsilon = 0.7 / math.sqrt(D)
    log_weight = -math.log2(tokens)
    f32 = jnp.float32

    group = XS * CORES
    y_groups = [[y * group + k for y in range(YS)] for k in range(group)]
    x_groups = [[y * group + k for k in range(group)] for y in range(YS)]

    def swap(value, groups):
        return lax.all_to_all(value, "noise", 0, 0, axis_index_groups=groups, tiled=True)

    x_near = jnp.concatenate([noise_rows, swap_x(noise_rows, FIRST)], axis=0)
    y_near = jnp.concatenate([data_rows, swap_y(data_rows, FIRST)], axis=0)
    x_near, y_near = lax.optimization_barrier((x_near, y_near))
    x_far, y_far = swap_x(x_near, SECOND), swap_y(y_near, SECOND)
    x_far, y_far, x_there = lax.optimization_barrier((x_far, y_far, to_other_core(x_near)))
    tall, wide = group * rows, YS * rows
    half = depth // 2
    chunk = (tall // depth, wide)
    keep, give, y_all = pl.pallas_call(
        functools.partial(partial_kernel, LOG2E / (epsilon * D)),
        out_shape=[jax.ShapeDtypeStruct((half,) + chunk, f32)] * 2
        + [jax.ShapeDtypeStruct((wide, features), jnp.bfloat16)],
        in_specs=[SMEM] + [VMEM] * 6,
        out_specs=[VMEM] * 3,
        scratch_shapes=[
            pltpu.VMEM((group * rows, features), jnp.bfloat16),
            pltpu.VMEM((1, wide), f32),
            pltpu.VMEM((depth,) + chunk, f32),
        ],
        compiler_params=PARAMS,
    )(place, x_near, x_far, x_there, to_other_core(x_far), y_near, y_far)

    everything = lax.all_gather(y_all, "noise", axis_index_groups=x_groups)
    everything = everything.reshape(group, YS, rows, features)

    got = send_z(give, z_partner)
    sums = pl.pallas_call(
        pair_kernel,
        out_shape=[jax.ShapeDtypeStruct(chunk, f32)] * half,
        in_specs=[VMEM] * 2,
        out_specs=[VMEM] * half,
        compiler_params=PARAMS,
    )(keep, got)

    def ahead(value, k):
        return send_z(value, lambda z, c: z + 2 * k if c == 0 else z - 2 * k)

    back = sums[6] + ahead(sums[4], -2) + ahead(sums[5], -1)
    fore = sums[2] + ahead(sums[3], 1)
    near = sums[0] + ahead(sums[7], -1) + ahead(sums[1], 1)
    own = near + ahead(back, -2) + ahead(fore, 2)

    pieces = swap(own.reshape(group, rows // depth, wide), x_groups)
    everything, pieces = lax.optimization_barrier((everything, pieces))
    gathered = lax.all_gather(pieces, "dp")
    z_groups = [
        [((y * group) + k) * depth + d for y in range(YS) for d in range(depth)] for k in range(group)
    ]
    few = tall // depth
    row_shape = jax.ShapeDtypeStruct((group, 1, few), f32)
    for step in range(EARLY):
        if step == 0:
            part = pl.pallas_call(
                first_rows_kernel,
                out_shape=row_shape,
                in_specs=[VMEM],
                out_specs=VMEM,
                compiler_params=PARAMS,
            )(own)
        else:
            part = pl.pallas_call(
                functools.partial(rows_kernel, log_weight),
                out_shape=row_shape,
                in_specs=[VMEM] * 2,
                out_specs=VMEM,
                compiler_params=PARAMS,
            )(own, part)
        part = swap(part, x_groups)
        part = pl.pallas_call(
            functools.partial(columns_kernel, log_weight),
            out_shape=jax.ShapeDtypeStruct((YS * depth, YS, rows), f32),
            in_specs=[VMEM] * 2,
            out_specs=VMEM,
            scratch_shapes=[pltpu.VMEM((few, wide), f32)],
            compiler_params=PARAMS,
        )(own, part)
        part = lax.all_to_all(
            part, ("noise", "dp"), 0, 0, axis_index_groups=z_groups, tiled=True
        )
    part = pl.pallas_call(
        join_kernel,
        out_shape=jax.ShapeDtypeStruct((group, YS, rows), f32),
        in_specs=[VMEM],
        out_specs=VMEM,
        compiler_params=PARAMS,
    )(part)
    part = swap(part, x_groups)

    copies = lax.axis_size("noise")
    high = 8
    block = tokens // high
    u_shape = jax.ShapeDtypeStruct((rows, rows), f32)
    l_shape = jax.ShapeDtypeStruct((copies, high, block), f32)
    for step in range(EARLY, ITERS):
        if step == EARLY:
            a, u, part = pl.pallas_call(
                functools.partial(whole_rows_kernel, log_weight),
                out_shape=[jax.ShapeDtypeStruct((rows, tokens), f32), u_shape, l_shape],
                in_specs=[VMEM] * 2,
                out_specs=[VMEM] * 3,
                compiler_params=PARAMS,
            )(gathered, part)
        else:
            u, part = pl.pallas_call(
                functools.partial(next_kernel, log_weight),
                out_shape=[u_shape, l_shape],
                in_specs=[VMEM] * 2,
                out_specs=[VMEM] * 2,
                compiler_params=PARAMS,
            )(a, part)
        part = lax.all_to_all(part, "noise", 0, 0, tiled=True)

    steps = YS
    targets, noise_potential, data_potential = pl.pallas_call(
        functools.partial(target_kernel, log_weight, epsilon / LOG2E, steps),
        grid=(steps,),
        out_shape=[
            jax.ShapeDtypeStruct((rows, features), jnp.bfloat16),
            jax.ShapeDtypeStruct((1, rows), f32),
            jax.ShapeDtypeStruct((1, block // 2), f32),
        ],
        in_specs=[
            SMEM,
            pl.BlockSpec((rows, tokens // steps), lambda k: (0, k)),
            pl.BlockSpec((rows, rows), lambda k: (0, 0)),
            pl.BlockSpec((copies, high, block), lambda k: (0, 0, 0)),
            pl.BlockSpec((group, None, rows, features), lambda k: (0, k, 0, 0)),
        ],
        out_specs=[
            pl.BlockSpec((rows, features), lambda k: (0, 0)),
            pl.BlockSpec((1, rows), lambda k: (0, 0)),
            pl.BlockSpec((1, block // 2), lambda k: (0, 0)),
        ],
        scratch_shapes=[
            pltpu.VMEM((rows, features), f32),
            pltpu.VMEM((rows, 1), f32),
            pltpu.VMEM((high, block), f32),
        ],
        compiler_params=PARAMS,
    )(place, a, u, part, everything)
    return targets, noise_potential.reshape(rows), data_potential.reshape(block // 2)


def solution(mesh):
    return jax.shard_map(
        on_device,
        mesh=mesh,
        in_specs=(P("noise", "dp"), P("noise", "dp")),
        out_specs=(P("noise", "dp"), P("noise"), P("dp")),
        check_vma=False,
    )
```

```python
import functools
import math

import jax
import jax.numpy as jnp
from jax import lax
from jax.experimental import pallas as pl
from jax.experimental.pallas import tpu as pltpu
from jax.sharding import PartitionSpec as P

D = 16384
ITERS = 4
EARLY = 2
YS, XS, CORES = 4, 4, 2
LOG2E = math.log2(math.e)
VMEM = pl.BlockSpec(memory_space=pltpu.VMEM)
SMEM = pl.BlockSpec(memory_space=pltpu.SMEM)
PARAMS = pltpu.CompilerParams(vmem_limit_bytes=48 * 1024 * 1024)


def noise_pairs(target):
    pairs = []
    for y in range(YS):
        for x in range(XS):
            for c in range(CORES):
                to_y, to_x, to_c = target(y, x, c)
                pairs.append(((y * XS + x) * CORES + c, (to_y * XS + to_x) * CORES + to_c))
    return pairs


def to_other_core(value):
    return lax.ppermute(value, "noise", noise_pairs(lambda y, x, c: (y, x, 1 - c)))


FIRST, SECOND, BOTH = (1, 3), (3, 1), 2
PLACES = ((0, 0), FIRST, SECOND, (BOTH, BOTH))


def swap_x(value, by):
    return lax.ppermute(value, "noise", noise_pairs(lambda y, x, c: (y, x ^ by[c], c)))


def swap_y(value, by):
    return lax.ppermute(value, "noise", noise_pairs(lambda y, x, c: (y ^ by[c], x, c)))


def send_z(value, target):
    size = lax.axis_size("dp")
    pairs = []
    for n in range(YS * XS * CORES):
        pairs += [(n * size + z, n * size + target(z, n % CORES) % size) for z in range(size)]
    return lax.ppermute(value, ("noise", "dp"), pairs)


def z_partner(z, c):
    return z ^ 1 if c == 0 else z + 1 if z % 2 else z - 1


def squares_row(block):
    wide = block.astype(jnp.float32)
    column = jnp.sum(wide * wide, axis=1, keepdims=True)
    n = block.shape[0]
    row_at = lax.broadcasted_iota(jnp.int32, (n, n), 0)
    column_at = lax.broadcasted_iota(jnp.int32, (n, n), 1)
    return jnp.sum(jnp.where(row_at == column_at, column, 0.0), axis=0, keepdims=True)


def partial_kernel(scale, place_ref, *refs):
    here, there, ys = refs[:2], refs[2:4], refs[4:6]
    keep, give, x_all, y_all, y_squares, chunks = refs[6:]
    rows = here[0].shape[0] // 2
    depth = chunks.shape[0]
    high = rows // depth
    z, y, x, c = place_ref[0], place_ref[1], place_ref[2], place_ref[3]
    for k, (first, second) in enumerate(PLACES):
        block = slice(k % 2 * rows, (k % 2 + 1) * rows)
        mine, other = jnp.where(c == 0, first, second), jnp.where(c == 0, second, first)
        at = pl.multiple_of((lax.bitwise_xor(x, mine) * CORES + c) * rows, rows)
        x_all[pl.ds(at, rows), :] = here[k // 2][block, :]
        at = pl.multiple_of((lax.bitwise_xor(x, other) * CORES + 1 - c) * rows, rows)
        x_all[pl.ds(at, rows), :] = there[k // 2][block, :]
        at = pl.multiple_of(lax.bitwise_xor(y, mine) * rows, rows)
        y_all[pl.ds(at, rows), :] = ys[k // 2][block, :]
    for k in range(YS):
        block = slice(k * rows, (k + 1) * rows)
        y_squares[:, block] = scale * squares_row(y_all[block, :])
    up = jnp.where(c == 0, lax.rem(z, 2) == 0, lax.rem(z, 2) == 1)
    partner = lax.rem(z + jnp.where(up, 1, depth - 1), depth)
    places = []
    for t in range(depth):
        same = lax.rem(z + t, 2) == 0
        base = jnp.where(same, z, partner)
        ahead = jnp.where(c == 0, lax.rem(t + depth - base, depth), lax.rem(base + depth - t, depth))
        places.append(ahead // 2 + jnp.where(same, 0, depth // 2))
    tall = 4 * rows
    for k in range(XS * CORES // 4):
        value = x_all[k * tall : (k + 1) * tall, :]
        wide = value.astype(jnp.float32)
        x_squares = scale * jnp.sum(wide * wide, axis=1, keepdims=True)
        cross = lax.dot_general(
            value, y_all[...], (((1,), (1,)), ((), ())), preferred_element_type=jnp.float32
        )
        value = (2.0 * scale) * cross - x_squares - y_squares[...]
        for i in range(4 * depth):
            block = k * 4 + i // depth
            chunks[places[i % depth], block * high : (block + 1) * high, :] = value[i * high : (i + 1) * high]
    for k in range(depth // 2):
        keep[k] = chunks[k]
        give[k] = chunks[depth // 2 + k]


def pair_kernel(keep, got, own, ahead, back, ahead_rest, back_rest):
    own[...] = keep[0] + got[0]
    middle = keep.shape[0] // 2
    ahead[...] = keep[middle] + got[middle]
    back[...] = keep[middle + 1] + got[middle + 1]
    for k in range(1, middle):
        ahead_rest[middle - 1 - k] = keep[k] + got[k]
    for k in range(middle + 2, keep.shape[0]):
        back_rest[k - middle - 2] = keep[k] + got[k]


def joined(parts):
    peak = jnp.max(parts, axis=0)
    return peak + jnp.log(jnp.sum(jnp.exp2(parts - peak), axis=0)) * LOG2E


def on_diagonal(n):
    rows = lax.broadcasted_iota(jnp.int32, (n, n), 0)
    return rows == lax.broadcasted_iota(jnp.int32, (n, n), 1)


def column_of(u, k):
    n = u.shape[1]
    return jnp.sum(jnp.where(on_diagonal(n), u[k : k + 1], 0.0), axis=1, keepdims=True)


def row_of(parts_ref, log_weight):
    v = log_weight - joined(parts_ref[...])
    return jnp.concatenate([v[k : k + 1] for k in range(v.shape[0])], axis=1)


def copy_out(out_ref):
    whole = out_ref[0]
    for k in range(1, out_ref.shape[0]):
        out_ref[k] = whole


def row_sums(a_ref, v, out_ref, n):
    for k in range(a_ref.shape[0] // n):
        value = a_ref[k * n : (k + 1) * n, :]
        if v is not None:
            value = value + v
        peak = jnp.max(value, axis=1, keepdims=True)
        total = jnp.sum(jnp.exp2(value - peak), axis=1, keepdims=True)
        part = peak + jnp.log(total) * LOG2E
        out_ref[0, k : k + 1, :] = jnp.sum(jnp.where(on_diagonal(n), part, 0.0), axis=0, keepdims=True)
    copy_out(out_ref)


def first_rows_kernel(a_ref, out_ref):
    row_sums(a_ref, None, out_ref, out_ref.shape[2])


def rows_kernel(log_weight, a_ref, parts_ref, out_ref):
    row_sums(a_ref, row_of(parts_ref, log_weight), out_ref, out_ref.shape[2])


def columns_kernel(log_weight, a_ref, parts_ref, out_ref, shifted):
    u = log_weight - joined(parts_ref[...])
    blocks, n = u.shape
    width = a_ref.shape[1]
    peak = None
    for k in range(blocks):
        value = a_ref[k * n : (k + 1) * n, :] + column_of(u, k)
        shifted[k * n : (k + 1) * n, :] = value
        block_peak = jnp.max(value.reshape(n // 8, 8, width), axis=0)
        peak = block_peak if peak is None else jnp.maximum(peak, block_peak)
    peak = jnp.max(peak, axis=0, keepdims=True)
    total = jnp.zeros((8, width), jnp.float32)
    for k in range(blocks):
        value = jnp.exp2(shifted[k * n : (k + 1) * n, :] - peak)
        total = total + jnp.sum(value.reshape(n // 8, 8, width), axis=0)
    part = peak + jnp.log(jnp.sum(total, axis=0, keepdims=True)) * LOG2E
    lanes = out_ref.shape[2]
    for k in range(out_ref.shape[1]):
        out_ref[0, k : k + 1, :] = part[:, k * lanes : (k + 1) * lanes]
    copy_out(out_ref)


def join_kernel(parts_ref, out_ref):
    out_ref[0] = joined(parts_ref[...])
    copy_out(out_ref)


def half_steps(log_weight, a_ref, v, u_ref, l_ref):
    rows, columns = a_ref.shape
    lanes = u_ref.shape[1]
    copies, high, width = l_ref.shape

    @pl.loop(0, rows // 8, step=2)
    def _(base):
        for i in range(2):
            at = pl.ds(pl.multiple_of((base + i) * 8, 8), 8)
            value = a_ref[at, :] + v
            peak = jnp.max(value, axis=1, keepdims=True)
            total = jnp.sum(jnp.exp2(value - peak), axis=1, keepdims=True)
            u = log_weight - (peak + jnp.log(total) * LOG2E)
            u_ref[at, :] = jnp.broadcast_to(u, (8, lanes))

    u = jnp.concatenate([u_ref[...]] * 2, axis=1)
    step = 2 * lanes
    for k in range(high):
        for i in range(width // step):
            at = k * width + i * step
            value = (a_ref[:, at : at + step] + u).reshape(rows // 8, 8, step)
            peak = jnp.max(jnp.max(value, axis=0), axis=0, keepdims=True)
            total = jnp.sum(jnp.sum(jnp.exp2(value - peak), axis=0), axis=0, keepdims=True)
            l_ref[0, k : k + 1, i * step : (i + 1) * step] = peak + jnp.log(total) * LOG2E
    whole = l_ref[0]
    for k in range(1, copies):
        l_ref[k] = whole


def whole_rows_kernel(log_weight, pieces_ref, parts_ref, a_ref, u_ref, l_ref):
    depth, blocks, high, width = pieces_ref.shape
    n = width // YS
    v = log_weight - parts_ref[...]
    for z in range(depth):
        for y in range(YS):
            for k in range(blocks):
                at = (y * blocks + k) * n
                a_ref[z * high : (z + 1) * high, at : at + n] = pieces_ref[z, k, :, y * n : (y + 1) * n]
    v = jnp.concatenate([v[k, y : y + 1] for y in range(YS) for k in range(blocks)], axis=1)
    half_steps(log_weight, a_ref, v, u_ref, l_ref)


def next_kernel(log_weight, a_ref, parts_ref, u_ref, l_ref):
    v = log_weight - joined(parts_ref[...])
    v = jnp.concatenate([v[k : k + 1] for k in range(v.shape[0])], axis=1)
    half_steps(log_weight, a_ref, v, u_ref, l_ref)


def target_kernel(
    log_weight, unit, steps, place_ref, a_ref, u_ref, parts_ref, y_ref, out_ref, f_ref, g_ref, total, mass, v_ref
):
    step = pl.program_id(0)
    lines = v_ref.shape[0] // steps

    @pl.when(step == 0)
    def _():
        total[...] = jnp.zeros_like(total)
        mass[...] = jnp.zeros_like(mass)
        u = u_ref[...]
        f_ref[...] = unit * jnp.sum(jnp.where(on_diagonal(u.shape[0]), u, 0.0), axis=0, keepdims=True)
        v_ref[...] = log_weight - joined(parts_ref[...])
        share = g_ref.shape[1]
        z = place_ref[0]
        line = v_ref[pl.ds(z // 2, 1), :]
        g_ref[...] = unit * jnp.where(lax.rem(z, 2) == 0, line[:, :share], line[:, share:])

    v = jnp.concatenate([v_ref[pl.ds(step * lines + k, 1), :] for k in range(lines)], axis=1)
    u = u_ref[:, :1]
    plan = jnp.exp2((u - log_weight + v) + a_ref[...]).astype(jnp.bfloat16)
    mass[...] += jnp.sum(plan.astype(jnp.float32), axis=1, keepdims=True)
    total[...] += jnp.dot(plan, y_ref[...], preferred_element_type=jnp.float32)

    @pl.when(step == steps - 1)
    def _():
        out_ref[...] = (total[...] / mass[...]).astype(out_ref.dtype)


def on_device(noise_rows, data_rows):
    rows, features = noise_rows.shape
    tokens = rows * lax.axis_size("noise")
    depth = lax.axis_size("dp")
    me, z = lax.axis_index("noise"), lax.axis_index("dp")
    place = jnp.stack([z, me // (XS * CORES), me // CORES % XS, me % CORES]).astype(jnp.int32)
    epsilon = 0.7 / math.sqrt(D)
    log_weight = -math.log2(tokens)
    f32 = jnp.float32

    group = XS * CORES
    y_groups = [[y * group + k for y in range(YS)] for k in range(group)]
    x_groups = [[y * group + k for k in range(group)] for y in range(YS)]

    def swap(value, groups):
        return lax.all_to_all(value, "noise", 0, 0, axis_index_groups=groups, tiled=True)

    x_near = jnp.concatenate([noise_rows, swap_x(noise_rows, FIRST)], axis=0)
    y_near = jnp.concatenate([data_rows, swap_y(data_rows, FIRST)], axis=0)
    x_near, y_near = lax.optimization_barrier((x_near, y_near))
    x_far, y_far = swap_x(x_near, SECOND), swap_y(y_near, SECOND)
    x_there, x_far_there, y_far, late_rows = lax.optimization_barrier(
        (to_other_core(x_near), to_other_core(x_far), y_far, data_rows)
    )
    everything = lax.all_gather(late_rows, "noise", axis=0, tiled=True)
    tall, wide = group * rows, YS * rows
    half = depth // 2
    middle = half // 2
    chunk = (tall // depth, wide)
    keep, give = pl.pallas_call(
        functools.partial(partial_kernel, LOG2E / (epsilon * D)),
        out_shape=[jax.ShapeDtypeStruct((half,) + chunk, f32)] * 2,
        in_specs=[SMEM] + [VMEM] * 6,
        out_specs=[VMEM] * 2,
        scratch_shapes=[
            pltpu.VMEM((group * rows, features), jnp.bfloat16),
            pltpu.VMEM((YS * rows, features), jnp.bfloat16),
            pltpu.VMEM((1, wide), f32),
            pltpu.VMEM((depth,) + chunk, f32),
        ],
        compiler_params=PARAMS,
    )(place, x_near, x_far, x_there, x_far_there, y_near, y_far)

    got = send_z(give, z_partner)
    own, ahead, back, ahead_rest, back_rest = pl.pallas_call(
        pair_kernel,
        out_shape=[
            jax.ShapeDtypeStruct(chunk, f32),
            jax.ShapeDtypeStruct(chunk, f32),
            jax.ShapeDtypeStruct(chunk, f32),
            jax.ShapeDtypeStruct((middle - 1,) + chunk, f32),
            jax.ShapeDtypeStruct((middle - 2,) + chunk, f32),
        ],
        in_specs=[VMEM] * 2,
        out_specs=[VMEM] * 5,
        compiler_params=PARAMS,
    )(keep, got)
    for step in range(middle):
        ahead = send_z(ahead, lambda z, c: z + 2 if c == 0 else z - 2)
        if step < middle - 1:
            ahead = ahead + ahead_rest[step]
            back = send_z(back, lambda z, c: z - 2 if c == 0 else z + 2)
            if step < middle - 2:
                back = back + back_rest[step]
    own = own + ahead + back

    pieces = swap(own.reshape(group, rows // depth, wide), x_groups)
    everything, pieces = lax.optimization_barrier((everything, pieces))
    gathered = lax.all_gather(pieces, "dp")
    z_groups = [
        [((y * group) + k) * depth + d for y in range(YS) for d in range(depth)] for k in range(group)
    ]
    few = tall // depth
    row_shape = jax.ShapeDtypeStruct((group, 1, few), f32)
    for step in range(EARLY):
        if step == 0:
            part = pl.pallas_call(
                first_rows_kernel,
                out_shape=row_shape,
                in_specs=[VMEM],
                out_specs=VMEM,
                compiler_params=PARAMS,
            )(own)
        else:
            part = pl.pallas_call(
                functools.partial(rows_kernel, log_weight),
                out_shape=row_shape,
                in_specs=[VMEM] * 2,
                out_specs=VMEM,
                compiler_params=PARAMS,
            )(own, part)
        part = swap(part, x_groups)
        part = pl.pallas_call(
            functools.partial(columns_kernel, log_weight),
            out_shape=jax.ShapeDtypeStruct((YS * depth, YS, rows), f32),
            in_specs=[VMEM] * 2,
            out_specs=VMEM,
            scratch_shapes=[pltpu.VMEM((few, wide), f32)],
            compiler_params=PARAMS,
        )(own, part)
        part = lax.all_to_all(
            part, ("noise", "dp"), 0, 0, axis_index_groups=z_groups, tiled=True
        )
    part = pl.pallas_call(
        join_kernel,
        out_shape=jax.ShapeDtypeStruct((group, YS, rows), f32),
        in_specs=[VMEM],
        out_specs=VMEM,
        compiler_params=PARAMS,
    )(part)
    part = swap(part, x_groups)

    copies = lax.axis_size("noise")
    high = 8
    block = tokens // high
    u_shape = jax.ShapeDtypeStruct((rows, rows), f32)
    l_shape = jax.ShapeDtypeStruct((copies, high, block), f32)
    for step in range(EARLY, ITERS):
        if step == EARLY:
            a, u, part = pl.pallas_call(
                functools.partial(whole_rows_kernel, log_weight),
                out_shape=[jax.ShapeDtypeStruct((rows, tokens), f32), u_shape, l_shape],
                in_specs=[VMEM] * 2,
                out_specs=[VMEM] * 3,
                compiler_params=PARAMS,
            )(gathered, part)
        else:
            u, part = pl.pallas_call(
                functools.partial(next_kernel, log_weight),
                out_shape=[u_shape, l_shape],
                in_specs=[VMEM] * 2,
                out_specs=[VMEM] * 2,
                compiler_params=PARAMS,
            )(a, part)
        part = lax.all_to_all(part, "noise", 0, 0, tiled=True)

    steps = 4
    targets, noise_potential, data_potential = pl.pallas_call(
        functools.partial(target_kernel, log_weight, epsilon / LOG2E, steps),
        grid=(steps,),
        out_shape=[
            jax.ShapeDtypeStruct((rows, features), jnp.bfloat16),
            jax.ShapeDtypeStruct((1, rows), f32),
            jax.ShapeDtypeStruct((1, block // 2), f32),
        ],
        in_specs=[
            SMEM,
            pl.BlockSpec((rows, tokens // steps), lambda k: (0, k)),
            pl.BlockSpec((rows, rows), lambda k: (0, 0)),
            pl.BlockSpec((copies, high, block), lambda k: (0, 0, 0)),
            pl.BlockSpec((tokens // steps, features), lambda k: (k, 0)),
        ],
        out_specs=[
            pl.BlockSpec((rows, features), lambda k: (0, 0)),
            pl.BlockSpec((1, rows), lambda k: (0, 0)),
            pl.BlockSpec((1, block // 2), lambda k: (0, 0)),
        ],
        scratch_shapes=[
            pltpu.VMEM((rows, features), f32),
            pltpu.VMEM((rows, 1), f32),
            pltpu.VMEM((high, block), f32),
        ],
        compiler_params=PARAMS,
    )(place, a, u, part, everything)
    return targets, noise_potential.reshape(rows), data_potential.reshape(block // 2)


def solution(mesh):
    return jax.shard_map(
        on_device,
        mesh=mesh,
        in_specs=(P("noise", "dp"), P("noise", "dp")),
        out_specs=(P("noise", "dp"), P("noise"), P("dp")),
        check_vma=False,
    )
```

```python
import functools
import math

import jax
import jax.numpy as jnp
from jax import lax
from jax.experimental import pallas as pl
from jax.experimental.pallas import tpu as pltpu
from jax.sharding import PartitionSpec as P

D = 16384
ITERS = 4
EARLY = 2
YS, XS, CORES = 4, 4, 2
LOG2E = math.log2(math.e)
VMEM = pl.BlockSpec(memory_space=pltpu.VMEM)
SMEM = pl.BlockSpec(memory_space=pltpu.SMEM)
PARAMS = pltpu.CompilerParams(vmem_limit_bytes=48 * 1024 * 1024)


def noise_pairs(target):
    pairs = []
    for y in range(YS):
        for x in range(XS):
            for c in range(CORES):
                to_y, to_x, to_c = target(y, x, c)
                pairs.append(((y * XS + x) * CORES + c, (to_y * XS + to_x) * CORES + to_c))
    return pairs


def to_other_core(value):
    return lax.ppermute(value, "noise", noise_pairs(lambda y, x, c: (y, x, 1 - c)))


FIRST, SECOND, BOTH = (1, 3), (3, 1), 2
PLACES = ((0, 0), FIRST, SECOND, (BOTH, BOTH))


def swap_x(value, by):
    return lax.ppermute(value, "noise", noise_pairs(lambda y, x, c: (y, x ^ by[c], c)))


def swap_y(value, by):
    return lax.ppermute(value, "noise", noise_pairs(lambda y, x, c: (y ^ by[c], x, c)))


def stacked(block, received):
    rows, features = block.shape
    both = lax.dynamic_update_slice(jnp.zeros((2 * rows, features), block.dtype), block, (0, 0))
    both = lax.optimization_barrier(both)
    return lax.dynamic_update_slice(both, received, (rows, 0))


def send_z(value, target):
    size = lax.axis_size("dp")
    pairs = []
    for n in range(YS * XS * CORES):
        pairs += [(n * size + z, n * size + target(z, n % CORES) % size) for z in range(size)]
    return lax.ppermute(value, ("noise", "dp"), pairs)


def z_partner(z, c):
    return z ^ 1 if c == 0 else z + 1 if z % 2 else z - 1


def squares_row(block):
    wide = block.astype(jnp.float32)
    column = jnp.sum(wide * wide, axis=1, keepdims=True)
    n = block.shape[0]
    row_at = lax.broadcasted_iota(jnp.int32, (n, n), 0)
    column_at = lax.broadcasted_iota(jnp.int32, (n, n), 1)
    return jnp.sum(jnp.where(row_at == column_at, column, 0.0), axis=0, keepdims=True)


def partial_kernel(scale, place_ref, *refs):
    here, there, ys = refs[:2], refs[2:4], refs[4:6]
    keep, give, x_all, y_all, y_squares, chunks = refs[6:]
    rows = here[0].shape[0] // 2
    depth = chunks.shape[0]
    high = rows // depth
    z, y, x, c = place_ref[0], place_ref[1], place_ref[2], place_ref[3]
    for k, (first, second) in enumerate(PLACES):
        block = slice(k % 2 * rows, (k % 2 + 1) * rows)
        mine, other = jnp.where(c == 0, first, second), jnp.where(c == 0, second, first)
        at = pl.multiple_of((lax.bitwise_xor(x, mine) * CORES + c) * rows, rows)
        x_all[pl.ds(at, rows), :] = here[k // 2][block, :]
        at = pl.multiple_of((lax.bitwise_xor(x, other) * CORES + 1 - c) * rows, rows)
        x_all[pl.ds(at, rows), :] = there[k // 2][block, :]
        at = pl.multiple_of(lax.bitwise_xor(y, mine) * rows, rows)
        y_all[pl.ds(at, rows), :] = ys[k // 2][block, :]
    for k in range(YS):
        block = slice(k * rows, (k + 1) * rows)
        y_squares[:, block] = scale * squares_row(y_all[block, :])
    up = jnp.where(c == 0, lax.rem(z, 2) == 0, lax.rem(z, 2) == 1)
    partner = lax.rem(z + jnp.where(up, 1, depth - 1), depth)
    places = []
    for t in range(depth):
        same = lax.rem(z + t, 2) == 0
        base = jnp.where(same, z, partner)
        ahead = jnp.where(c == 0, lax.rem(t + depth - base, depth), lax.rem(base + depth - t, depth))
        places.append(ahead // 2 + jnp.where(same, 0, depth // 2))
    tall = 4 * rows
    for k in range(XS * CORES // 4):
        value = x_all[k * tall : (k + 1) * tall, :]
        wide = value.astype(jnp.float32)
        x_squares = scale * jnp.sum(wide * wide, axis=1, keepdims=True)
        cross = lax.dot_general(
            value, y_all[...], (((1,), (1,)), ((), ())), preferred_element_type=jnp.float32
        )
        value = (2.0 * scale) * cross - x_squares - y_squares[...]
        for i in range(4 * depth):
            block = k * 4 + i // depth
            chunks[places[i % depth], block * high : (block + 1) * high, :] = value[i * high : (i + 1) * high]
    for k in range(depth // 2):
        keep[k] = chunks[k]
        give[k] = chunks[depth // 2 + k]


def pair_kernel(keep, got, own, ahead, back, ahead_rest, back_rest):
    own[...] = keep[0] + got[0]
    middle = keep.shape[0] // 2
    ahead[...] = keep[middle] + got[middle]
    back[...] = keep[middle + 1] + got[middle + 1]
    for k in range(1, middle):
        ahead_rest[middle - 1 - k] = keep[k] + got[k]
    for k in range(middle + 2, keep.shape[0]):
        back_rest[k - middle - 2] = keep[k] + got[k]


def joined(parts):
    peak = jnp.max(parts, axis=0)
    return peak + jnp.log(jnp.sum(jnp.exp2(parts - peak), axis=0)) * LOG2E


def on_diagonal(n):
    rows = lax.broadcasted_iota(jnp.int32, (n, n), 0)
    return rows == lax.broadcasted_iota(jnp.int32, (n, n), 1)


def column_of(u, k):
    n = u.shape[1]
    return jnp.sum(jnp.where(on_diagonal(n), u[k : k + 1], 0.0), axis=1, keepdims=True)


def row_of(parts_ref, log_weight):
    v = log_weight - joined(parts_ref[...])
    return jnp.concatenate([v[k : k + 1] for k in range(v.shape[0])], axis=1)


def copy_out(out_ref):
    whole = out_ref[0]
    for k in range(1, out_ref.shape[0]):
        out_ref[k] = whole


def row_sums(a_ref, v, out_ref, n):
    for k in range(a_ref.shape[0] // n):
        value = a_ref[k * n : (k + 1) * n, :]
        if v is not None:
            value = value + v
        peak = jnp.max(value, axis=1, keepdims=True)
        total = jnp.sum(jnp.exp2(value - peak), axis=1, keepdims=True)
        part = peak + jnp.log(total) * LOG2E
        out_ref[0, k : k + 1, :] = jnp.sum(jnp.where(on_diagonal(n), part, 0.0), axis=0, keepdims=True)
    copy_out(out_ref)


def first_rows_kernel(a_ref, out_ref, sums):
    copies, both, width = out_ref.shape
    high, n = both // 2, a_ref.shape[0]
    row_sums(a_ref, None, sums, n)
    for k in range(copies):
        out_ref[k, :high, :] = a_ref[k * high : (k + 1) * high, :]
        out_ref[k, high:, :] = jnp.zeros((high, width), jnp.float32)
        out_ref[k, high : high + 1, :n] = sums[0]


def rows_kernel(log_weight, a_ref, parts_ref, out_ref):
    row_sums(a_ref, row_of(parts_ref, log_weight), out_ref, out_ref.shape[2])


def columns_kernel(log_weight, under, a_ref, parts_ref, out_ref, shifted):
    parts = parts_ref[:, under : under + 1, : a_ref.shape[0]]
    u = log_weight - joined(parts)
    blocks, n = u.shape
    width = a_ref.shape[1]
    peak = None
    for k in range(blocks):
        value = a_ref[k * n : (k + 1) * n, :] + column_of(u, k)
        shifted[k * n : (k + 1) * n, :] = value
        block_peak = jnp.max(value.reshape(n // 8, 8, width), axis=0)
        peak = block_peak if peak is None else jnp.maximum(peak, block_peak)
    peak = jnp.max(peak, axis=0, keepdims=True)
    total = jnp.zeros((8, width), jnp.float32)
    for k in range(blocks):
        value = jnp.exp2(shifted[k * n : (k + 1) * n, :] - peak)
        total = total + jnp.sum(value.reshape(n // 8, 8, width), axis=0)
    part = peak + jnp.log(jnp.sum(total, axis=0, keepdims=True)) * LOG2E
    lanes = out_ref.shape[2]
    for k in range(out_ref.shape[1]):
        out_ref[0, k : k + 1, :] = part[:, k * lanes : (k + 1) * lanes]
    copy_out(out_ref)


def join_kernel(parts_ref, out_ref):
    out_ref[0] = joined(parts_ref[...])
    copy_out(out_ref)


def half_steps(log_weight, a_ref, v, u_ref, l_ref):
    rows, columns = a_ref.shape
    lanes = u_ref.shape[1]
    copies, high, width = l_ref.shape

    @pl.loop(0, rows // 8, step=2)
    def _(base):
        for i in range(2):
            at = pl.ds(pl.multiple_of((base + i) * 8, 8), 8)
            value = a_ref[at, :] + v
            peak = jnp.max(value, axis=1, keepdims=True)
            total = jnp.sum(jnp.exp2(value - peak), axis=1, keepdims=True)
            u = log_weight - (peak + jnp.log(total) * LOG2E)
            u_ref[at, :] = jnp.broadcast_to(u, (8, lanes))

    u = jnp.concatenate([u_ref[...]] * 2, axis=1)
    step = 2 * lanes
    for k in range(high):
        for i in range(width // step):
            at = k * width + i * step
            value = (a_ref[:, at : at + step] + u).reshape(rows // 8, 8, step)
            peak = jnp.max(jnp.max(value, axis=0), axis=0, keepdims=True)
            total = jnp.sum(jnp.sum(jnp.exp2(value - peak), axis=0), axis=0, keepdims=True)
            l_ref[0, k : k + 1, i * step : (i + 1) * step] = peak + jnp.log(total) * LOG2E
    whole = l_ref[0]
    for k in range(1, copies):
        l_ref[k] = whole


def whole_rows_kernel(log_weight, place_ref, pieces_ref, parts_ref, a_ref, u_ref, l_ref):
    depth, blocks, high, width = pieces_ref.shape
    n = width // YS
    v = log_weight - parts_ref[...]
    c = place_ref[3]
    for z in range(depth):
        to = pl.ds(pl.multiple_of(jnp.where(c == 0, z, depth - 1 - z) * high, high), high)
        for y in range(YS):
            for k in range(blocks):
                at = (y * blocks + k) * n
                a_ref[to, at : at + n] = pieces_ref[z, k, :, y * n : (y + 1) * n]
    v = jnp.concatenate([v[k, y : y + 1] for y in range(YS) for k in range(blocks)], axis=1)
    half_steps(log_weight, a_ref, v, u_ref, l_ref)


def next_kernel(log_weight, a_ref, parts_ref, u_ref, l_ref):
    v = log_weight - joined(parts_ref[...])
    v = jnp.concatenate([v[k : k + 1] for k in range(v.shape[0])], axis=1)
    half_steps(log_weight, a_ref, v, u_ref, l_ref)


def target_kernel(
    log_weight, unit, steps, place_ref, a_ref, u_ref, parts_ref, y_ref, out_ref, f_ref, g_ref, total, mass, v_ref
):
    step = pl.program_id(0)
    lines = v_ref.shape[0] // steps

    @pl.when(step == 0)
    def _():
        total[...] = jnp.zeros_like(total)
        mass[...] = jnp.zeros_like(mass)
        u = u_ref[...]
        f_ref[...] = unit * jnp.sum(jnp.where(on_diagonal(u.shape[0]), u, 0.0), axis=0, keepdims=True)
        v_ref[...] = log_weight - joined(parts_ref[...])
        share = g_ref.shape[1]
        z = place_ref[0]
        line = v_ref[pl.ds(z // 2, 1), :]
        g_ref[...] = unit * jnp.where(lax.rem(z, 2) == 0, line[:, :share], line[:, share:])

    v = jnp.concatenate([v_ref[pl.ds(step * lines + k, 1), :] for k in range(lines)], axis=1)
    u = u_ref[:, :1]
    plan = jnp.exp2((u - log_weight + v) + a_ref[...]).astype(jnp.bfloat16)
    mass[...] += jnp.sum(plan.astype(jnp.float32), axis=1, keepdims=True)
    total[...] += jnp.dot(plan, y_ref[...], preferred_element_type=jnp.float32)

    @pl.when(step == steps - 1)
    def _():
        out_ref[...] = (total[...] / mass[...]).astype(out_ref.dtype)


def on_device(noise_rows, data_rows):
    rows, features = noise_rows.shape
    tokens = rows * lax.axis_size("noise")
    depth = lax.axis_size("dp")
    me, z = lax.axis_index("noise"), lax.axis_index("dp")
    place = jnp.stack([z, me // (XS * CORES), me // CORES % XS, me % CORES]).astype(jnp.int32)
    epsilon = 0.7 / math.sqrt(D)
    log_weight = -math.log2(tokens)
    f32 = jnp.float32

    group = XS * CORES
    y_groups = [[y * group + k for y in range(YS)] for k in range(group)]
    x_groups = [[y * group + k for k in range(group)] for y in range(YS)]

    def swap(value, groups):
        return lax.all_to_all(value, "noise", 0, 0, axis_index_groups=groups, tiled=True)

    x_near = stacked(noise_rows, swap_x(noise_rows, FIRST))
    y_near = stacked(data_rows, swap_y(data_rows, FIRST))
    x_near, y_near = lax.optimization_barrier((x_near, y_near))
    x_far, y_far = swap_x(x_near, SECOND), swap_y(y_near, SECOND)
    x_there, x_far_there, y_far, late_rows = lax.optimization_barrier(
        (to_other_core(x_near), to_other_core(x_far), y_far, data_rows)
    )
    everything = lax.all_gather(late_rows, "noise", axis=0, tiled=True)
    tall, wide = group * rows, YS * rows
    half = depth // 2
    middle = half // 2
    chunk = (tall // depth, wide)
    keep, give = pl.pallas_call(
        functools.partial(partial_kernel, LOG2E / (epsilon * D)),
        out_shape=[jax.ShapeDtypeStruct((half,) + chunk, f32)] * 2,
        in_specs=[SMEM] + [VMEM] * 6,
        out_specs=[VMEM] * 2,
        scratch_shapes=[
            pltpu.VMEM((group * rows, features), jnp.bfloat16),
            pltpu.VMEM((YS * rows, features), jnp.bfloat16),
            pltpu.VMEM((1, wide), f32),
            pltpu.VMEM((depth,) + chunk, f32),
        ],
        compiler_params=PARAMS,
    )(place, x_near, x_far, x_there, x_far_there, y_near, y_far)

    got = send_z(give, z_partner)
    own, ahead, back, ahead_rest, back_rest = pl.pallas_call(
        pair_kernel,
        out_shape=[
            jax.ShapeDtypeStruct(chunk, f32),
            jax.ShapeDtypeStruct(chunk, f32),
            jax.ShapeDtypeStruct(chunk, f32),
            jax.ShapeDtypeStruct((middle - 1,) + chunk, f32),
            jax.ShapeDtypeStruct((middle - 2,) + chunk, f32),
        ],
        in_specs=[VMEM] * 2,
        out_specs=[VMEM] * 5,
        compiler_params=PARAMS,
    )(keep, got)
    for step in range(middle):
        ahead = send_z(ahead, lambda z, c: z + 2 if c == 0 else z - 2)
        if step < middle - 1:
            ahead = ahead + ahead_rest[step]
            back = send_z(back, lambda z, c: z - 2 if c == 0 else z + 2)
            if step < middle - 2:
                back = back + back_rest[step]
    own = own + ahead + back

    few = tall // depth
    high = rows // depth
    part = pl.pallas_call(
        first_rows_kernel,
        out_shape=jax.ShapeDtypeStruct((group, 2 * high, wide), f32),
        in_specs=[VMEM],
        out_specs=VMEM,
        scratch_shapes=[pltpu.VMEM((1, 1, few), f32)],
        compiler_params=PARAMS,
    )(own)
    part = swap(part, x_groups)
    everything, pieces = lax.optimization_barrier((everything, part[:, :high]))
    ring_groups = [
        [n * depth + (depth - 1 - d if n % CORES else d) for d in range(depth)] for n in range(YS * group)
    ]
    gathered = lax.all_gather(pieces, ("noise", "dp"), axis_index_groups=ring_groups)
    z_groups = [
        [((y * group) + k) * depth + d for y in range(YS) for d in range(depth)] for k in range(group)
    ]
    row_shape = jax.ShapeDtypeStruct((group, 1, few), f32)
    for step in range(EARLY):
        if step > 0:
            part = pl.pallas_call(
                functools.partial(rows_kernel, log_weight),
                out_shape=row_shape,
                in_specs=[VMEM] * 2,
                out_specs=VMEM,
                compiler_params=PARAMS,
            )(own, part)
            part = swap(part, x_groups)
        part = pl.pallas_call(
            functools.partial(columns_kernel, log_weight, 0 if step > 0 else high),
            out_shape=jax.ShapeDtypeStruct((YS * depth, YS, rows), f32),
            in_specs=[VMEM] * 2,
            out_specs=VMEM,
            scratch_shapes=[pltpu.VMEM((few, wide), f32)],
            compiler_params=PARAMS,
        )(own, part)
        part = lax.all_to_all(
            part, ("noise", "dp"), 0, 0, axis_index_groups=z_groups, tiled=True
        )
    part = pl.pallas_call(
        join_kernel,
        out_shape=jax.ShapeDtypeStruct((group, YS, rows), f32),
        in_specs=[VMEM],
        out_specs=VMEM,
        compiler_params=PARAMS,
    )(part)
    part = swap(part, x_groups)

    copies = lax.axis_size("noise")
    lines = 8
    block = tokens // lines
    u_shape = jax.ShapeDtypeStruct((rows, rows), f32)
    l_shape = jax.ShapeDtypeStruct((copies, lines, block), f32)
    for step in range(EARLY, ITERS):
        if step == EARLY:
            a, u, part = pl.pallas_call(
                functools.partial(whole_rows_kernel, log_weight),
                out_shape=[jax.ShapeDtypeStruct((rows, tokens), f32), u_shape, l_shape],
                in_specs=[SMEM] + [VMEM] * 2,
                out_specs=[VMEM] * 3,
                compiler_params=PARAMS,
            )(place, gathered, part)
        else:
            u, part = pl.pallas_call(
                functools.partial(next_kernel, log_weight),
                out_shape=[u_shape, l_shape],
                in_specs=[VMEM] * 2,
                out_specs=[VMEM] * 2,
                compiler_params=PARAMS,
            )(a, part)
        part = lax.all_to_all(part, "noise", 0, 0, tiled=True)

    steps = 4
    targets, noise_potential, data_potential = pl.pallas_call(
        functools.partial(target_kernel, log_weight, epsilon / LOG2E, steps),
        grid=(steps,),
        out_shape=[
            jax.ShapeDtypeStruct((rows, features), jnp.bfloat16),
            jax.ShapeDtypeStruct((1, rows), f32),
            jax.ShapeDtypeStruct((1, block // 2), f32),
        ],
        in_specs=[
            SMEM,
            pl.BlockSpec((rows, tokens // steps), lambda k: (0, k)),
            pl.BlockSpec((rows, rows), lambda k: (0, 0)),
            pl.BlockSpec((copies, lines, block), lambda k: (0, 0, 0)),
            pl.BlockSpec((tokens // steps, features), lambda k: (k, 0)),
        ],
        out_specs=[
            pl.BlockSpec((rows, features), lambda k: (0, 0)),
            pl.BlockSpec((1, rows), lambda k: (0, 0)),
            pl.BlockSpec((1, block // 2), lambda k: (0, 0)),
        ],
        scratch_shapes=[
            pltpu.VMEM((rows, features), f32),
            pltpu.VMEM((rows, 1), f32),
            pltpu.VMEM((lines, block), f32),
        ],
        compiler_params=PARAMS,
    )(place, a, u, part, everything)
    return targets, noise_potential.reshape(rows), data_potential.reshape(block // 2)


def solution(mesh):
    return jax.shard_map(
        on_device,
        mesh=mesh,
        in_specs=(P("noise", "dp"), P("noise", "dp")),
        out_specs=(P("noise", "dp"), P("noise"), P("dp")),
        check_vma=False,
    )
```

```python
import functools
import math

import jax
import jax.numpy as jnp
from jax import lax
from jax.experimental import pallas as pl
from jax.experimental.pallas import tpu as pltpu
from jax.sharding import PartitionSpec as P

D = 16384
ITERS = 4
EARLY = 2
YS, XS, CORES = 4, 4, 2
LOG2E = math.log2(math.e)
VMEM = pl.BlockSpec(memory_space=pltpu.VMEM)
SMEM = pl.BlockSpec(memory_space=pltpu.SMEM)
PARAMS = pltpu.CompilerParams(vmem_limit_bytes=48 * 1024 * 1024)


def noise_pairs(target):
    pairs = []
    for y in range(YS):
        for x in range(XS):
            for c in range(CORES):
                to_y, to_x, to_c = target(y, x, c)
                pairs.append(((y * XS + x) * CORES + c, (to_y * XS + to_x) * CORES + to_c))
    return pairs


def to_other_core(value):
    return lax.ppermute(value, "noise", noise_pairs(lambda y, x, c: (y, x, 1 - c)))


FIRST, SECOND, BOTH = (1, 3), (3, 1), 2
PLACES = ((0, 0), FIRST, SECOND, (BOTH, BOTH))


def swap_x(value, by):
    return lax.ppermute(value, "noise", noise_pairs(lambda y, x, c: (y, x ^ by[c], c)))


def swap_y(value, by):
    return lax.ppermute(value, "noise", noise_pairs(lambda y, x, c: (y ^ by[c], x, c)))


def stacked(block, received):
    rows, features = block.shape
    both = lax.dynamic_update_slice(jnp.zeros((2 * rows, features), block.dtype), block, (0, 0))
    both = lax.optimization_barrier(both)
    return lax.dynamic_update_slice(both, received, (rows, 0))


def send_z(value, target):
    size = lax.axis_size("dp")
    pairs = []
    for n in range(YS * XS * CORES):
        pairs += [(n * size + z, n * size + target(z, n % CORES) % size) for z in range(size)]
    return lax.ppermute(value, ("noise", "dp"), pairs)


def z_partner(z, c):
    return z ^ 1 if c == 0 else z + 1 if z % 2 else z - 1


def squares_row(block):
    wide = block.astype(jnp.float32)
    column = jnp.sum(wide * wide, axis=1, keepdims=True)
    n = block.shape[0]
    row_at = lax.broadcasted_iota(jnp.int32, (n, n), 0)
    column_at = lax.broadcasted_iota(jnp.int32, (n, n), 1)
    return jnp.sum(jnp.where(row_at == column_at, column, 0.0), axis=0, keepdims=True)


def partial_kernel(scale, place_ref, *refs):
    here, there, ys = refs[:2], refs[2:4], refs[4:6]
    keep, give, x_all, y_all, y_squares, chunks = refs[6:]
    rows = here[0].shape[0] // 2
    depth = chunks.shape[0]
    high = rows // depth
    z, y, x, c = place_ref[0], place_ref[1], place_ref[2], place_ref[3]
    for k, (first, second) in enumerate(PLACES):
        block = slice(k % 2 * rows, (k % 2 + 1) * rows)
        mine, other = jnp.where(c == 0, first, second), jnp.where(c == 0, second, first)
        at = pl.multiple_of((lax.bitwise_xor(x, mine) * CORES + c) * rows, rows)
        x_all[pl.ds(at, rows), :] = here[k // 2][block, :]
        at = pl.multiple_of((lax.bitwise_xor(x, other) * CORES + 1 - c) * rows, rows)
        x_all[pl.ds(at, rows), :] = there[k // 2][block, :]
        at = pl.multiple_of(lax.bitwise_xor(y, mine) * rows, rows)
        y_all[pl.ds(at, rows), :] = ys[k // 2][block, :]
    for k in range(YS):
        block = slice(k * rows, (k + 1) * rows)
        y_squares[:, block] = scale * squares_row(y_all[block, :])
    up = jnp.where(c == 0, lax.rem(z, 2) == 0, lax.rem(z, 2) == 1)
    partner = lax.rem(z + jnp.where(up, 1, depth - 1), depth)
    places = []
    for t in range(depth):
        same = lax.rem(z + t, 2) == 0
        base = jnp.where(same, z, partner)
        ahead = jnp.where(c == 0, lax.rem(t + depth - base, depth), lax.rem(base + depth - t, depth))
        places.append(ahead // 2 + jnp.where(same, 0, depth // 2))
    tall = 4 * rows
    for k in range(XS * CORES // 4):
        value = x_all[k * tall : (k + 1) * tall, :]
        wide = value.astype(jnp.float32)
        x_squares = scale * jnp.sum(wide * wide, axis=1, keepdims=True)
        cross = lax.dot_general(
            value, y_all[...], (((1,), (1,)), ((), ())), preferred_element_type=jnp.float32
        )
        value = (2.0 * scale) * cross - x_squares - y_squares[...]
        for i in range(4 * depth):
            block = k * 4 + i // depth
            chunks[places[i % depth], block * high : (block + 1) * high, :] = value[i * high : (i + 1) * high]
    for k in range(depth // 2):
        keep[k] = chunks[k]
        give[k] = chunks[depth // 2 + k]


def pair_kernel(keep, got, own, ahead, back, ahead_rest, back_rest):
    own[...] = keep[0] + got[0]
    middle = keep.shape[0] // 2
    ahead[...] = keep[middle] + got[middle]
    back[...] = keep[middle + 1] + got[middle + 1]
    for k in range(1, middle):
        ahead_rest[middle - 1 - k] = keep[k] + got[k]
    for k in range(middle + 2, keep.shape[0]):
        back_rest[k - middle - 2] = keep[k] + got[k]


def joined(parts):
    peak = jnp.max(parts, axis=0)
    return peak + jnp.log(jnp.sum(jnp.exp2(parts - peak), axis=0)) * LOG2E


def on_diagonal(n):
    rows = lax.broadcasted_iota(jnp.int32, (n, n), 0)
    return rows == lax.broadcasted_iota(jnp.int32, (n, n), 1)


def column_of(u, k):
    n = u.shape[1]
    return jnp.sum(jnp.where(on_diagonal(n), u[k : k + 1], 0.0), axis=1, keepdims=True)


def row_of(parts_ref, log_weight):
    v = log_weight - joined(parts_ref[...])
    return jnp.concatenate([v[k : k + 1] for k in range(v.shape[0])], axis=1)


def copy_out(out_ref):
    whole = out_ref[0]
    for k in range(1, out_ref.shape[0]):
        out_ref[k] = whole


def row_sums(a_ref, v, out_ref, n):
    for k in range(a_ref.shape[0] // n):
        value = a_ref[k * n : (k + 1) * n, :]
        if v is not None:
            value = value + v
        peak = jnp.max(value, axis=1, keepdims=True)
        total = jnp.sum(jnp.exp2(value - peak), axis=1, keepdims=True)
        part = peak + jnp.log(total) * LOG2E
        out_ref[0, k : k + 1, :] = jnp.sum(jnp.where(on_diagonal(n), part, 0.0), axis=0, keepdims=True)
    copy_out(out_ref)


def first_rows_kernel(a_ref, out_ref, sums):
    copies, high, width = out_ref.shape
    n, columns = a_ref.shape
    row_sums(a_ref, None, sums, n)
    for k in range(copies):
        out_ref[k, :, :columns] = a_ref[k * high : (k + 1) * high, :]
        out_ref[k, :, columns:] = jnp.zeros((high, width - columns), jnp.float32)
        out_ref[k, :1, columns : columns + n] = sums[0]


def rows_kernel(log_weight, a_ref, parts_ref, out_ref):
    row_sums(a_ref, row_of(parts_ref, log_weight), out_ref, out_ref.shape[2])


def columns_kernel(log_weight, beside, a_ref, parts_ref, out_ref, shifted):
    parts = parts_ref[:, :1, beside : beside + a_ref.shape[0]]
    u = log_weight - joined(parts)
    blocks, n = u.shape
    width = a_ref.shape[1]
    peak = None
    for k in range(blocks):
        value = a_ref[k * n : (k + 1) * n, :] + column_of(u, k)
        shifted[k * n : (k + 1) * n, :] = value
        block_peak = jnp.max(value.reshape(n // 8, 8, width), axis=0)
        peak = block_peak if peak is None else jnp.maximum(peak, block_peak)
    peak = jnp.max(peak, axis=0, keepdims=True)
    total = jnp.zeros((8, width), jnp.float32)
    for k in range(blocks):
        value = jnp.exp2(shifted[k * n : (k + 1) * n, :] - peak)
        total = total + jnp.sum(value.reshape(n // 8, 8, width), axis=0)
    part = peak + jnp.log(jnp.sum(total, axis=0, keepdims=True)) * LOG2E
    lanes = out_ref.shape[2]
    for k in range(out_ref.shape[1]):
        out_ref[0, k : k + 1, :] = part[:, k * lanes : (k + 1) * lanes]
    copy_out(out_ref)


def join_kernel(parts_ref, out_ref):
    out_ref[0] = joined(parts_ref[...])
    copy_out(out_ref)


def row_step(log_weight, value, u_ref, at):
    peak = jnp.max(value, axis=1, keepdims=True)
    total = jnp.sum(jnp.exp2(value - peak), axis=1, keepdims=True)
    u = log_weight - (peak + jnp.log(total) * LOG2E)
    u_ref[at, :] = jnp.broadcast_to(u, (value.shape[0], u_ref.shape[1]))


def column_step(a_ref, u_ref, l_ref):
    rows, lanes = u_ref.shape
    copies, high, width = l_ref.shape
    u = jnp.concatenate([u_ref[...]] * 2, axis=1)
    step = 2 * lanes
    for k in range(high):
        for i in range(width // step):
            at = k * width + i * step
            value = (a_ref[:, at : at + step] + u).reshape(rows // 8, 8, step)
            peak = jnp.max(jnp.max(value, axis=0), axis=0, keepdims=True)
            total = jnp.sum(jnp.sum(jnp.exp2(value - peak), axis=0), axis=0, keepdims=True)
            l_ref[0, k : k + 1, i * step : (i + 1) * step] = peak + jnp.log(total) * LOG2E
    copy_out(l_ref)


def whole_rows_kernel(log_weight, pieces_ref, parts_ref, a_ref, u_ref, l_ref, pieces, arrived):
    depth, blocks, high, width = pieces.shape
    n = width // YS
    copies = [pltpu.make_async_copy(pieces_ref.at[z], pieces.at[z], arrived.at[z]) for z in range(depth)]
    for copy in copies:
        copy.start()
    v = log_weight - parts_ref[...]
    v = jnp.concatenate([v[k, y : y + 1] for y in range(YS) for k in range(blocks)], axis=1)
    for z in range(depth):
        copies[z].wait()
        value = [pieces[z, k, :, y * n : (y + 1) * n] for y in range(YS) for k in range(blocks)]
        value = jnp.concatenate(value, axis=1)
        at = pl.ds(z * high, high)
        a_ref[at, :] = value
        row_step(log_weight, value + v, u_ref, at)
    column_step(a_ref, u_ref, l_ref)


def next_kernel(log_weight, a_ref, parts_ref, u_ref, l_ref):
    v = row_of(parts_ref, log_weight)

    @pl.loop(0, a_ref.shape[0] // 8, step=2)
    def _(base):
        for i in range(2):
            at = pl.ds(pl.multiple_of((base + i) * 8, 8), 8)
            row_step(log_weight, a_ref[at, :] + v, u_ref, at)

    column_step(a_ref, u_ref, l_ref)


def target_kernel(
    log_weight, unit, steps, place_ref, a_ref, u_ref, parts_ref, y_ref, out_ref, f_ref, g_ref, total, mass, v_ref
):
    step = pl.program_id(0)
    lines = v_ref.shape[0] // steps

    @pl.when(step == 0)
    def _():
        total[...] = jnp.zeros_like(total)
        mass[...] = jnp.zeros_like(mass)
        u = u_ref[...]
        f_ref[...] = unit * jnp.sum(jnp.where(on_diagonal(u.shape[0]), u, 0.0), axis=0, keepdims=True)
        v_ref[...] = log_weight - joined(parts_ref[...])
        share = g_ref.shape[1]
        z = place_ref[0]
        line = v_ref[pl.ds(z // 2, 1), :]
        g_ref[...] = unit * jnp.where(lax.rem(z, 2) == 0, line[:, :share], line[:, share:])

    v = jnp.concatenate([v_ref[pl.ds(step * lines + k, 1), :] for k in range(lines)], axis=1)
    u = u_ref[:, :1]
    plan = jnp.exp2((u - log_weight + v) + a_ref[...]).astype(jnp.bfloat16)
    mass[...] += jnp.sum(plan.astype(jnp.float32), axis=1, keepdims=True)
    total[...] += jnp.dot(plan, y_ref[...], preferred_element_type=jnp.float32)

    @pl.when(step == steps - 1)
    def _():
        out_ref[...] = (total[...] / mass[...]).astype(out_ref.dtype)


def on_device(noise_rows, data_rows):
    rows, features = noise_rows.shape
    tokens = rows * lax.axis_size("noise")
    depth = lax.axis_size("dp")
    me, z = lax.axis_index("noise"), lax.axis_index("dp")
    place = jnp.stack([z, me // (XS * CORES), me // CORES % XS, me % CORES]).astype(jnp.int32)
    epsilon = 0.7 / math.sqrt(D)
    log_weight = -math.log2(tokens)
    f32 = jnp.float32

    group = XS * CORES
    y_groups = [[y * group + k for y in range(YS)] for k in range(group)]
    x_groups = [[y * group + k for k in range(group)] for y in range(YS)]

    def swap(value, groups):
        return lax.all_to_all(value, "noise", 0, 0, axis_index_groups=groups, tiled=True)

    x_near = stacked(noise_rows, swap_x(noise_rows, FIRST))
    y_near = stacked(data_rows, swap_y(data_rows, FIRST))
    x_near, y_near = lax.optimization_barrier((x_near, y_near))
    x_far, y_far = swap_x(x_near, SECOND), swap_y(y_near, SECOND)
    x_there, x_far_there, y_far, late_rows = lax.optimization_barrier(
        (to_other_core(x_near), to_other_core(x_far), y_far, data_rows)
    )
    everything = lax.all_gather(late_rows, "noise", axis=0, tiled=True)
    tall, wide = group * rows, YS * rows
    half = depth // 2
    middle = half // 2
    chunk = (tall // depth, wide)
    keep, give = pl.pallas_call(
        functools.partial(partial_kernel, LOG2E / (epsilon * D)),
        out_shape=[jax.ShapeDtypeStruct((half,) + chunk, f32)] * 2,
        in_specs=[SMEM] + [VMEM] * 6,
        out_specs=[VMEM] * 2,
        scratch_shapes=[
            pltpu.VMEM((group * rows, features), jnp.bfloat16),
            pltpu.VMEM((YS * rows, features), jnp.bfloat16),
            pltpu.VMEM((1, wide), f32),
            pltpu.VMEM((depth,) + chunk, f32),
        ],
        compiler_params=PARAMS,
    )(place, x_near, x_far, x_there, x_far_there, y_near, y_far)

    got = send_z(give, z_partner)
    own, ahead, back, ahead_rest, back_rest = pl.pallas_call(
        pair_kernel,
        out_shape=[
            jax.ShapeDtypeStruct(chunk, f32),
            jax.ShapeDtypeStruct(chunk, f32),
            jax.ShapeDtypeStruct(chunk, f32),
            jax.ShapeDtypeStruct((middle - 1,) + chunk, f32),
            jax.ShapeDtypeStruct((middle - 2,) + chunk, f32),
        ],
        in_specs=[VMEM] * 2,
        out_specs=[VMEM] * 5,
        compiler_params=PARAMS,
    )(keep, got)
    for step in range(middle):
        ahead = send_z(ahead, lambda z, c: z + 2 if c == 0 else z - 2)
        if step < middle - 1:
            ahead = ahead + ahead_rest[step]
            back = send_z(back, lambda z, c: z - 2 if c == 0 else z + 2)
            if step < middle - 2:
                back = back + back_rest[step]
    own = own + ahead + back

    few = tall // depth
    high = rows // depth
    part = pl.pallas_call(
        first_rows_kernel,
        out_shape=jax.ShapeDtypeStruct((group, high, wide + rows), f32),
        in_specs=[VMEM],
        out_specs=VMEM,
        scratch_shapes=[pltpu.VMEM((1, 1, few), f32)],
        compiler_params=PARAMS,
    )(own)
    part = swap(part, x_groups)
    everything, pieces = lax.optimization_barrier((everything, part[:, :, :wide]))
    gathered = lax.all_gather(pieces, "dp")
    z_groups = [
        [((y * group) + k) * depth + d for y in range(YS) for d in range(depth)] for k in range(group)
    ]
    row_shape = jax.ShapeDtypeStruct((group, 1, few), f32)
    for step in range(EARLY):
        if step > 0:
            part = pl.pallas_call(
                functools.partial(rows_kernel, log_weight),
                out_shape=row_shape,
                in_specs=[VMEM] * 2,
                out_specs=VMEM,
                compiler_params=PARAMS,
            )(own, part)
            part = swap(part, x_groups)
        part = pl.pallas_call(
            functools.partial(columns_kernel, log_weight, 0 if step > 0 else wide),
            out_shape=jax.ShapeDtypeStruct((YS * depth, YS, rows), f32),
            in_specs=[VMEM] * 2,
            out_specs=VMEM,
            scratch_shapes=[pltpu.VMEM((few, wide), f32)],
            compiler_params=PARAMS,
        )(own, part)
        part = lax.all_to_all(
            part, ("noise", "dp"), 0, 0, axis_index_groups=z_groups, tiled=True
        )
    part = pl.pallas_call(
        join_kernel,
        out_shape=jax.ShapeDtypeStruct((group, YS, rows), f32),
        in_specs=[VMEM],
        out_specs=VMEM,
        compiler_params=PARAMS,
    )(part)
    part = swap(part, x_groups)

    copies = lax.axis_size("noise")
    lines = 8
    block = tokens // lines
    u_shape = jax.ShapeDtypeStruct((rows, rows), f32)
    l_shape = jax.ShapeDtypeStruct((copies, lines, block), f32)
    for step in range(EARLY, ITERS):
        if step == EARLY:
            a, u, part = pl.pallas_call(
                functools.partial(whole_rows_kernel, log_weight),
                out_shape=[jax.ShapeDtypeStruct((rows, tokens), f32), u_shape, l_shape],
                in_specs=[pl.BlockSpec(memory_space=pl.ANY), VMEM],
                out_specs=[VMEM] * 3,
                scratch_shapes=[
                    pltpu.VMEM((depth, group, high, wide), f32),
                    pltpu.SemaphoreType.DMA((depth,)),
                ],
                compiler_params=PARAMS,
            )(gathered, part)
        else:
            u, part = pl.pallas_call(
                functools.partial(next_kernel, log_weight),
                out_shape=[u_shape, l_shape],
                in_specs=[VMEM] * 2,
                out_specs=[VMEM] * 2,
                compiler_params=PARAMS,
            )(a, part)
        part = lax.all_to_all(part, "noise", 0, 0, tiled=True)

    steps = 4
    targets, noise_potential, data_potential = pl.pallas_call(
        functools.partial(target_kernel, log_weight, epsilon / LOG2E, steps),
        grid=(steps,),
        out_shape=[
            jax.ShapeDtypeStruct((rows, features), jnp.bfloat16),
            jax.ShapeDtypeStruct((1, rows), f32),
            jax.ShapeDtypeStruct((1, block // 2), f32),
        ],
        in_specs=[
            SMEM,
            pl.BlockSpec((rows, tokens // steps), lambda k: (0, k)),
            pl.BlockSpec((rows, rows), lambda k: (0, 0)),
            pl.BlockSpec((copies, lines, block), lambda k: (0, 0, 0)),
            pl.BlockSpec((tokens // steps, features), lambda k: (k, 0)),
        ],
        out_specs=[
            pl.BlockSpec((rows, features), lambda k: (0, 0)),
            pl.BlockSpec((1, rows), lambda k: (0, 0)),
            pl.BlockSpec((1, block // 2), lambda k: (0, 0)),
        ],
        scratch_shapes=[
            pltpu.VMEM((rows, features), f32),
            pltpu.VMEM((rows, 1), f32),
            pltpu.VMEM((lines, block), f32),
        ],
        compiler_params=PARAMS,
    )(place, a, u, part, everything)
    return targets, noise_potential.reshape(rows), data_potential.reshape(block // 2)


def solution(mesh):
    return jax.shard_map(
        on_device,
        mesh=mesh,
        in_specs=(P("noise", "dp"), P("noise", "dp")),
        out_specs=(P("noise", "dp"), P("noise"), P("dp")),
        check_vma=False,
    )
```

```python
import functools
import math

import jax
import jax.numpy as jnp
from jax import lax
from jax.experimental import pallas as pl
from jax.experimental.pallas import tpu as pltpu
from jax.sharding import PartitionSpec as P

D = 16384
ITERS = 4
EARLY = 2
YS, XS, CORES = 4, 4, 2
LOG2E = math.log2(math.e)
VMEM = pl.BlockSpec(memory_space=pltpu.VMEM)
SMEM = pl.BlockSpec(memory_space=pltpu.SMEM)
PARAMS = pltpu.CompilerParams(vmem_limit_bytes=48 * 1024 * 1024)


def noise_pairs(target):
    pairs = []
    for y in range(YS):
        for x in range(XS):
            for c in range(CORES):
                to_y, to_x, to_c = target(y, x, c)
                pairs.append(((y * XS + x) * CORES + c, (to_y * XS + to_x) * CORES + to_c))
    return pairs


def to_other_core(value):
    return lax.ppermute(value, "noise", noise_pairs(lambda y, x, c: (y, x, 1 - c)))


FIRST, SECOND, BOTH = (1, 3), (3, 1), 2
PLACES = ((0, 0), FIRST, SECOND, (BOTH, BOTH))


def swap_x(value, by):
    return lax.ppermute(value, "noise", noise_pairs(lambda y, x, c: (y, x ^ by[c], c)))


def swap_y(value, by):
    return lax.ppermute(value, "noise", noise_pairs(lambda y, x, c: (y ^ by[c], x, c)))


def stacked(block, received):
    rows, features = block.shape
    both = lax.dynamic_update_slice(jnp.zeros((2 * rows, features), block.dtype), block, (0, 0))
    both = lax.optimization_barrier(both)
    return lax.dynamic_update_slice(both, received, (rows, 0))


def send_z(value, target):
    size = lax.axis_size("dp")
    pairs = []
    for n in range(YS * XS * CORES):
        pairs += [(n * size + z, n * size + target(z, n % CORES) % size) for z in range(size)]
    return lax.ppermute(value, ("noise", "dp"), pairs)


def z_partner(z, c):
    return z ^ 1 if c == 0 else z + 1 if z % 2 else z - 1


def squares_row(block):
    wide = block.astype(jnp.float32)
    column = jnp.sum(wide * wide, axis=1, keepdims=True)
    n = block.shape[0]
    row_at = lax.broadcasted_iota(jnp.int32, (n, n), 0)
    column_at = lax.broadcasted_iota(jnp.int32, (n, n), 1)
    return jnp.sum(jnp.where(row_at == column_at, column, 0.0), axis=0, keepdims=True)


def partial_kernel(scale, place_ref, *refs):
    here, there, ys = refs[:2], refs[2:4], refs[4:6]
    keep, give, x_all, y_all, y_squares, chunks = refs[6:]
    rows = here[0].shape[0] // 2
    depth = chunks.shape[0]
    high = rows // depth
    z, y, x, c = place_ref[0], place_ref[1], place_ref[2], place_ref[3]
    for k, (first, second) in enumerate(PLACES):
        block = slice(k % 2 * rows, (k % 2 + 1) * rows)
        mine, other = jnp.where(c == 0, first, second), jnp.where(c == 0, second, first)
        at = pl.multiple_of((lax.bitwise_xor(x, mine) * CORES + c) * rows, rows)
        x_all[pl.ds(at, rows), :] = here[k // 2][block, :]
        at = pl.multiple_of((lax.bitwise_xor(x, other) * CORES + 1 - c) * rows, rows)
        x_all[pl.ds(at, rows), :] = there[k // 2][block, :]
        at = pl.multiple_of(lax.bitwise_xor(y, mine) * rows, rows)
        y_all[pl.ds(at, rows), :] = ys[k // 2][block, :]
    for k in range(YS):
        block = slice(k * rows, (k + 1) * rows)
        y_squares[:, block] = scale * squares_row(y_all[block, :])
    up = jnp.where(c == 0, lax.rem(z, 2) == 0, lax.rem(z, 2) == 1)
    partner = lax.rem(z + jnp.where(up, 1, depth - 1), depth)
    places = []
    for t in range(depth):
        same = lax.rem(z + t, 2) == 0
        base = jnp.where(same, z, partner)
        ahead = jnp.where(c == 0, lax.rem(t + depth - base, depth), lax.rem(base + depth - t, depth))
        places.append(ahead // 2 + jnp.where(same, 0, depth // 2))
    tall = 4 * rows
    for k in range(XS * CORES // 4):
        value = x_all[k * tall : (k + 1) * tall, :]
        wide = value.astype(jnp.float32)
        x_squares = scale * jnp.sum(wide * wide, axis=1, keepdims=True)
        cross = lax.dot_general(
            value, y_all[...], (((1,), (1,)), ((), ())), preferred_element_type=jnp.float32
        )
        value = (2.0 * scale) * cross - x_squares - y_squares[...]
        for i in range(4 * depth):
            block = k * 4 + i // depth
            chunks[places[i % depth], block * high : (block + 1) * high, :] = value[i * high : (i + 1) * high]
    for k in range(depth // 2):
        keep[k] = chunks[k]
        give[k] = chunks[depth // 2 + k]


def pair_kernel(keep, got, own, ahead, back, ahead_rest, back_rest):
    own[...] = keep[0] + got[0]
    middle = keep.shape[0] // 2
    ahead[...] = keep[middle] + got[middle]
    back[...] = keep[middle + 1] + got[middle + 1]
    for k in range(1, middle):
        ahead_rest[middle - 1 - k] = keep[k] + got[k]
    for k in range(middle + 2, keep.shape[0]):
        back_rest[k - middle - 2] = keep[k] + got[k]


def joined(parts):
    peak = jnp.max(parts, axis=0)
    return peak + jnp.log(jnp.sum(jnp.exp2(parts - peak), axis=0)) * LOG2E


def on_diagonal(n):
    rows = lax.broadcasted_iota(jnp.int32, (n, n), 0)
    return rows == lax.broadcasted_iota(jnp.int32, (n, n), 1)


def column_of(u, k):
    n = u.shape[1]
    return jnp.sum(jnp.where(on_diagonal(n), u[k : k + 1], 0.0), axis=1, keepdims=True)


def row_of(parts_ref, log_weight):
    v = log_weight - joined(parts_ref[...])
    return jnp.concatenate([v[k : k + 1] for k in range(v.shape[0])], axis=1)


def copy_out(out_ref):
    whole = out_ref[0]
    for k in range(1, out_ref.shape[0]):
        out_ref[k] = whole


def row_sums(a_ref, v, out_ref, n):
    for k in range(a_ref.shape[0] // n):
        value = a_ref[k * n : (k + 1) * n, :]
        if v is not None:
            value = value + v
        peak = jnp.max(value, axis=1, keepdims=True)
        total = jnp.sum(jnp.exp2(value - peak), axis=1, keepdims=True)
        part = peak + jnp.log(total) * LOG2E
        out_ref[0, k : k + 1, :] = jnp.sum(jnp.where(on_diagonal(n), part, 0.0), axis=0, keepdims=True)
    copy_out(out_ref)


def first_rows_kernel(a_ref, out_ref, sums):
    copies, high, width = out_ref.shape
    n, columns = a_ref.shape
    row_sums(a_ref, None, sums, n)
    for k in range(copies):
        out_ref[k, :, :columns] = a_ref[k * high : (k + 1) * high, :]
        out_ref[k, :, columns:] = jnp.zeros((high, width - columns), jnp.float32)
        out_ref[k, :1, columns : columns + n] = sums[0]


def rows_kernel(log_weight, a_ref, parts_ref, out_ref):
    row_sums(a_ref, row_of(parts_ref, log_weight), out_ref, out_ref.shape[2])


def columns_kernel(log_weight, beside, a_ref, parts_ref, out_ref, shifted):
    parts = parts_ref[:, :1, beside : beside + a_ref.shape[0]]
    u = log_weight - joined(parts)
    blocks, n = u.shape
    width = a_ref.shape[1]
    peak = None
    for k in range(blocks):
        value = a_ref[k * n : (k + 1) * n, :] + column_of(u, k)
        shifted[k * n : (k + 1) * n, :] = value
        block_peak = jnp.max(value.reshape(n // 8, 8, width), axis=0)
        peak = block_peak if peak is None else jnp.maximum(peak, block_peak)
    peak = jnp.max(peak, axis=0, keepdims=True)
    total = jnp.zeros((8, width), jnp.float32)
    for k in range(blocks):
        value = jnp.exp2(shifted[k * n : (k + 1) * n, :] - peak)
        total = total + jnp.sum(value.reshape(n // 8, 8, width), axis=0)
    part = peak + jnp.log(jnp.sum(total, axis=0, keepdims=True)) * LOG2E
    lanes = out_ref.shape[2]
    for k in range(out_ref.shape[1]):
        out_ref[0, k : k + 1, :] = part[:, k * lanes : (k + 1) * lanes]
    copy_out(out_ref)


def join_kernel(parts_ref, out_ref):
    out_ref[0] = joined(parts_ref[...])
    copy_out(out_ref)


def half_steps(log_weight, a_ref, v, u_ref, l_ref):
    rows, columns = a_ref.shape
    lanes = u_ref.shape[1]
    copies, high, width = l_ref.shape

    @pl.loop(0, rows // 8, step=2)
    def _(base):
        for i in range(2):
            at = pl.ds(pl.multiple_of((base + i) * 8, 8), 8)
            value = a_ref[at, :] + v
            peak = jnp.max(value, axis=1, keepdims=True)
            total = jnp.sum(jnp.exp2(value - peak), axis=1, keepdims=True)
            u = log_weight - (peak + jnp.log(total) * LOG2E)
            u_ref[at, :] = jnp.broadcast_to(u, (8, lanes))

    for k in range(high):
        for i in range(width // lanes):
            at = pl.ds(k * width + i * lanes, lanes)
            value = a_ref[:, at] + u_ref[...]
            peak = jnp.max(value, axis=0, keepdims=True)
            total = jnp.sum(jnp.exp2(value - peak), axis=0, keepdims=True)
            l_ref[0, k : k + 1, i * lanes : (i + 1) * lanes] = peak + jnp.log(total) * LOG2E
    whole = l_ref[0]
    for k in range(1, copies):
        l_ref[k] = whole


def whole_rows_kernel(log_weight, pieces_ref, parts_ref, a_ref, u_ref, l_ref):
    depth, blocks, high, width = pieces_ref.shape
    n = width // YS
    v = log_weight - parts_ref[...]
    for z in range(depth):
        for y in range(YS):
            for k in range(blocks):
                at = (y * blocks + k) * n
                a_ref[z * high : (z + 1) * high, at : at + n] = pieces_ref[z, k, :, y * n : (y + 1) * n]
    v = jnp.concatenate([v[k, y : y + 1] for y in range(YS) for k in range(blocks)], axis=1)
    half_steps(log_weight, a_ref, v, u_ref, l_ref)


def next_kernel(log_weight, a_ref, parts_ref, u_ref, l_ref):
    v = log_weight - joined(parts_ref[...])
    v = jnp.concatenate([v[k : k + 1] for k in range(v.shape[0])], axis=1)
    half_steps(log_weight, a_ref, v, u_ref, l_ref)


def target_kernel(
    log_weight, unit, steps, place_ref, a_ref, u_ref, parts_ref, y_ref, out_ref, f_ref, g_ref, total, mass, v_ref
):
    step = pl.program_id(0)
    lines = v_ref.shape[0] // steps

    @pl.when(step == 0)
    def _():
        total[...] = jnp.zeros_like(total)
        mass[...] = jnp.zeros_like(mass)
        u = u_ref[...]
        f_ref[...] = unit * jnp.sum(jnp.where(on_diagonal(u.shape[0]), u, 0.0), axis=0, keepdims=True)
        v_ref[...] = log_weight - joined(parts_ref[...])
        share = g_ref.shape[1]
        z = place_ref[0]
        line = v_ref[pl.ds(z // 2, 1), :]
        g_ref[...] = unit * jnp.where(lax.rem(z, 2) == 0, line[:, :share], line[:, share:])

    v = jnp.concatenate([v_ref[pl.ds(step * lines + k, 1), :] for k in range(lines)], axis=1)
    u = u_ref[:, :1]
    plan = jnp.exp2((u - log_weight + v) + a_ref[...]).astype(jnp.bfloat16)
    mass[...] += jnp.sum(plan.astype(jnp.float32), axis=1, keepdims=True)
    total[...] += jnp.dot(plan, y_ref[...], preferred_element_type=jnp.float32)

    @pl.when(step == steps - 1)
    def _():
        out_ref[...] = (total[...] / mass[...]).astype(out_ref.dtype)


def on_device(noise_rows, data_rows):
    rows, features = noise_rows.shape
    tokens = rows * lax.axis_size("noise")
    depth = lax.axis_size("dp")
    me, z = lax.axis_index("noise"), lax.axis_index("dp")
    place = jnp.stack([z, me // (XS * CORES), me // CORES % XS, me % CORES]).astype(jnp.int32)
    epsilon = 0.7 / math.sqrt(D)
    log_weight = -math.log2(tokens)
    f32 = jnp.float32

    group = XS * CORES
    y_groups = [[y * group + k for y in range(YS)] for k in range(group)]
    x_groups = [[y * group + k for k in range(group)] for y in range(YS)]

    def swap(value, groups):
        return lax.all_to_all(value, "noise", 0, 0, axis_index_groups=groups, tiled=True)

    x_near = stacked(noise_rows, swap_x(noise_rows, FIRST))
    y_near = stacked(data_rows, swap_y(data_rows, FIRST))
    x_near, y_near = lax.optimization_barrier((x_near, y_near))
    x_far, y_far = swap_x(x_near, SECOND), swap_y(y_near, SECOND)
    x_there, x_far_there, y_far, late_rows = lax.optimization_barrier(
        (to_other_core(x_near), to_other_core(x_far), y_far, data_rows)
    )
    everything = lax.all_gather(late_rows, "noise", axis=0, tiled=True)
    tall, wide = group * rows, YS * rows
    half = depth // 2
    middle = half // 2
    chunk = (tall // depth, wide)
    keep, give = pl.pallas_call(
        functools.partial(partial_kernel, LOG2E / (epsilon * D)),
        out_shape=[jax.ShapeDtypeStruct((half,) + chunk, f32)] * 2,
        in_specs=[SMEM] + [VMEM] * 6,
        out_specs=[VMEM] * 2,
        scratch_shapes=[
            pltpu.VMEM((group * rows, features), jnp.bfloat16),
            pltpu.VMEM((YS * rows, features), jnp.bfloat16),
            pltpu.VMEM((1, wide), f32),
            pltpu.VMEM((depth,) + chunk, f32),
        ],
        compiler_params=PARAMS,
    )(place, x_near, x_far, x_there, x_far_there, y_near, y_far)

    got = send_z(give, z_partner)
    own, ahead, back, ahead_rest, back_rest = pl.pallas_call(
        pair_kernel,
        out_shape=[
            jax.ShapeDtypeStruct(chunk, f32),
            jax.ShapeDtypeStruct(chunk, f32),
            jax.ShapeDtypeStruct(chunk, f32),
            jax.ShapeDtypeStruct((middle - 1,) + chunk, f32),
            jax.ShapeDtypeStruct((middle - 2,) + chunk, f32),
        ],
        in_specs=[VMEM] * 2,
        out_specs=[VMEM] * 5,
        compiler_params=PARAMS,
    )(keep, got)
    for step in range(middle):
        ahead = send_z(ahead, lambda z, c: z + 2 if c == 0 else z - 2)
        if step < middle - 1:
            ahead = ahead + ahead_rest[step]
            back = send_z(back, lambda z, c: z - 2 if c == 0 else z + 2)
            if step < middle - 2:
                back = back + back_rest[step]
    own = own + ahead + back

    few = tall // depth
    high = rows // depth
    part = pl.pallas_call(
        first_rows_kernel,
        out_shape=jax.ShapeDtypeStruct((group, high, wide + rows), f32),
        in_specs=[VMEM],
        out_specs=VMEM,
        scratch_shapes=[pltpu.VMEM((1, 1, few), f32)],
        compiler_params=PARAMS,
    )(own)
    part = swap(part, x_groups)
    everything, pieces = lax.optimization_barrier((everything, part[:, :, :wide]))
    gathered = lax.all_gather(pieces, "dp")
    z_groups = [
        [((y * group) + k) * depth + d for y in range(YS) for d in range(depth)] for k in range(group)
    ]
    row_shape = jax.ShapeDtypeStruct((group, 1, few), f32)
    for step in range(EARLY):
        if step > 0:
            part = pl.pallas_call(
                functools.partial(rows_kernel, log_weight),
                out_shape=row_shape,
                in_specs=[VMEM] * 2,
                out_specs=VMEM,
                compiler_params=PARAMS,
            )(own, part)
            part = swap(part, x_groups)
        part = pl.pallas_call(
            functools.partial(columns_kernel, log_weight, 0 if step > 0 else wide),
            out_shape=jax.ShapeDtypeStruct((YS * depth, YS, rows), f32),
            in_specs=[VMEM] * 2,
            out_specs=VMEM,
            scratch_shapes=[pltpu.VMEM((few, wide), f32)],
            compiler_params=PARAMS,
        )(own, part)
        part = lax.all_to_all(
            part, ("noise", "dp"), 0, 0, axis_index_groups=z_groups, tiled=True
        )
    part = pl.pallas_call(
        join_kernel,
        out_shape=jax.ShapeDtypeStruct((group, YS, rows), f32),
        in_specs=[VMEM],
        out_specs=VMEM,
        compiler_params=PARAMS,
    )(part)
    part = swap(part, x_groups)

    copies = lax.axis_size("noise")
    lines = 8
    block = tokens // lines
    u_shape = jax.ShapeDtypeStruct((rows, rows), f32)
    l_shape = jax.ShapeDtypeStruct((copies, lines, block), f32)
    for step in range(EARLY, ITERS):
        if step == EARLY:
            a, u, part = pl.pallas_call(
                functools.partial(whole_rows_kernel, log_weight),
                out_shape=[jax.ShapeDtypeStruct((rows, tokens), f32), u_shape, l_shape],
                in_specs=[VMEM] * 2,
                out_specs=[VMEM] * 3,
                compiler_params=PARAMS,
            )(gathered, part)
        else:
            u, part = pl.pallas_call(
                functools.partial(next_kernel, log_weight),
                out_shape=[u_shape, l_shape],
                in_specs=[VMEM] * 2,
                out_specs=[VMEM] * 2,
                compiler_params=PARAMS,
            )(a, part)
        part = lax.all_to_all(part, "noise", 0, 0, tiled=True)

    steps = 4
    targets, noise_potential, data_potential = pl.pallas_call(
        functools.partial(target_kernel, log_weight, epsilon / LOG2E, steps),
        grid=(steps,),
        out_shape=[
            jax.ShapeDtypeStruct((rows, features), jnp.bfloat16),
            jax.ShapeDtypeStruct((1, rows), f32),
            jax.ShapeDtypeStruct((1, block // 2), f32),
        ],
        in_specs=[
            SMEM,
            pl.BlockSpec((rows, tokens // steps), lambda k: (0, k)),
            pl.BlockSpec((rows, rows), lambda k: (0, 0)),
            pl.BlockSpec((copies, lines, block), lambda k: (0, 0, 0)),
            pl.BlockSpec((tokens // steps, features), lambda k: (k, 0)),
        ],
        out_specs=[
            pl.BlockSpec((rows, features), lambda k: (0, 0)),
            pl.BlockSpec((1, rows), lambda k: (0, 0)),
            pl.BlockSpec((1, block // 2), lambda k: (0, 0)),
        ],
        scratch_shapes=[
            pltpu.VMEM((rows, features), f32),
            pltpu.VMEM((rows, 1), f32),
            pltpu.VMEM((lines, block), f32),
        ],
        compiler_params=PARAMS,
    )(place, a, u, part, everything)
    return targets, noise_potential.reshape(rows), data_potential.reshape(block // 2)


def solution(mesh):
    return jax.shard_map(
        on_device,
        mesh=mesh,
        in_specs=(P("noise", "dp"), P("noise", "dp")),
        out_specs=(P("noise", "dp"), P("noise"), P("dp")),
        check_vma=False,
    )
```

```python
import functools
import math

import jax
import jax.numpy as jnp
from jax import lax
from jax.experimental import pallas as pl
from jax.experimental.pallas import tpu as pltpu
from jax.sharding import PartitionSpec as P

D = 16384
ITERS = 4
EARLY = 2
YS, XS, CORES = 4, 4, 2
LOG2E = math.log2(math.e)
VMEM = pl.BlockSpec(memory_space=pltpu.VMEM)
SMEM = pl.BlockSpec(memory_space=pltpu.SMEM)
PARAMS = pltpu.CompilerParams(vmem_limit_bytes=48 * 1024 * 1024)


def noise_pairs(target):
    pairs = []
    for y in range(YS):
        for x in range(XS):
            for c in range(CORES):
                to_y, to_x, to_c = target(y, x, c)
                pairs.append(((y * XS + x) * CORES + c, (to_y * XS + to_x) * CORES + to_c))
    return pairs


def to_other_core(value):
    return lax.ppermute(value, "noise", noise_pairs(lambda y, x, c: (y, x, 1 - c)))


FIRST, SECOND, BOTH = (1, 3), (3, 1), 2
PLACES = ((0, 0), FIRST, SECOND, (BOTH, BOTH))


ORDERS = ((4, 5, 3, 6), (2, 7, 1, 0))


def swap_x(value, by):
    return lax.ppermute(value, "noise", noise_pairs(lambda y, x, c: (y, x ^ by[c], c)))


def swap_y(value, by):
    return lax.ppermute(value, "noise", noise_pairs(lambda y, x, c: (y ^ by[c], x, c)))


def stacked(block, received):
    rows, features = block.shape
    both = lax.dynamic_update_slice(jnp.zeros((2 * rows, features), block.dtype), block, (0, 0))
    both = lax.optimization_barrier(both)
    return lax.dynamic_update_slice(both, received, (rows, 0))


def send_z(value, target):
    size = lax.axis_size("dp")
    pairs = []
    for n in range(YS * XS * CORES):
        pairs += [(n * size + z, n * size + target(z, n % CORES) % size) for z in range(size)]
    return lax.ppermute(value, ("noise", "dp"), pairs)


def z_partner(z, c):
    return z ^ 1 if c == 0 else z + 1 if z % 2 else z - 1


def squares_row(block):
    wide = block.astype(jnp.float32)
    column = jnp.sum(wide * wide, axis=1, keepdims=True)
    n = block.shape[0]
    row_at = lax.broadcasted_iota(jnp.int32, (n, n), 0)
    column_at = lax.broadcasted_iota(jnp.int32, (n, n), 1)
    return jnp.sum(jnp.where(row_at == column_at, column, 0.0), axis=0, keepdims=True)


def partial_kernel(scale, place_ref, *refs):
    here, there, ys = refs[:2], refs[2:4], refs[4:6]
    keep, give, (x_all, y_all, y_squares, chunks) = refs[6:8], refs[8:10], refs[10:]
    rows = here[0].shape[0] // 2
    depth = chunks.shape[0]
    high = rows // depth
    z, y, x, c = place_ref[0], place_ref[1], place_ref[2], place_ref[3]
    for k, (first, second) in enumerate(PLACES):
        block = slice(k % 2 * rows, (k % 2 + 1) * rows)
        mine, other = jnp.where(c == 0, first, second), jnp.where(c == 0, second, first)
        at = pl.multiple_of((lax.bitwise_xor(x, mine) * CORES + c) * rows, rows)
        x_all[pl.ds(at, rows), :] = here[k // 2][block, :]
        at = pl.multiple_of((lax.bitwise_xor(x, other) * CORES + 1 - c) * rows, rows)
        x_all[pl.ds(at, rows), :] = there[k // 2][block, :]
        at = pl.multiple_of(lax.bitwise_xor(y, mine) * rows, rows)
        y_all[pl.ds(at, rows), :] = ys[k // 2][block, :]
    for k in range(YS):
        block = slice(k * rows, (k + 1) * rows)
        y_squares[:, block] = scale * squares_row(y_all[block, :])
    up = jnp.where(c == 0, lax.rem(z, 2) == 0, lax.rem(z, 2) == 1)
    partner = lax.rem(z + jnp.where(up, 1, depth - 1), depth)
    places = []
    for t in range(depth):
        same = lax.rem(z + t, 2) == 0
        base = jnp.where(same, z, partner)
        ahead = jnp.where(c == 0, lax.rem(t + depth - base, depth), lax.rem(base + depth - t, depth))
        places.append(ahead // 2 + jnp.where(same, 0, depth // 2))
    tall = 4 * rows
    for k in range(XS * CORES // 4):
        value = x_all[k * tall : (k + 1) * tall, :]
        wide = value.astype(jnp.float32)
        x_squares = scale * jnp.sum(wide * wide, axis=1, keepdims=True)
        cross = lax.dot_general(
            value, y_all[...], (((1,), (1,)), ((), ())), preferred_element_type=jnp.float32
        )
        value = (2.0 * scale) * cross - x_squares - y_squares[...]
        for i in range(4 * depth):
            block = k * 4 + i // depth
            chunks[places[i % depth], block * high : (block + 1) * high, :] = value[i * high : (i + 1) * high]
    for part, order in enumerate(ORDERS):
        for i, k in enumerate(order):
            keep[part][i] = chunks[k]
            give[part][i] = chunks[depth // 2 + k]


def pair_kernel(keep, got, *outs):
    for k, out in enumerate(outs):
        out[...] = keep[k] + got[k]


def joined(parts):
    peak = jnp.max(parts, axis=0)
    return peak + jnp.log(jnp.sum(jnp.exp2(parts - peak), axis=0)) * LOG2E


def on_diagonal(n):
    rows = lax.broadcasted_iota(jnp.int32, (n, n), 0)
    return rows == lax.broadcasted_iota(jnp.int32, (n, n), 1)


def column_of(u, k):
    n = u.shape[1]
    return jnp.sum(jnp.where(on_diagonal(n), u[k : k + 1], 0.0), axis=1, keepdims=True)


def row_of(parts_ref, log_weight):
    v = log_weight - joined(parts_ref[...])
    return jnp.concatenate([v[k : k + 1] for k in range(v.shape[0])], axis=1)


def copy_out(out_ref):
    whole = out_ref[0]
    for k in range(1, out_ref.shape[0]):
        out_ref[k] = whole


def row_sums(a_ref, v, out_ref, n):
    for k in range(a_ref.shape[0] // n):
        value = a_ref[k * n : (k + 1) * n, :]
        if v is not None:
            value = value + v
        peak = jnp.max(value, axis=1, keepdims=True)
        total = jnp.sum(jnp.exp2(value - peak), axis=1, keepdims=True)
        part = peak + jnp.log(total) * LOG2E
        out_ref[0, k : k + 1, :] = jnp.sum(jnp.where(on_diagonal(n), part, 0.0), axis=0, keepdims=True)
    copy_out(out_ref)


def first_rows_kernel(a_ref, out_ref, sums):
    copies, high, width = out_ref.shape
    n, columns = a_ref.shape
    row_sums(a_ref, None, sums, n)
    for k in range(copies):
        out_ref[k, :, :columns] = a_ref[k * high : (k + 1) * high, :]
        out_ref[k, :, columns:] = jnp.zeros((high, width - columns), jnp.float32)
        out_ref[k, :1, columns : columns + n] = sums[0]


def rows_kernel(log_weight, a_ref, parts_ref, out_ref):
    row_sums(a_ref, row_of(parts_ref, log_weight), out_ref, out_ref.shape[2])


def columns_kernel(log_weight, beside, a_ref, parts_ref, out_ref, shifted):
    parts = parts_ref[:, :1, beside : beside + a_ref.shape[0]]
    u = log_weight - joined(parts)
    blocks, n = u.shape
    width = a_ref.shape[1]
    peak = None
    for k in range(blocks):
        value = a_ref[k * n : (k + 1) * n, :] + column_of(u, k)
        shifted[k * n : (k + 1) * n, :] = value
        block_peak = jnp.max(value.reshape(n // 8, 8, width), axis=0)
        peak = block_peak if peak is None else jnp.maximum(peak, block_peak)
    peak = jnp.max(peak, axis=0, keepdims=True)
    total = jnp.zeros((8, width), jnp.float32)
    for k in range(blocks):
        value = jnp.exp2(shifted[k * n : (k + 1) * n, :] - peak)
        total = total + jnp.sum(value.reshape(n // 8, 8, width), axis=0)
    part = peak + jnp.log(jnp.sum(total, axis=0, keepdims=True)) * LOG2E
    lanes = out_ref.shape[2]
    for k in range(out_ref.shape[1]):
        out_ref[0, k : k + 1, :] = part[:, k * lanes : (k + 1) * lanes]
    copy_out(out_ref)


def join_kernel(parts_ref, out_ref):
    out_ref[0] = joined(parts_ref[...])
    copy_out(out_ref)


def half_steps(log_weight, a_ref, v, u_ref, l_ref):
    rows, columns = a_ref.shape
    lanes = u_ref.shape[1]
    copies, high, width = l_ref.shape

    @pl.loop(0, rows // 8, step=2)
    def _(base):
        for i in range(2):
            at = pl.ds(pl.multiple_of((base + i) * 8, 8), 8)
            value = a_ref[at, :] + v
            peak = jnp.max(value, axis=1, keepdims=True)
            total = jnp.sum(jnp.exp2(value - peak), axis=1, keepdims=True)
            u = log_weight - (peak + jnp.log(total) * LOG2E)
            u_ref[at, :] = jnp.broadcast_to(u, (8, lanes))

    for k in range(high):
        for i in range(width // lanes):
            at = pl.ds(k * width + i * lanes, lanes)
            value = a_ref[:, at] + u_ref[...]
            peak = jnp.max(value, axis=0, keepdims=True)
            total = jnp.sum(jnp.exp2(value - peak), axis=0, keepdims=True)
            l_ref[0, k : k + 1, i * lanes : (i + 1) * lanes] = peak + jnp.log(total) * LOG2E
    whole = l_ref[0]
    for k in range(1, copies):
        l_ref[k] = whole


def whole_rows_kernel(log_weight, pieces_ref, parts_ref, a_ref, u_ref, l_ref):
    depth, blocks, high, width = pieces_ref.shape
    n = width // YS
    v = log_weight - parts_ref[...]
    for z in range(depth):
        for y in range(YS):
            for k in range(blocks):
                at = (y * blocks + k) * n
                a_ref[z * high : (z + 1) * high, at : at + n] = pieces_ref[z, k, :, y * n : (y + 1) * n]
    v = jnp.concatenate([v[k, y : y + 1] for y in range(YS) for k in range(blocks)], axis=1)
    half_steps(log_weight, a_ref, v, u_ref, l_ref)


def next_kernel(log_weight, a_ref, parts_ref, u_ref, l_ref):
    v = log_weight - joined(parts_ref[...])
    v = jnp.concatenate([v[k : k + 1] for k in range(v.shape[0])], axis=1)
    half_steps(log_weight, a_ref, v, u_ref, l_ref)


def target_kernel(
    log_weight, unit, steps, place_ref, a_ref, u_ref, parts_ref, y_ref, out_ref, f_ref, g_ref, total, mass, v_ref
):
    step = pl.program_id(0)
    lines = v_ref.shape[0] // steps

    @pl.when(step == 0)
    def _():
        total[...] = jnp.zeros_like(total)
        mass[...] = jnp.zeros_like(mass)
        u = u_ref[...]
        f_ref[...] = unit * jnp.sum(jnp.where(on_diagonal(u.shape[0]), u, 0.0), axis=0, keepdims=True)
        v_ref[...] = log_weight - joined(parts_ref[...])
        share = g_ref.shape[1]
        z = place_ref[0]
        line = v_ref[pl.ds(z // 2, 1), :]
        g_ref[...] = unit * jnp.where(lax.rem(z, 2) == 0, line[:, :share], line[:, share:])

    v = jnp.concatenate([v_ref[pl.ds(step * lines + k, 1), :] for k in range(lines)], axis=1)
    u = u_ref[:, :1]
    plan = jnp.exp2((u - log_weight + v) + a_ref[...]).astype(jnp.bfloat16)
    mass[...] += jnp.sum(plan.astype(jnp.float32), axis=1, keepdims=True)
    total[...] += jnp.dot(plan, y_ref[...], preferred_element_type=jnp.float32)

    @pl.when(step == steps - 1)
    def _():
        out_ref[...] = (total[...] / mass[...]).astype(out_ref.dtype)


def on_device(noise_rows, data_rows):
    rows, features = noise_rows.shape
    tokens = rows * lax.axis_size("noise")
    depth = lax.axis_size("dp")
    me, z = lax.axis_index("noise"), lax.axis_index("dp")
    place = jnp.stack([z, me // (XS * CORES), me // CORES % XS, me % CORES]).astype(jnp.int32)
    epsilon = 0.7 / math.sqrt(D)
    log_weight = -math.log2(tokens)
    f32 = jnp.float32

    group = XS * CORES
    y_groups = [[y * group + k for y in range(YS)] for k in range(group)]
    x_groups = [[y * group + k for k in range(group)] for y in range(YS)]

    def swap(value, groups):
        return lax.all_to_all(value, "noise", 0, 0, axis_index_groups=groups, tiled=True)

    x_near = stacked(noise_rows, swap_x(noise_rows, FIRST))
    y_near = stacked(data_rows, swap_y(data_rows, FIRST))
    x_near, y_near = lax.optimization_barrier((x_near, y_near))
    x_far, y_far = swap_x(x_near, SECOND), swap_y(y_near, SECOND)
    x_there, x_far_there, y_far, late_rows = lax.optimization_barrier(
        (to_other_core(x_near), to_other_core(x_far), y_far, data_rows)
    )
    everything = lax.all_gather(late_rows, "noise", axis=0, tiled=True)
    tall, wide = group * rows, YS * rows
    half = depth // 2
    middle = half // 2
    chunk = (tall // depth, wide)
    *keep, give, give_later = pl.pallas_call(
        functools.partial(partial_kernel, LOG2E / (epsilon * D)),
        out_shape=[jax.ShapeDtypeStruct((half // 2,) + chunk, f32)] * 4,
        in_specs=[SMEM] + [VMEM] * 6,
        out_specs=[VMEM] * 4,
        scratch_shapes=[
            pltpu.VMEM((group * rows, features), jnp.bfloat16),
            pltpu.VMEM((YS * rows, features), jnp.bfloat16),
            pltpu.VMEM((1, wide), f32),
            pltpu.VMEM((depth,) + chunk, f32),
        ],
        compiler_params=PARAMS,
    )(place, x_near, x_far, x_there, x_far_there, y_near, y_far)

    sums = {}
    for part, got in enumerate((send_z(give, z_partner), send_z(give_later, z_partner))):
        outs = pl.pallas_call(
            pair_kernel,
            out_shape=[jax.ShapeDtypeStruct(chunk, f32)] * (half // 2),
            in_specs=[VMEM] * 2,
            out_specs=[VMEM] * (half // 2),
            compiler_params=PARAMS,
        )(keep[part], got)
        sums.update(zip(ORDERS[part], outs))
    own, ahead, back = sums[0], sums[4], sums[5]
    ahead_rest, back_rest = [sums[3], sums[2], sums[1]], [sums[6], sums[7]]
    for step in range(middle):
        ahead = send_z(ahead, lambda z, c: z + 2 if c == 0 else z - 2)
        if step < middle - 1:
            ahead = ahead + ahead_rest[step]
            back = send_z(back, lambda z, c: z - 2 if c == 0 else z + 2)
            if step < middle - 2:
                back = back + back_rest[step]
    own = own + ahead + back

    few = tall // depth
    high = rows // depth
    part = pl.pallas_call(
        first_rows_kernel,
        out_shape=jax.ShapeDtypeStruct((group, high, wide + rows), f32),
        in_specs=[VMEM],
        out_specs=VMEM,
        scratch_shapes=[pltpu.VMEM((1, 1, few), f32)],
        compiler_params=PARAMS,
    )(own)
    part = swap(part, x_groups)
    everything, pieces = lax.optimization_barrier((everything, part[:, :, :wide]))
    gathered = lax.all_gather(pieces, "dp")
    z_groups = [
        [((y * group) + k) * depth + d for y in range(YS) for d in range(depth)] for k in range(group)
    ]
    row_shape = jax.ShapeDtypeStruct((group, 1, few), f32)
    for step in range(EARLY):
        if step > 0:
            part = pl.pallas_call(
                functools.partial(rows_kernel, log_weight),
                out_shape=row_shape,
                in_specs=[VMEM] * 2,
                out_specs=VMEM,
                compiler_params=PARAMS,
            )(own, part)
            part = swap(part, x_groups)
        part = pl.pallas_call(
            functools.partial(columns_kernel, log_weight, 0 if step > 0 else wide),
            out_shape=jax.ShapeDtypeStruct((YS * depth, YS, rows), f32),
            in_specs=[VMEM] * 2,
            out_specs=VMEM,
            scratch_shapes=[pltpu.VMEM((few, wide), f32)],
            compiler_params=PARAMS,
        )(own, part)
        part = lax.all_to_all(
            part, ("noise", "dp"), 0, 0, axis_index_groups=z_groups, tiled=True
        )
    part = pl.pallas_call(
        join_kernel,
        out_shape=jax.ShapeDtypeStruct((group, YS, rows), f32),
        in_specs=[VMEM],
        out_specs=VMEM,
        compiler_params=PARAMS,
    )(part)
    part = swap(part, x_groups)

    copies = lax.axis_size("noise")
    lines = 8
    block = tokens // lines
    u_shape = jax.ShapeDtypeStruct((rows, rows), f32)
    l_shape = jax.ShapeDtypeStruct((copies, lines, block), f32)
    for step in range(EARLY, ITERS):
        if step == EARLY:
            a, u, part = pl.pallas_call(
                functools.partial(whole_rows_kernel, log_weight),
                out_shape=[jax.ShapeDtypeStruct((rows, tokens), f32), u_shape, l_shape],
                in_specs=[VMEM] * 2,
                out_specs=[VMEM] * 3,
                compiler_params=PARAMS,
            )(gathered, part)
        else:
            u, part = pl.pallas_call(
                functools.partial(next_kernel, log_weight),
                out_shape=[u_shape, l_shape],
                in_specs=[VMEM] * 2,
                out_specs=[VMEM] * 2,
                compiler_params=PARAMS,
            )(a, part)
        part = lax.all_to_all(part, "noise", 0, 0, tiled=True)

    steps = 4
    targets, noise_potential, data_potential = pl.pallas_call(
        functools.partial(target_kernel, log_weight, epsilon / LOG2E, steps),
        grid=(steps,),
        out_shape=[
            jax.ShapeDtypeStruct((rows, features), jnp.bfloat16),
            jax.ShapeDtypeStruct((1, rows), f32),
            jax.ShapeDtypeStruct((1, block // 2), f32),
        ],
        in_specs=[
            SMEM,
            pl.BlockSpec((rows, tokens // steps), lambda k: (0, k)),
            pl.BlockSpec((rows, rows), lambda k: (0, 0)),
            pl.BlockSpec((copies, lines, block), lambda k: (0, 0, 0)),
            pl.BlockSpec((tokens // steps, features), lambda k: (k, 0)),
        ],
        out_specs=[
            pl.BlockSpec((rows, features), lambda k: (0, 0)),
            pl.BlockSpec((1, rows), lambda k: (0, 0)),
            pl.BlockSpec((1, block // 2), lambda k: (0, 0)),
        ],
        scratch_shapes=[
            pltpu.VMEM((rows, features), f32),
            pltpu.VMEM((rows, 1), f32),
            pltpu.VMEM((lines, block), f32),
        ],
        compiler_params=PARAMS,
    )(place, a, u, part, everything)
    return targets, noise_potential.reshape(rows), data_potential.reshape(block // 2)


def solution(mesh):
    return jax.shard_map(
        on_device,
        mesh=mesh,
        in_specs=(P("noise", "dp"), P("noise", "dp")),
        out_specs=(P("noise", "dp"), P("noise"), P("dp")),
        check_vma=False,
    )
```

```python
import functools
import math

import jax
import jax.numpy as jnp
from jax import lax
from jax.experimental import pallas as pl
from jax.experimental.pallas import tpu as pltpu
from jax.sharding import PartitionSpec as P

D = 16384
ITERS = 4
EARLY = 2
YS, XS, CORES = 4, 4, 2
LOG2E = math.log2(math.e)
VMEM = pl.BlockSpec(memory_space=pltpu.VMEM)
SMEM = pl.BlockSpec(memory_space=pltpu.SMEM)
PARAMS = pltpu.CompilerParams(vmem_limit_bytes=48 * 1024 * 1024)


def noise_pairs(target):
    pairs = []
    for y in range(YS):
        for x in range(XS):
            for c in range(CORES):
                to_y, to_x, to_c = target(y, x, c)
                pairs.append(((y * XS + x) * CORES + c, (to_y * XS + to_x) * CORES + to_c))
    return pairs


def to_other_core(value):
    return lax.ppermute(value, "noise", noise_pairs(lambda y, x, c: (y, x, 1 - c)))


FIRST, SECOND, BOTH = (1, 3), (3, 1), 2
PLACES = ((0, 0), FIRST, SECOND, (BOTH, BOTH))


ORDERS = ((4, 5), (3, 6, 2, 7, 1, 0))


def swap_x(value, by):
    return lax.ppermute(value, "noise", noise_pairs(lambda y, x, c: (y, x ^ by[c], c)))


def swap_y(value, by):
    return lax.ppermute(value, "noise", noise_pairs(lambda y, x, c: (y ^ by[c], x, c)))


def stacked(block, received):
    rows, features = block.shape
    both = lax.dynamic_update_slice(jnp.zeros((2 * rows, features), block.dtype), block, (0, 0))
    both = lax.optimization_barrier(both)
    return lax.dynamic_update_slice(both, received, (rows, 0))


def send_z(value, target):
    size = lax.axis_size("dp")
    pairs = []
    for n in range(YS * XS * CORES):
        pairs += [(n * size + z, n * size + target(z, n % CORES) % size) for z in range(size)]
    return lax.ppermute(value, ("noise", "dp"), pairs)


def z_partner(z, c):
    return z ^ 1 if c == 0 else z + 1 if z % 2 else z - 1


def squares_row(block):
    wide = block.astype(jnp.float32)
    column = jnp.sum(wide * wide, axis=1, keepdims=True)
    n = block.shape[0]
    row_at = lax.broadcasted_iota(jnp.int32, (n, n), 0)
    column_at = lax.broadcasted_iota(jnp.int32, (n, n), 1)
    return jnp.sum(jnp.where(row_at == column_at, column, 0.0), axis=0, keepdims=True)


def partial_kernel(scale, place_ref, *refs):
    here, there, ys = refs[:2], refs[2:4], refs[4:6]
    keep, give, (x_all, y_all, y_squares, chunks) = refs[6:8], refs[8:10], refs[10:]
    rows = here[0].shape[0] // 2
    depth = chunks.shape[0]
    high = rows // depth
    z, y, x, c = place_ref[0], place_ref[1], place_ref[2], place_ref[3]
    for k, (first, second) in enumerate(PLACES):
        block = slice(k % 2 * rows, (k % 2 + 1) * rows)
        mine, other = jnp.where(c == 0, first, second), jnp.where(c == 0, second, first)
        at = pl.multiple_of((lax.bitwise_xor(x, mine) * CORES + c) * rows, rows)
        x_all[pl.ds(at, rows), :] = here[k // 2][block, :]
        at = pl.multiple_of((lax.bitwise_xor(x, other) * CORES + 1 - c) * rows, rows)
        x_all[pl.ds(at, rows), :] = there[k // 2][block, :]
        at = pl.multiple_of(lax.bitwise_xor(y, mine) * rows, rows)
        y_all[pl.ds(at, rows), :] = ys[k // 2][block, :]
    for k in range(YS):
        block = slice(k * rows, (k + 1) * rows)
        y_squares[:, block] = scale * squares_row(y_all[block, :])
    up = jnp.where(c == 0, lax.rem(z, 2) == 0, lax.rem(z, 2) == 1)
    partner = lax.rem(z + jnp.where(up, 1, depth - 1), depth)
    places = []
    for t in range(depth):
        same = lax.rem(z + t, 2) == 0
        base = jnp.where(same, z, partner)
        ahead = jnp.where(c == 0, lax.rem(t + depth - base, depth), lax.rem(base + depth - t, depth))
        places.append(ahead // 2 + jnp.where(same, 0, depth // 2))
    tall = 4 * rows
    for k in range(XS * CORES // 4):
        value = x_all[k * tall : (k + 1) * tall, :]
        wide = value.astype(jnp.float32)
        x_squares = scale * jnp.sum(wide * wide, axis=1, keepdims=True)
        cross = lax.dot_general(
            value, y_all[...], (((1,), (1,)), ((), ())), preferred_element_type=jnp.float32
        )
        value = (2.0 * scale) * cross - x_squares - y_squares[...]
        for i in range(4 * depth):
            block = k * 4 + i // depth
            chunks[places[i % depth], block * high : (block + 1) * high, :] = value[i * high : (i + 1) * high]
    for part, order in enumerate(ORDERS):
        for i, k in enumerate(order):
            keep[part][i] = chunks[k]
            give[part][i] = chunks[depth // 2 + k]


def pair_kernel(keep, got, *outs):
    for k, out in enumerate(outs):
        out[...] = keep[k] + got[k]


def joined(parts):
    peak = jnp.max(parts, axis=0)
    return peak + jnp.log(jnp.sum(jnp.exp2(parts - peak), axis=0)) * LOG2E


def on_diagonal(n):
    rows = lax.broadcasted_iota(jnp.int32, (n, n), 0)
    return rows == lax.broadcasted_iota(jnp.int32, (n, n), 1)


def column_of(u, k):
    n = u.shape[1]
    return jnp.sum(jnp.where(on_diagonal(n), u[k : k + 1], 0.0), axis=1, keepdims=True)


def row_of(parts_ref, log_weight):
    v = log_weight - joined(parts_ref[...])
    return jnp.concatenate([v[k : k + 1] for k in range(v.shape[0])], axis=1)


def copy_out(out_ref):
    whole = out_ref[0]
    for k in range(1, out_ref.shape[0]):
        out_ref[k] = whole


def row_sums(a_ref, v, out_ref, n):
    for k in range(a_ref.shape[0] // n):
        value = a_ref[k * n : (k + 1) * n, :]
        if v is not None:
            value = value + v
        peak = jnp.max(value, axis=1, keepdims=True)
        total = jnp.sum(jnp.exp2(value - peak), axis=1, keepdims=True)
        part = peak + jnp.log(total) * LOG2E
        out_ref[0, k : k + 1, :] = jnp.sum(jnp.where(on_diagonal(n), part, 0.0), axis=0, keepdims=True)
    copy_out(out_ref)


def first_rows_kernel(a_ref, out_ref, sums):
    copies, high, width = out_ref.shape
    n, columns = a_ref.shape
    row_sums(a_ref, None, sums, n)
    for k in range(copies):
        out_ref[k, :, :columns] = a_ref[k * high : (k + 1) * high, :]
        out_ref[k, :, columns:] = jnp.zeros((high, width - columns), jnp.float32)
        out_ref[k, :1, columns : columns + n] = sums[0]


def rows_kernel(log_weight, a_ref, parts_ref, out_ref):
    row_sums(a_ref, row_of(parts_ref, log_weight), out_ref, out_ref.shape[2])


def columns_kernel(log_weight, beside, a_ref, parts_ref, out_ref, shifted):
    parts = parts_ref[:, :1, beside : beside + a_ref.shape[0]]
    u = log_weight - joined(parts)
    blocks, n = u.shape
    width = a_ref.shape[1]
    peak = None
    for k in range(blocks):
        value = a_ref[k * n : (k + 1) * n, :] + column_of(u, k)
        shifted[k * n : (k + 1) * n, :] = value
        block_peak = jnp.max(value.reshape(n // 8, 8, width), axis=0)
        peak = block_peak if peak is None else jnp.maximum(peak, block_peak)
    peak = jnp.max(peak, axis=0, keepdims=True)
    total = jnp.zeros((8, width), jnp.float32)
    for k in range(blocks):
        value = jnp.exp2(shifted[k * n : (k + 1) * n, :] - peak)
        total = total + jnp.sum(value.reshape(n // 8, 8, width), axis=0)
    part = peak + jnp.log(jnp.sum(total, axis=0, keepdims=True)) * LOG2E
    lanes = out_ref.shape[2]
    for k in range(out_ref.shape[1]):
        out_ref[0, k : k + 1, :] = part[:, k * lanes : (k + 1) * lanes]
    copy_out(out_ref)


def join_kernel(parts_ref, out_ref):
    out_ref[0] = joined(parts_ref[...])
    copy_out(out_ref)


def half_steps(log_weight, a_ref, v, u_ref, l_ref):
    rows, columns = a_ref.shape
    lanes = u_ref.shape[1]
    copies, high, width = l_ref.shape

    @pl.loop(0, rows // 8, step=2)
    def _(base):
        for i in range(2):
            at = pl.ds(pl.multiple_of((base + i) * 8, 8), 8)
            value = a_ref[at, :] + v
            peak = jnp.max(value, axis=1, keepdims=True)
            total = jnp.sum(jnp.exp2(value - peak), axis=1, keepdims=True)
            u = log_weight - (peak + jnp.log(total) * LOG2E)
            u_ref[at, :] = jnp.broadcast_to(u, (8, lanes))

    for k in range(high):
        for i in range(width // lanes):
            at = pl.ds(k * width + i * lanes, lanes)
            value = a_ref[:, at] + u_ref[...]
            peak = jnp.max(value, axis=0, keepdims=True)
            total = jnp.sum(jnp.exp2(value - peak), axis=0, keepdims=True)
            l_ref[0, k : k + 1, i * lanes : (i + 1) * lanes] = peak + jnp.log(total) * LOG2E
    whole = l_ref[0]
    for k in range(1, copies):
        l_ref[k] = whole


def whole_rows_kernel(log_weight, pieces_ref, parts_ref, a_ref, u_ref, l_ref):
    depth, blocks, high, width = pieces_ref.shape
    n = width // YS
    v = log_weight - parts_ref[...]
    for z in range(depth):
        for y in range(YS):
            for k in range(blocks):
                at = (y * blocks + k) * n
                a_ref[z * high : (z + 1) * high, at : at + n] = pieces_ref[z, k, :, y * n : (y + 1) * n]
    v = jnp.concatenate([v[k, y : y + 1] for y in range(YS) for k in range(blocks)], axis=1)
    half_steps(log_weight, a_ref, v, u_ref, l_ref)


def next_kernel(log_weight, a_ref, parts_ref, u_ref, l_ref):
    v = log_weight - joined(parts_ref[...])
    v = jnp.concatenate([v[k : k + 1] for k in range(v.shape[0])], axis=1)
    half_steps(log_weight, a_ref, v, u_ref, l_ref)


def target_kernel(
    log_weight, unit, steps, place_ref, a_ref, u_ref, parts_ref, y_ref, out_ref, f_ref, g_ref, total, mass, v_ref
):
    step = pl.program_id(0)
    lines = v_ref.shape[0] // steps

    @pl.when(step == 0)
    def _():
        total[...] = jnp.zeros_like(total)
        mass[...] = jnp.zeros_like(mass)
        u = u_ref[...]
        f_ref[...] = unit * jnp.sum(jnp.where(on_diagonal(u.shape[0]), u, 0.0), axis=0, keepdims=True)
        v_ref[...] = log_weight - joined(parts_ref[...])
        share = g_ref.shape[1]
        z = place_ref[0]
        line = v_ref[pl.ds(z // 2, 1), :]
        g_ref[...] = unit * jnp.where(lax.rem(z, 2) == 0, line[:, :share], line[:, share:])

    v = jnp.concatenate([v_ref[pl.ds(step * lines + k, 1), :] for k in range(lines)], axis=1)
    u = u_ref[:, :1]
    plan = jnp.exp2((u - log_weight + v) + a_ref[...]).astype(jnp.bfloat16)
    mass[...] += jnp.sum(plan.astype(jnp.float32), axis=1, keepdims=True)
    total[...] += jnp.dot(plan, y_ref[...], preferred_element_type=jnp.float32)

    @pl.when(step == steps - 1)
    def _():
        out_ref[...] = (total[...] / mass[...]).astype(out_ref.dtype)


def on_device(noise_rows, data_rows):
    rows, features = noise_rows.shape
    tokens = rows * lax.axis_size("noise")
    depth = lax.axis_size("dp")
    me, z = lax.axis_index("noise"), lax.axis_index("dp")
    place = jnp.stack([z, me // (XS * CORES), me // CORES % XS, me % CORES]).astype(jnp.int32)
    epsilon = 0.7 / math.sqrt(D)
    log_weight = -math.log2(tokens)
    f32 = jnp.float32

    group = XS * CORES
    y_groups = [[y * group + k for y in range(YS)] for k in range(group)]
    x_groups = [[y * group + k for k in range(group)] for y in range(YS)]

    def swap(value, groups):
        return lax.all_to_all(value, "noise", 0, 0, axis_index_groups=groups, tiled=True)

    x_near = stacked(noise_rows, swap_x(noise_rows, FIRST))
    y_near = stacked(data_rows, swap_y(data_rows, FIRST))
    x_near, y_near = lax.optimization_barrier((x_near, y_near))
    x_far, y_far = swap_x(x_near, SECOND), swap_y(y_near, SECOND)
    x_there, x_far_there, y_far, late_rows = lax.optimization_barrier(
        (to_other_core(x_near), to_other_core(x_far), y_far, data_rows)
    )
    everything = lax.all_gather(late_rows, "noise", axis=0, tiled=True)
    tall, wide = group * rows, YS * rows
    half = depth // 2
    middle = half // 2
    chunk = (tall // depth, wide)
    *keep, give, give_later = pl.pallas_call(
        functools.partial(partial_kernel, LOG2E / (epsilon * D)),
        out_shape=[jax.ShapeDtypeStruct((len(order),) + chunk, f32) for order in ORDERS * 2],
        in_specs=[SMEM] + [VMEM] * 6,
        out_specs=[VMEM] * 4,
        scratch_shapes=[
            pltpu.VMEM((group * rows, features), jnp.bfloat16),
            pltpu.VMEM((YS * rows, features), jnp.bfloat16),
            pltpu.VMEM((1, wide), f32),
            pltpu.VMEM((depth,) + chunk, f32),
        ],
        compiler_params=PARAMS,
    )(place, x_near, x_far, x_there, x_far_there, y_near, y_far)

    sums = {}
    for part, got in enumerate((send_z(give, z_partner), send_z(give_later, z_partner))):
        outs = pl.pallas_call(
            pair_kernel,
            out_shape=[jax.ShapeDtypeStruct(chunk, f32)] * len(ORDERS[part]),
            in_specs=[VMEM] * 2,
            out_specs=[VMEM] * len(ORDERS[part]),
            compiler_params=PARAMS,
        )(keep[part], got)
        sums.update(zip(ORDERS[part], outs))
    own, ahead, back = sums[0], sums[4], sums[5]
    ahead_rest, back_rest = [sums[3], sums[2], sums[1]], [sums[6], sums[7]]
    for step in range(middle):
        ahead = send_z(ahead, lambda z, c: z + 2 if c == 0 else z - 2)
        if step < middle - 1:
            ahead = ahead + ahead_rest[step]
            back = send_z(back, lambda z, c: z - 2 if c == 0 else z + 2)
            if step < middle - 2:
                back = back + back_rest[step]
    own = own + ahead + back

    few = tall // depth
    high = rows // depth
    part = pl.pallas_call(
        first_rows_kernel,
        out_shape=jax.ShapeDtypeStruct((group, high, wide + rows), f32),
        in_specs=[VMEM],
        out_specs=VMEM,
        scratch_shapes=[pltpu.VMEM((1, 1, few), f32)],
        compiler_params=PARAMS,
    )(own)
    part = swap(part, x_groups)
    everything, pieces = lax.optimization_barrier((everything, part[:, :, :wide]))
    gathered = lax.all_gather(pieces, "dp")
    z_groups = [
        [((y * group) + k) * depth + d for y in range(YS) for d in range(depth)] for k in range(group)
    ]
    row_shape = jax.ShapeDtypeStruct((group, 1, few), f32)
    for step in range(EARLY):
        if step > 0:
            part = pl.pallas_call(
                functools.partial(rows_kernel, log_weight),
                out_shape=row_shape,
                in_specs=[VMEM] * 2,
                out_specs=VMEM,
                compiler_params=PARAMS,
            )(own, part)
            part = swap(part, x_groups)
        part = pl.pallas_call(
            functools.partial(columns_kernel, log_weight, 0 if step > 0 else wide),
            out_shape=jax.ShapeDtypeStruct((YS * depth, YS, rows), f32),
            in_specs=[VMEM] * 2,
            out_specs=VMEM,
            scratch_shapes=[pltpu.VMEM((few, wide), f32)],
            compiler_params=PARAMS,
        )(own, part)
        part = lax.all_to_all(
            part, ("noise", "dp"), 0, 0, axis_index_groups=z_groups, tiled=True
        )
    part = pl.pallas_call(
        join_kernel,
        out_shape=jax.ShapeDtypeStruct((group, YS, rows), f32),
        in_specs=[VMEM],
        out_specs=VMEM,
        compiler_params=PARAMS,
    )(part)
    part = swap(part, x_groups)

    copies = lax.axis_size("noise")
    lines = 8
    block = tokens // lines
    u_shape = jax.ShapeDtypeStruct((rows, rows), f32)
    l_shape = jax.ShapeDtypeStruct((copies, lines, block), f32)
    for step in range(EARLY, ITERS):
        if step == EARLY:
            a, u, part = pl.pallas_call(
                functools.partial(whole_rows_kernel, log_weight),
                out_shape=[jax.ShapeDtypeStruct((rows, tokens), f32), u_shape, l_shape],
                in_specs=[VMEM] * 2,
                out_specs=[VMEM] * 3,
                compiler_params=PARAMS,
            )(gathered, part)
        else:
            u, part = pl.pallas_call(
                functools.partial(next_kernel, log_weight),
                out_shape=[u_shape, l_shape],
                in_specs=[VMEM] * 2,
                out_specs=[VMEM] * 2,
                compiler_params=PARAMS,
            )(a, part)
        part = lax.all_to_all(part, "noise", 0, 0, tiled=True)

    steps = 4
    targets, noise_potential, data_potential = pl.pallas_call(
        functools.partial(target_kernel, log_weight, epsilon / LOG2E, steps),
        grid=(steps,),
        out_shape=[
            jax.ShapeDtypeStruct((rows, features), jnp.bfloat16),
            jax.ShapeDtypeStruct((1, rows), f32),
            jax.ShapeDtypeStruct((1, block // 2), f32),
        ],
        in_specs=[
            SMEM,
            pl.BlockSpec((rows, tokens // steps), lambda k: (0, k)),
            pl.BlockSpec((rows, rows), lambda k: (0, 0)),
            pl.BlockSpec((copies, lines, block), lambda k: (0, 0, 0)),
            pl.BlockSpec((tokens // steps, features), lambda k: (k, 0)),
        ],
        out_specs=[
            pl.BlockSpec((rows, features), lambda k: (0, 0)),
            pl.BlockSpec((1, rows), lambda k: (0, 0)),
            pl.BlockSpec((1, block // 2), lambda k: (0, 0)),
        ],
        scratch_shapes=[
            pltpu.VMEM((rows, features), f32),
            pltpu.VMEM((rows, 1), f32),
            pltpu.VMEM((lines, block), f32),
        ],
        compiler_params=PARAMS,
    )(place, a, u, part, everything)
    return targets, noise_potential.reshape(rows), data_potential.reshape(block // 2)


def solution(mesh):
    return jax.shard_map(
        on_device,
        mesh=mesh,
        in_specs=(P("noise", "dp"), P("noise", "dp")),
        out_specs=(P("noise", "dp"), P("noise"), P("dp")),
        check_vma=False,
    )
```
